32 devices in a mesh: img: 16 (over z, y, x), ch: 2 (over core).
Axes of the slice: x: 2, y: 2, z: 4, core: 2. Of those that a mesh axis runs over, the one named last changes fastest.
Arguments:
- pixels: bfloat16 [768, 65536], P('ch', 'img'), may hold values from -6 to 6
- image_sizes: int32 [256, 2], P('img'), may hold values from 2 to 16, as said below
- out_grad: bfloat16 [768, 65536], P('ch', 'img'), may hold values from -6 to 6
- up_weight: float32 [768, 3072], P(None, 'ch'), may hold values from -0.21875 to 0.21875
- down_weight: float32 [3072, 768], P('ch'), may hold values from -0.109375 to 0.109375
- mixer_params: float32 [768, 512], P('ch'), may hold values from -4 to 3
- channel_params: float32 [5, 768], P(None, 'ch'), may hold values from -0.5 to 1.5
- hidden_bias: float32 [3072], P('ch'), may hold values from -4 to 4
- up_rows: float32 [768], replicated, as said below
- up_cols: float32 [3072], P('ch'), as said below
- down_rows: float32 [3072], P('ch'), as said below
- down_cols: float32 [768], replicated, as said below
- mixer_rows: float32 [768], P('ch'), as said below
- mixer_cols: float32 [512], replicated, as said below
- channel_moment: float32 [5, 768], P(None, 'ch'), as said below
- bias_moment: float32 [3072], P('ch'), as said below
- up_average: float32 [768, 3072], P(None, 'ch'), may hold values from -0.21875 to 0.21875
- down_average: float32 [3072, 768], P('ch'), may hold values from -0.109375 to 0.109375
- mixer_average: float32 [768, 512], P('ch'), may hold values from -4 to 3
- channel_average: float32 [5, 768], P(None, 'ch'), may hold values from -0.5 to 1.5
- bias_average: float32 [3072], P('ch'), may hold values from -4 to 4
Outputs:
- block_out: float32 [768, 65536], P('ch', 'img')
- pixel_grad: float32 [768, 65536], P('ch', 'img')
- update_rms: float32 [], replicated
- up_grad: float32 [768, 3072], P(None, 'ch')
- up_rows_new: float32 [768], replicated
- up_cols_new: float32 [3072], P('ch')
- up_new: float32 [768, 3072], P(None, 'ch')
- up_average_new: float32 [768, 3072], P(None, 'ch')
- down_grad: float32 [3072, 768], P('ch')
- down_rows_new: float32 [3072], P('ch')
- down_cols_new: float32 [768], replicated
- down_new: float32 [3072, 768], P('ch')
- down_average_new: float32 [3072, 768], P('ch')
- mixer_grad: float32 [768, 512], P('ch')
- mixer_rows_new: float32 [768], P('ch')
- mixer_cols_new: float32 [512], replicated
- mixer_new: float32 [768, 512], P('ch')
- mixer_average_new: float32 [768, 512], P('ch')
- channel_grad: float32 [5, 768], P(None, 'ch')
- channel_moment_new: float32 [5, 768], P(None, 'ch')
- channel_new: float32 [5, 768], P(None, 'ch')
- channel_average_new: float32 [5, 768], P(None, 'ch')
- bias_grad: float32 [3072], P('ch')
- bias_moment_new: float32 [3072], P('ch')
- bias_new: float32 [3072], P('ch')
- bias_average_new: float32 [3072], P('ch')
The draws below stay inside these ranges and needn't reach their ends.
Inputs may be any that keep to these rules, and one draw needn't show every extreme that they name: `image_sizes`: heights and widths of the valid corner of each image slot of 16 x 16 pixels; some image has 16 x 16. `up_rows`: Positive. `up_cols`: Positive. `down_rows`: Positive. `down_cols`: Positive. `mixer_rows`: Positive. `mixer_cols`: Positive. `channel_moment`: Positive. `bias_moment`: Positive.
All inputs are finite; a program needn't handle non-finite values.
Results may differ from the reference program's by a relative error of at most 0.01.
Values may be sent and summed in bfloat16 or wider, within the bound.
No kernel may reach another device: no remote copies, remote signals or barrier semaphores. Data moves between devices by JAX's collectives and lax.ppermute only.
A program may use at most 320 MiB of HBM per device.

```python
import jax
import jax.numpy as jnp
from jax import lax

C = 768
F = 3072
N = 64
S = 16
STEP = 10
IMG_DEV = 16
IMAGES = 256
PIXELS = 65536


def moment_table(key, shape, base, falling):
    first_key, second_key = jax.random.split(key)
    spread = jnp.exp(jax.random.uniform(first_key, shape, jnp.float32, -0.6931, 0.6931))
    if falling:
        length = shape[-1]
        place = jnp.arange(length).astype(jnp.float32) / max(length - 1, 1)
        level = 4.5 * jnp.exp(place * jnp.log(0.8 / 4.5))
    else:
        level = jax.random.uniform(second_key, shape, jnp.float32, 1.0, 4.0)
    fresh = STEP ** (-0.8)
    return (level * spread * (base * fresh / (1.0 - fresh))).astype(jnp.float32)


def mixer_table(key):
    rate_key, freq_key, coef_key = jax.random.split(key, 3)
    rates = jax.random.uniform(rate_key, (C, 2, 1, N), jnp.float32, -4.0, 0.0)
    freqs = jax.random.uniform(freq_key, (C, 2, 1, N), jnp.float32, -3.0, 3.0)
    coefs = 0.05 * jnp.clip(jax.random.normal(coef_key, (C, 2, 2, N), jnp.float32), -6.0, 6.0)
    return jnp.concatenate([rates, freqs, coefs], axis=2).reshape(C, 8 * N)


def channel_table(key):
    lower = jnp.array([0.6, -0.5, 0.5, 0.5, -0.5], jnp.float32)[:, None]
    upper = jnp.array([1.4, 0.5, 1.5, 1.5, 0.5], jnp.float32)[:, None]
    return lower + (upper - lower) * jax.random.uniform(key, (5, C), jnp.float32)


def draw_image_sizes(key, part):
    key = jax.random.fold_in(key, 1)
    first_key, second_key = jax.random.split(key)
    groups = IMAGES // IMG_DEV
    group = jnp.arange(IMAGES) // IMG_DEV
    lowest = 2 + (S - 2) * group // max(groups - 1, 1)
    span = (S + 1 - lowest)[:, None]
    first = jax.random.randint(first_key, (IMAGES, 2), 0, 1 << 20)
    second = jax.random.randint(second_key, (IMAGES, 2), 0, 1 << 20)
    sides = lowest[:, None] + jnp.minimum(first % span, second % span)
    sides = sides.at[0, 0].set(2)
    return sides.astype(jnp.int32)


def draw_mixer_params(key, part):
    key = jax.random.fold_in(key, 2)
    return mixer_table(key)


def draw_mixer_average(key, part):
    key = jax.random.fold_in(key, 3)
    return mixer_table(key)


def draw_channel_params(key, part):
    key = jax.random.fold_in(key, 4)
    return channel_table(key)


def draw_channel_average(key, part):
    key = jax.random.fold_in(key, 5)
    return channel_table(key)


def draw_up_rows(key, part):
    key = jax.random.fold_in(key, 11)
    return moment_table(key, (C,), 0.04 * IMAGES * S * S, False)


def draw_up_cols(key, part):
    key = jax.random.fold_in(key, 12)
    return moment_table(key, (F,), 0.04 * IMAGES * S * S, True)


def draw_down_rows(key, part):
    key = jax.random.fold_in(key, 13)
    return moment_table(key, (F,), 0.15 * IMAGES * S * S, True)


def draw_down_cols(key, part):
    key = jax.random.fold_in(key, 14)
    return moment_table(key, (C,), 0.15 * IMAGES * S * S, False)


def draw_mixer_rows(key, part):
    key = jax.random.fold_in(key, 15)
    return moment_table(key, (C,), 0.05 * IMAGES * S * S, True)


def draw_mixer_cols(key, part):
    key = jax.random.fold_in(key, 16)
    return moment_table(key, (8 * N,), 0.05 * IMAGES * S * S, False)


def draw_channel_moment(key, part):
    key = jax.random.fold_in(key, 17)
    return moment_table(key, (5, C), 0.2 * IMAGES * S * S, True)


def draw_bias_moment(key, part):
    key = jax.random.fold_in(key, 18)
    return moment_table(key, (F,), 0.04 * IMAGES * S * S, True)


def steps_of(rng, shape, cuts, least, high):
    def one(axis_at, blocks):
        steps = jax.random.uniform(jax.random.fold_in(jax.random.fold_in(rng, 6), axis_at), (blocks,), jnp.float32, least / len(cuts), high / len(cuts))
        return jnp.repeat(jnp.exp(steps), shape[axis_at] // blocks).reshape((-1,) + (1,) * (len(shape) - axis_at - 1))

    level = one(*cuts[0])
    for cut in cuts[1:]:
        level = level * one(*cut)
    return level


def bell_draw(key, shape, width, limit, pieces=(), kind=jnp.bfloat16):
    entries = jax.random.normal(key, shape, jnp.float32) * width
    if len(pieces) > 0:
        entries = steps_of(key, shape, pieces, -0.22, 0.18) * entries
    return jnp.clip(entries, min=-limit, max=limit).astype(kind)


def setup_inputs(seed: int = 0) -> dict:
    keys = jax.random.split(jax.random.key(seed), 22)
    return {
        "pixels": bell_draw(keys[0], (C, PIXELS), 1.0, 6.0, ((0, 2), (1, 16))),
        "image_sizes": draw_image_sizes(jax.random.fold_in(keys[21], 71), 0),
        "out_grad": bell_draw(keys[2], (C, PIXELS), 1.0, 6.0, ((0, 2), (1, 16))),
        "up_weight": bell_draw(keys[3], (C, F), C ** -0.5, 0.21875, ((1, 2),), jnp.float32),
        "down_weight": bell_draw(keys[4], (F, C), F ** -0.5, 0.109375, ((0, 2),), jnp.float32),
        "mixer_params": draw_mixer_params(jax.random.fold_in(keys[21], 71), 0),
        "channel_params": draw_channel_params(jax.random.fold_in(keys[21], 71), 0),
        "hidden_bias": bell_draw(keys[7], (F,), 0.3, 4.0, ((0, 2),), jnp.float32),
        "up_rows": draw_up_rows(jax.random.fold_in(keys[21], 71), 0),
        "up_cols": draw_up_cols(jax.random.fold_in(keys[21], 71), 0),
        "down_rows": draw_down_rows(jax.random.fold_in(keys[21], 71), 0),
        "down_cols": draw_down_cols(jax.random.fold_in(keys[21], 71), 0),
        "mixer_rows": draw_mixer_rows(jax.random.fold_in(keys[21], 71), 0),
        "mixer_cols": draw_mixer_cols(jax.random.fold_in(keys[21], 71), 0),
        "channel_moment": draw_channel_moment(jax.random.fold_in(keys[21], 71), 0),
        "bias_moment": draw_bias_moment(jax.random.fold_in(keys[21], 71), 0),
        "up_average": bell_draw(keys[16], (C, F), C ** -0.5, 0.21875, ((1, 2),), jnp.float32),
        "down_average": bell_draw(keys[17], (F, C), F ** -0.5, 0.109375, ((0, 2),), jnp.float32),
        "mixer_average": draw_mixer_average(jax.random.fold_in(keys[21], 71), 0),
        "channel_average": draw_channel_average(jax.random.fold_in(keys[21], 71), 0),
        "bias_average": bell_draw(keys[20], (F,), 0.3, 4.0, ((0, 2),), jnp.float32),
    }


@jax.custom_vjp
def low(v):
    return lax.optimization_barrier(v.astype(jnp.bfloat16)).astype(jnp.float32)

@jax.custom_vjp
def low_back(v):
    return v

def low_keep(v):
    return (low(v), None)

def low_pass(kept, grad):
    return (grad,)

def back_keep(v):
    return (v, None)

def back_low(kept, grad):
    return (low(grad),)
low.defvjp(low_keep, low_pass)
low_back.defvjp(back_keep, back_low)
HIGH = lax.Precision.HIGHEST
EPSILON_NORM = 1e-06
EPSILON_SQUARE = 1e-30
EPSILON_SCALE = 0.001
LEARN_RATE = 0.3
CLIP_LEVEL = 1.0
AVERAGE_KEEP = 0.9

def kernel_rows(params, length):
    count = params.shape[1] // 4
    rate = jnp.exp(params[:, :count])
    freq = params[:, count:2 * count]
    real_part = params[:, 2 * count:3 * count]
    imag_part = params[:, 3 * count:]
    places = jnp.arange(length).astype(jnp.float32)
    damp = jnp.exp(-rate[:, :, None] * places)
    phase = freq[:, :, None] * places
    terms = damp * (real_part[:, :, None] * jnp.cos(phase) - imag_part[:, :, None] * jnp.sin(phase))
    return lax.optimization_barrier(jnp.sum(terms, axis=1))

def toeplitz(kernel, length):
    places = jnp.arange(length)
    offsets = places[:, None] - places[None, :]
    onehot = (offsets[None, :, :] == places[:, None, None]).astype(jnp.float32)
    return jnp.einsum('cd,dij->cij', kernel, onehot, precision=HIGH)

def mixer(cells, params, skip):
    length = cells.shape[1]
    half = params.shape[1] // 2
    along_h = low(toeplitz(kernel_rows(params[:, :half], length), length))
    along_w = low(toeplitz(kernel_rows(params[:, half:], length), length))
    first = low_back(low(jnp.einsum('cij,bjwc->biwc', along_h, cells, precision=HIGH)))
    second = jnp.einsum('cij,bhjc->bhic', along_w, first, precision=HIGH)
    return second + skip * cells

def block_forward(params, source, inside):
    up_weight, down_weight, mixer_params, channel_params, hidden_bias = params
    cells = source * inside
    mixed = low_back(low(mixer(cells, mixer_params, channel_params[2])))
    flat = mixed.reshape(-1, mixed.shape[-1])
    center = flat - lax.optimization_barrier(jnp.mean(flat, axis=1, keepdims=True))
    normed = center * lax.rsqrt(lax.optimization_barrier(jnp.mean(center * center, axis=1, keepdims=True)) + EPSILON_NORM)
    act_in = low(normed * low(channel_params[0]) + low(channel_params[1]))
    pre = low_back(jnp.dot(act_in, low(up_weight), precision=HIGH) + low(hidden_bias))
    hidden = low(jax.nn.gelu(pre, approximate=False))
    proj = low_back(jnp.dot(hidden, low(down_weight), precision=HIGH))
    mask_flat = inside.reshape(-1, 1)
    return source.reshape(flat.shape) + mask_flat * channel_params[3] * (proj + channel_params[4])

def reference(pixels, image_sizes, out_grad, up_weight, down_weight, mixer_params, channel_params, hidden_bias, up_rows, up_cols, down_rows, down_cols, mixer_rows, mixer_cols, channel_moment, bias_moment, up_average, down_average, mixer_average, channel_average, bias_average):
    images = image_sizes.shape[0]
    places = jnp.arange(S)
    inside = ((places[None, :, None] < image_sizes[:, 0, None, None]) & (places[None, None, :] < image_sizes[:, 1, None, None])).astype(jnp.float32)
    blocks = images // IMG_DEV
    sources = pixels.astype(jnp.float32).T.reshape(blocks, IMG_DEV, S, S, C)
    cotangents = out_grad.astype(jnp.float32).T.reshape(blocks, IMG_DEV * S * S, C)
    masks = inside.reshape(blocks, IMG_DEV, S, S, 1)
    params = (up_weight, down_weight, mixer_params, channel_params, hidden_bias)

    def one_block(totals, item):
        source, cotangent, inside_block = item

        def forward(weights, values):
            return block_forward(weights, values, inside_block)
        output, pull = jax.vjp(forward, params, source)
        weight_grads, source_grad = pull(cotangent)
        totals = jax.tree.map(lambda left, right: left + right, totals, weight_grads)
        return (totals, (output, source_grad))
    zeros = jax.tree.map(jnp.zeros_like, params)
    grads, (outputs, source_grads) = lax.scan(one_block, zeros, (sources, cotangents, masks))
    block_out = outputs.reshape(-1, C).T
    pixel_grad = source_grads.reshape(-1, C).T
    up_grad, down_grad, mixer_grad, channel_grad, bias_grad = grads
    decay = 1.0 - STEP ** (-0.8)
    fresh = 1.0 - decay

    def factored(grad, rows_old, cols_old):
        square = grad * grad + EPSILON_SQUARE
        rows_new = decay * rows_old + fresh * lax.optimization_barrier(jnp.mean(square, axis=1))
        cols_new = decay * cols_old + fresh * lax.optimization_barrier(jnp.mean(square, axis=0))
        update = grad * lax.rsqrt(rows_new[:, None] * cols_new[None, :] / jnp.mean(rows_new))
        return (rows_new, cols_new, update)

    def plain(grad, moment_old):
        moment_new = decay * moment_old + fresh * (grad * grad + EPSILON_SQUARE)
        return (moment_new, grad * lax.rsqrt(moment_new))
    up_rows_new, up_cols_new, up_update = factored(up_grad, up_rows, up_cols)
    down_rows_new, down_cols_new, down_update = factored(down_grad, down_rows, down_cols)
    mixer_rows_new, mixer_cols_new, mixer_update = factored(mixer_grad, mixer_rows, mixer_cols)
    channel_moment_new, channel_update = plain(channel_grad, channel_moment)
    bias_moment_new, bias_update = plain(bias_grad, bias_moment)
    total = jnp.sum(up_update * up_update) + jnp.sum(down_update * down_update) + jnp.sum(mixer_update * mixer_update) + jnp.sum(channel_update * channel_update) + jnp.sum(bias_update * bias_update)
    count = 2 * C * F + 8 * N * C + 5 * C + F
    update_rms = jnp.sqrt(total / count)
    factor = CLIP_LEVEL / jnp.maximum(CLIP_LEVEL, update_rms)

    def spread(weight):
        return jnp.maximum(EPSILON_SCALE, jnp.sqrt(jnp.mean(weight * weight)))
    up_new = up_weight - LEARN_RATE * spread(up_weight) * factor * up_update
    down_new = down_weight - LEARN_RATE * spread(down_weight) * factor * down_update
    mixer_new = mixer_params - LEARN_RATE * spread(mixer_params) * factor * mixer_update
    channel_spread = jnp.maximum(EPSILON_SCALE, jnp.sqrt(lax.optimization_barrier(jnp.mean(channel_params * channel_params, axis=1, keepdims=True))))
    channel_new = channel_params - LEARN_RATE * channel_spread * factor * channel_update
    bias_new = hidden_bias - LEARN_RATE * spread(hidden_bias) * factor * bias_update

    def average(old, new):
        return AVERAGE_KEEP * old + (1.0 - AVERAGE_KEEP) * new
    return (block_out, pixel_grad, update_rms, up_grad, up_rows_new, up_cols_new, up_new, average(up_average, up_new), down_grad, down_rows_new, down_cols_new, down_new, average(down_average, down_new), mixer_grad, mixer_rows_new, mixer_cols_new, mixer_new, average(mixer_average, mixer_new), channel_grad, channel_moment_new, channel_new, average(channel_average, channel_new), bias_grad, bias_moment_new, bias_new, average(bias_average, bias_new))
```

```python
import functools

import jax
import jax.numpy as jnp
import ml_dtypes
import numpy as np
from jax import lax
from jax.experimental import pallas as pl
from jax.experimental.pallas import tpu as pltpu
from jax.sharding import PartitionSpec as P

S = 16
AREA = S * S
STEP = 10
LANES = 128

EPSILON_NORM = 1e-06
EPSILON_SQUARE = 1e-30
EPSILON_SCALE = 0.001
LEARN_RATE = 0.3
CLIP_LEVEL = 1.0
AVERAGE_KEEP = 0.9
HALF_ROOT = 0.7071067811865476
DENSITY = 0.3989422804014327
DECAY = 1.0 - STEP ** (-0.8)
FRESH = 1.0 - DECAY
ERF_P = 0.3275911
ERF_A = (0.254829592, -0.284496736, 1.421413741, -1.453152027, 1.061405429)
CHUNKS = 2
PARTS = 4
VMEM = 60 * 1024 * 1024

f32 = jnp.float32
bf16 = jnp.bfloat16
NT = (((1,), (1,)), ((), ()))
TN = (((0,), (0,)), ((), ()))
NN = (((1,), (0,)), ((), ()))


def dot(left, right, dims=NN):
    return lax.dot_general(left, right, dims, preferred_element_type=f32)


def params(**extra):
    return pltpu.CompilerParams(vmem_limit_bytes=VMEM, **extra)


def cost(flops, nbytes):
    return pl.CostEstimate(flops=int(flops), bytes_accessed=int(nbytes), transcendentals=0)


def image_mask(sizes_ref, image):
    place = lax.broadcasted_iota(jnp.int32, (1, AREA), 1)
    row, column = lax.shift_right_logical(place, 4), place & (S - 1)
    inside = (row < sizes_ref[image, 0]) & (column < sizes_ref[image, 1])
    return jnp.where(inside, 1.0, 0.0).astype(f32)


def first_power(table, half):
    base = half * 256
    rate = jnp.exp(table[base : base + 64])
    freq = table[base + 64 : base + 128]
    damp = jnp.exp(-rate)
    return (
        rate,
        damp * jnp.cos(freq),
        damp * jnp.sin(freq),
        table[base + 128 : base + 192],
        table[base + 192 : base + 256],
    )


def taps_kernel(params_ref, out_ref):
    table = params_ref[...].T
    for half in range(2):
        _, step_real, step_imag, real, imag = first_power(table, half)
        here_real, here_imag = jnp.ones_like(step_real), jnp.zeros_like(step_real)
        for place in range(S):
            tap = jnp.sum(real * here_real - imag * here_imag, axis=0, keepdims=True)
            out_ref[half, place : place + 1, :] = tap.astype(bf16).astype(f32)
            here_real, here_imag = (
                here_real * step_real - here_imag * step_imag,
                here_real * step_imag + here_imag * step_real,
            )


def mixer_taps(mixer_params):
    width = mixer_params.shape[0]
    return pl.pallas_call(
        taps_kernel,
        out_shape=jax.ShapeDtypeStruct((2, S, width), f32),
        compiler_params=params(),
        name="mixer_taps",
    )(mixer_params)


def taps_back(params_ref, grad_ref, table_ref):
    table = params_ref[...].T
    for half in range(2):
        rate, step_real, step_imag, real, imag = first_power(table, half)
        here_real, here_imag = jnp.ones_like(step_real), jnp.zeros_like(step_real)
        zero = jnp.zeros_like(step_real)
        sum_real, sum_imag, far_real, far_imag = zero, zero, zero, zero
        for place in range(S):
            grad = grad_ref[half * S + place : half * S + place + 1, :]
            wave_real, wave_imag = grad * here_real, grad * here_imag
            sum_real, sum_imag = sum_real + wave_real, sum_imag + wave_imag
            far_real, far_imag = far_real + place * wave_real, far_imag + place * wave_imag
            here_real, here_imag = (
                here_real * step_real - here_imag * step_imag,
                here_real * step_imag + here_imag * step_real,
            )
        base = half * 256
        table_ref[base : base + 64] = -rate * (real * far_real - imag * far_imag)
        table_ref[base + 64 : base + 128] = -(real * far_imag + imag * far_real)
        table_ref[base + 128 : base + 192] = sum_real
        table_ref[base + 192 : base + 256] = -sum_imag


def block_rows(place):
    return slice(place * S, (place + 1) * S)


def causal(source_ref, taps_ref, half, lanes, base=0):
    rows = [source_ref[base + place * S : base + (place + 1) * S, lanes] for place in range(S)]
    for place in range(S):
        total = rows[place] * taps_ref[half, 0:1, lanes]
        for back in range(1, place + 1):
            total += rows[place - back] * taps_ref[half, back : back + 1, lanes]
        yield total


def anticausal(source_ref, taps_ref, half, lanes):
    rows = [source_ref[block_rows(place), lanes] for place in range(S)]
    for place in range(S):
        total = rows[place] * taps_ref[half, 0:1, lanes]
        for ahead in range(1, S - place):
            total += rows[place + ahead] * taps_ref[half, ahead : ahead + 1, lanes]
        yield total


def mixer_kernel(
    sizes_ref, pixels_ref, taps_ref, channel_ref, turn_ref, mixed_ref, first_ref, cells_ref, low_ref, wide_ref, *, per_step
):
    width = pixels_ref.shape[0]
    for part in range(per_step):
        spot = slice(part * AREA, (part + 1) * AREA)
        mask = image_mask(sizes_ref, pl.program_id(0) * per_step + part)
        masked = (pixels_ref[:, spot].astype(f32) * mask).astype(bf16)
        cells, low, wide = cells_ref.at[part], low_ref.at[part], wide_ref.at[part]
        cells[...] = dot(turn_ref[...], masked, NT)
        for start in range(0, width, LANES):
            lanes = slice(start, start + LANES)
            for place, value in enumerate(causal(cells, taps_ref, 0, lanes)):
                low[block_rows(place), lanes] = value.astype(bf16)
        wide[...] = dot(turn_ref[AREA:, :], low[...])
        first_ref[spot, :] = wide[...].astype(bf16)
        for start in range(0, width, LANES):
            lanes = slice(start, start + LANES)
            skip = channel_ref[2:3, lanes]
            for place, value in enumerate(causal(wide, taps_ref, 1, lanes)):
                own = cells[AREA + place * S : AREA + (place + 1) * S, lanes]
                low[block_rows(place), lanes] = (value + skip * own).astype(bf16)
        mixed_ref[:, spot] = dot(low[...], turn_ref[AREA:, :], TN).astype(bf16)


def mixer_forward(sizes, pixels, taps, channel, turn):
    width, count = pixels.shape
    per_step = 2
    span = per_step * AREA
    grid_spec = pltpu.PrefetchScalarGridSpec(
        num_scalar_prefetch=1,
        grid=(count // span,),
        in_specs=[
            pl.BlockSpec((width, span), lambda i, *_: (0, i)),
            pl.BlockSpec(taps.shape, lambda i, *_: (0, 0, 0)),
            pl.BlockSpec(channel.shape, lambda i, *_: (0, 0)),
            pl.BlockSpec(turn.shape, lambda i, *_: (0, 0)),
        ],
        out_specs=[
            pl.BlockSpec((width, span), lambda i, *_: (0, i)),
            pl.BlockSpec((span, width), lambda i, *_: (i, 0)),
        ],
        scratch_shapes=[
            pltpu.VMEM((per_step, 2 * AREA, width), f32),
            pltpu.VMEM((per_step, AREA, width), bf16),
            pltpu.VMEM((per_step, AREA, width), f32),
        ],
    )
    return pl.pallas_call(
        functools.partial(mixer_kernel, per_step=per_step),
        grid_spec=grid_spec,
        out_shape=[
            jax.ShapeDtypeStruct((width, count), bf16),
            jax.ShapeDtypeStruct((count, width), bf16),
        ],
        compiler_params=params(),
        cost_estimate=cost(8e9, 9e6),
        name="mixer_forward",
    )(sizes, pixels, taps, channel, turn)


def norm_kernel(
    place_ref, sizes_ref, own_ref, other_ref, own_grad_ref, other_grad_ref, own_cols_ref, other_cols_ref, act_ref, low_ref, stat_ref, *, per_step
):
    width = 2.0 * own_ref.shape[0]
    mine = place_ref[0]
    for part in range(per_step):
        spot = slice(part * AREA, (part + 1) * AREA)
        mask = image_mask(sizes_ref, pl.program_id(0) * per_step + part)
        own, other = own_ref[:, spot].astype(f32), other_ref[:, spot].astype(f32)
        mean = (jnp.sum(own, axis=0, keepdims=True) + jnp.sum(other, axis=0, keepdims=True)) / width
        own, other = own - mean, other - mean
        spread = (
            jnp.sum(own * own, axis=0, keepdims=True) + jnp.sum(other * other, axis=0, keepdims=True)
        ) / width
        scale = lax.rsqrt(spread + EPSILON_NORM)
        stat_ref[0:1, spot] = mean
        stat_ref[1:2, spot] = scale
        for which, value, grad_ref, cols_ref in (
            (mine, own, own_grad_ref, own_cols_ref),
            (1 - mine, other, other_grad_ref, other_cols_ref),
        ):
            act_ref[which, :, spot] = (
                value * scale * cols_ref[:, 0:1] + cols_ref[:, 1:2]
            ).astype(bf16)
            grad = grad_ref[:, spot].astype(f32)
            low_ref[which, :, spot] = (grad * (mask * cols_ref[:, 3:4])).astype(bf16)


def norm_forward(place, sizes, own, other, own_grad, other_grad, own_cols, other_cols):
    width, count = own.shape
    per_step = 2
    span = per_step * AREA
    block = pl.BlockSpec((width, span), lambda i, *_: (0, i))
    cols = pl.BlockSpec(own_cols.shape, lambda i, *_: (0, 0))
    pair = pl.BlockSpec((2, width, span), lambda i, *_: (0, 0, i))
    grid_spec = pltpu.PrefetchScalarGridSpec(
        num_scalar_prefetch=2,
        grid=(count // span,),
        in_specs=[block, block, block, block, cols, cols],
        out_specs=[pair, pair, pl.BlockSpec((8, span), lambda i, *_: (0, i))],
    )
    return pl.pallas_call(
        functools.partial(norm_kernel, per_step=per_step),
        grid_spec=grid_spec,
        out_shape=[
            jax.ShapeDtypeStruct((2, width, count), bf16),
            jax.ShapeDtypeStruct((2, width, count), bf16),
            jax.ShapeDtypeStruct((8, count), f32),
        ],
        compiler_params=params(),
        cost_estimate=cost(1e9, 26e6),
        name="norm_forward",
    )(place, sizes, own, other, own_grad, other_grad, own_cols, other_cols)


def weights_kernel(up_ref, down_ref, up_low_ref, up_turned_ref, down_low_ref, down_turned_ref, square_ref):
    @pl.when(pl.program_id(0) == 0)
    def _():
        square_ref[...] = jnp.zeros_like(square_ref)

    for row, source_ref, low_ref, turned_ref in (
        (0, up_ref, up_low_ref, up_turned_ref),
        (1, down_ref, down_low_ref, down_turned_ref),
    ):
        value = source_ref[...]
        units = square_ref.shape[1]
        for start in range(0, value.shape[1], units):
            part = value[:, start : start + units]
            square_ref[row : row + 1, :] += jnp.sum(part * part, axis=0, keepdims=True)
        low_ref[...] = value.astype(bf16)
        turned_ref[...] = value.T.astype(bf16)


def weights_low(up, down):
    full, hidden_local = up.shape
    units = 384
    column = lambda i: (0, i)
    row = lambda i: (i, 0)
    return pl.pallas_call(
        weights_kernel,
        grid=(hidden_local // units,),
        in_specs=[pl.BlockSpec((full, units), column), pl.BlockSpec((full // 2, full), row)],
        out_specs=[
            pl.BlockSpec((full, units), column),
            pl.BlockSpec((units, full), row),
            pl.BlockSpec((units, full), row),
            pl.BlockSpec((full, units), column),
            pl.BlockSpec((8, units), lambda i: (0, 0)),
        ],
        out_shape=[
            jax.ShapeDtypeStruct((full, hidden_local), bf16),
            jax.ShapeDtypeStruct((hidden_local, full), bf16),
            jax.ShapeDtypeStruct((hidden_local, full), bf16),
            jax.ShapeDtypeStruct((full, hidden_local), bf16),
            jax.ShapeDtypeStruct((8, units), f32),
        ],
        compiler_params=params(),
        cost_estimate=cost(1e7, 19e6),
        name="weights_low",
    )(up, down)


def gelu_pair(pre):
    bell = jnp.exp(-0.5 * pre * pre)
    base = 1.0 + (ERF_P * HALF_ROOT) * jnp.abs(pre)
    guess = pl.reciprocal(base, approx=True)
    part = guess * (2.0 - base * guess)
    poly = 0.5 * ERF_A[4]
    for factor in ERF_A[3::-1]:
        poly = poly * part + 0.5 * factor
    tail = poly * part * bell
    upper = jnp.where(pre >= 0.0, 1.0 - tail, tail)
    return pre * upper, upper + pre * bell * DENSITY


def split_out(source_ref, digit, send_refs, keep_ref):
    rows = keep_ref.shape[0]
    for away, ref in enumerate([keep_ref] + list(send_refs)):
        start = pl.multiple_of((digit ^ away) * rows, rows)
        ref[...] = source_ref[pl.ds(start, rows), :].astype(ref.dtype)


def chunk_kernel(
    place_ref,
    act_ref,
    low_ref,
    up_ref,
    down_ref,
    bias_ref,
    *refs,
):
    hidden_ref, slope_ref, up_send_ref, up_keep_ref, down_send_ref, down_keep_ref, bias_grad_ref = refs[-10:-3]
    up_acc, down_acc, bias_acc = refs[-3:]
    step = pl.program_id(0)

    @pl.when(step == 0)
    def _():
        up_acc[...] = jnp.zeros_like(up_acc)
        down_acc[...] = jnp.zeros_like(down_acc)
        bias_acc[...] = jnp.zeros_like(bias_acc)

    halves, width, span = act_ref.shape
    act = act_ref[...].reshape(halves * width, span)
    low = low_ref[...].reshape(halves * width, span)
    tile = 256

    def products(start):
        spot = slice(start, start + tile)
        return dot(up_ref[...], act[:, spot]) + bias_ref[...], dot(down_ref[...], low[:, spot])

    ready = products(0)
    for start in range(0, span, tile):
        pre, back = ready
        if start + tile < span:
            ready = products(start + tile)
        spot = slice(start, start + tile)
        hidden, slope = gelu_pair(pre)
        hidden_ref[:, spot] = hidden.astype(bf16)
        slope_ref[:, spot] = (back * slope).astype(bf16)
    slopes = slope_ref[...]
    up_acc[...] += dot(act, slopes, NT)
    down_acc[...] += dot(hidden_ref[...], low, NT)
    bias_acc[...] += dot(jnp.ones((S, span), bf16), slopes, NT)

    @pl.when(step == pl.num_programs(0) - 1)
    def _():
        split_out(up_acc, place_ref[1], [up_send_ref], up_keep_ref)
        split_out(down_acc, place_ref[2], [down_send_ref], down_keep_ref)
        bias_grad_ref[...] = bias_acc[0:8, :]


def feed_chunk(chunk, place, act, low, up_turned, down, bias, earlier):
    halves, width, count = act.shape
    full = halves * width
    hidden_local = down.shape[0]
    units = hidden_local // CHUNKS
    span = 512
    pair = pl.BlockSpec((halves, width, span), lambda i, *_: (0, 0, i))
    weight = pl.BlockSpec((units, full), lambda i, *_: (chunk, 0))
    wide = pl.BlockSpec((units, span), lambda i, *_: (chunk, i))
    whole = lambda i, *_: (0, 0)
    anywhere = pl.BlockSpec(memory_space=pl.ANY)
    grid_spec = pltpu.PrefetchScalarGridSpec(
        num_scalar_prefetch=1,
        grid=(count // span,),
        in_specs=[pair, pair, weight, weight, pl.BlockSpec((units, 1), lambda i, *_: (chunk, 0))]
        + [anywhere] * len(earlier),
        out_specs=[
            wide,
            wide,
            pl.BlockSpec((full // 2, units), whole),
            pl.BlockSpec((full // 2, units), whole),
            pl.BlockSpec((units // 2, full), whole),
            pl.BlockSpec((units // 2, full), whole),
            pl.BlockSpec((8, units), whole),
        ],
        scratch_shapes=[
            pltpu.VMEM((full, units), f32),
            pltpu.VMEM((units, full), f32),
            pltpu.VMEM((S, units), f32),
        ],
    )
    return pl.pallas_call(
        chunk_kernel,
        grid_spec=grid_spec,
        out_shape=[
            jax.ShapeDtypeStruct((hidden_local, count), bf16),
            jax.ShapeDtypeStruct((hidden_local, count), bf16),
            jax.ShapeDtypeStruct((full // 2, units), bf16),
            jax.ShapeDtypeStruct((full // 2, units), f32),
            jax.ShapeDtypeStruct((units // 2, full), bf16),
            jax.ShapeDtypeStruct((units // 2, full), f32),
            jax.ShapeDtypeStruct((8, units), f32),
        ],
        input_output_aliases={6: 0, 7: 1} if earlier else {},
        compiler_params=params(),
        cost_estimate=cost(8 * count * full * units, 4 * count * (full + units)),
        name="feed_chunk_%d" % chunk,
    )(place, act, low, up_turned, down, bias, *earlier)


def stage_kernel(place_ref, *refs, digits, gains):
    at = 0
    ins, outs = [], []
    for gain in gains:
        ins.append(refs[at : at + 1 + gain[0]])
        at += 1 + gain[0]
    at += gains[0][2]
    for gain in gains:
        outs.append(refs[at : at + gain[1]])
        at += gain[1]
    for source, target, digit, total_ref in zip(ins, outs, digits, refs[at:]):
        total = source[0][...]
        for ref in source[1:]:
            total = total + ref[...].astype(f32)
        if len(target) == 1:
            target[0][...] = total.astype(target[0].dtype)
        else:
            total_ref[...] = total
            split_out(total_ref, place_ref[digit], target[:-1], target[-1])


def stage(place, sums, digits, radix, after, name):
    operands, gains, out_shape, scratch = [], [], [], []
    for group in sums:
        kept = group[0]
        gains.append((len(group) - 1, radix, len(after)))
        operands += list(group)
        rows, columns = kept.shape
        out_shape += [jax.ShapeDtypeStruct((rows // radix, columns), bf16)] * (radix - 1)
        out_shape.append(jax.ShapeDtypeStruct((rows // radix, columns), f32 if radix > 1 else bf16))
        scratch.append(pltpu.VMEM(kept.shape, f32))
    in_vmem = pl.BlockSpec(memory_space=pltpu.VMEM)
    values = pl.pallas_call(
        functools.partial(stage_kernel, digits=digits, gains=gains),
        in_specs=[pl.BlockSpec(memory_space=pltpu.SMEM)]
        + [in_vmem] * len(operands)
        + [pl.BlockSpec(memory_space=pl.ANY)] * len(after),
        out_specs=[in_vmem] * len(out_shape),
        out_shape=out_shape,
        scratch_shapes=scratch,
        compiler_params=params(),
        cost_estimate=cost(1e6, 4e6),
        name=name,
    )(place, *operands, *after)
    return [values[at * radix : (at + 1) * radix] for at in range(len(sums))]


def stack_kernel(place_ref, *refs, count, waits):
    for at in range(2):
        target = refs[2 * count + waits + at]
        rows = refs[0].shape[0]
        for away in range(count):
            start = pl.multiple_of((place_ref[3] ^ away) * rows, rows)
            target[pl.ds(start, rows), :] = refs[at * count + away][...]


def stack(place, pieces, after, name):
    count = len(pieces[0])
    operands = [piece for group in pieces for piece in group]
    in_vmem = pl.BlockSpec(memory_space=pltpu.VMEM)
    return pl.pallas_call(
        functools.partial(stack_kernel, count=count, waits=len(after)),
        in_specs=[pl.BlockSpec(memory_space=pltpu.SMEM)]
        + [in_vmem] * len(operands)
        + [pl.BlockSpec(memory_space=pl.ANY)] * len(after),
        out_specs=[in_vmem] * 2,
        out_shape=[
            jax.ShapeDtypeStruct((count * group[0].shape[0], group[0].shape[1]), bf16) for group in pieces
        ],
        compiler_params=params(),
        cost_estimate=cost(1e6, 2e6),
        name=name,
    )(place, *operands, *after)


def across(value, stride):
    size = lax.axis_size("img")
    return lax.ppermute(value, "img", [(i, i ^ stride) for i in range(size)])


LINE = 4
FIRST, SECOND = 1, 2


class GradientSum:
    def __init__(self, chunk, place, up, down):
        self.chunk, self.place, self.at = chunk, place, 0
        self.kept = [up[1], down[1]]
        self.got = [[across(up[0], FIRST)], [across(down[0], SECOND)]]
        self.stacks = None

    def name(self):
        return "img_%d_%d" % (self.chunk, self.at)

    def step(self, after):
        if self.stacks is not None:
            return None
        done = None
        if self.at == 0:
            outs = stage(self.place, list(zip(self.kept, *zip(*self.got))), (2, 1), 2, after, self.name())
            self.kept = [out[1] for out in outs]
            self.got = [[across(outs[0][0], SECOND)], [across(outs[1][0], FIRST)]]
            done = self.kept[0]
        elif self.at == 1:
            sums = [(kept, *got) for kept, got in zip(self.kept, self.got)]
            outs = stage(self.place, sums, (3, 3), LINE, after, self.name())
            self.kept = [out[-1] for out in outs]
            self.got = [[across(out[away - 1], LINE * away) for away in range(1, LINE)] for out in outs]
            done = self.kept[0]
        elif self.at == 2:
            sums = [(kept, *got) for kept, got in zip(self.kept, self.got)]
            outs = stage(self.place, sums, (0, 0), 1, after, self.name())
            pieces = [out[0] for out in outs]
            stride = LINE * LINE
            while stride < lax.axis_size("img"):
                pieces = [
                    (piece.astype(f32) + across(piece, stride).astype(f32)).astype(bf16) for piece in pieces
                ]
                stride *= 2
            self.got = [[piece] + [across(piece, LINE * away) for away in range(1, LINE)] for piece in pieces]
            done = pieces[0]
        elif self.at == 3:
            own = stack(self.place, self.got, after, self.name())
            near = [across(own[0], SECOND), across(own[1], FIRST)]
            far = [
                [across(own[0], FIRST), across(near[0], FIRST)],
                [across(own[1], SECOND), across(near[1], SECOND)],
            ]
            self.stacks = [[own[at], near[at]] + far[at] for at in range(2)]
            done = own[0]
        self.at += 1
        return done


def small_sum(value):
    for base in (1, LINE):
        near = value + across(value, base)
        far = across(value, 2 * base) + across(value, 3 * base)
        value = near + far
    stride = LINE * LINE
    while stride < lax.axis_size("img"):
        value = value + across(value, stride)
        stride *= 2
    return value


def sums_kernel(place_ref, hidden_ref, slope_ref, down_ref, up_ref, own_ref, other_ref, stat_ref, own_cols_ref, other_cols_ref, *refs):
    own_proj_ref, other_proj_ref, own_act_ref, other_act_ref, sum_ref, total_ref = refs[-6:]
    width = own_ref.shape[0]
    mine = place_ref[0]
    own_rows = pl.ds(pl.multiple_of(mine * width, width), width)
    other_rows = pl.ds(pl.multiple_of((1 - mine) * width, width), width)
    total_ref[0] = dot(down_ref[...], hidden_ref[...])
    total_ref[1] = dot(up_ref[...], slope_ref[...])
    own_proj_ref[...] = total_ref[0, own_rows, :]
    other_proj_ref[...] = total_ref[0, other_rows, :].astype(bf16)
    mean, scale = stat_ref[0:1, :], stat_ref[1:2, :]
    sums = []
    for rows, out_ref, value_ref, cols_ref in (
        (own_rows, own_act_ref, own_ref, own_cols_ref),
        (other_rows, other_act_ref, other_ref, other_cols_ref),
    ):
        act = total_ref[1, rows, :]
        out_ref[...] = act.astype(out_ref.dtype)
        act = act * cols_ref[:, 0:1]
        normed = (value_ref[...].astype(f32) - mean) * scale
        sums.append(jnp.sum(act, axis=0, keepdims=True))
        sums.append(jnp.sum(act * normed, axis=0, keepdims=True))
    sum_ref[0:1, :] = sums[0] + sums[2]
    sum_ref[1:2, :] = sums[1] + sums[3]


def hidden_sums(place, hidden, slopes, down_turned, up, own, other, stat, own_cols, other_cols, part, after):
    width, total = own.shape
    count = total // PARTS
    hidden_local = hidden.shape[0]
    span = 512
    base = part * (count // span)
    column = lambda i, *_: (0, base + i)
    out = lambda i, *_: (0, i)
    fixed = lambda i, *_: (0, 0)
    wide = pl.BlockSpec((hidden_local, span), column)
    block = pl.BlockSpec((width, span), column)
    result = pl.BlockSpec((width, span), out)
    cols = pl.BlockSpec(own_cols.shape, fixed)
    grid_spec = pltpu.PrefetchScalarGridSpec(
        num_scalar_prefetch=1,
        grid=(count // span,),
        in_specs=[
            wide,
            wide,
            pl.BlockSpec(down_turned.shape, fixed),
            pl.BlockSpec(up.shape, fixed),
            block,
            block,
            pl.BlockSpec((8, span), column),
            cols,
            cols,
        ]
        + [pl.BlockSpec(memory_space=pl.ANY)] * len(after),
        out_specs=[result, result, result, result, pl.BlockSpec((8, span), out)],
        scratch_shapes=[pltpu.VMEM((2, 2 * width, span), f32)],
    )
    return pl.pallas_call(
        sums_kernel,
        grid_spec=grid_spec,
        out_shape=[
            jax.ShapeDtypeStruct((width, count), f32),
            jax.ShapeDtypeStruct((width, count), bf16),
            jax.ShapeDtypeStruct((width, count), f32),
            jax.ShapeDtypeStruct((width, count), bf16),
            jax.ShapeDtypeStruct((8, count), f32),
        ],
        compiler_params=params(),
        cost_estimate=cost(8 * count * width * hidden_local, 4 * count * (hidden_local + 3 * width)),
        name="hidden_sums_%d" % part,
    )(place, hidden, slopes, down_turned, up, own, other, stat, own_cols, other_cols, *after)


TAPS, ROWS, BIAS = 0, 32, 40


def correlate(left_ref, right_ref, sum_ref, half, lanes):
    left = [left_ref[block_rows(place), lanes] for place in range(S)]
    right = [right_ref[block_rows(place), lanes].astype(f32) for place in range(S)]
    for back in range(S):
        total = left[back] * right[0]
        for place in range(back + 1, S):
            total += left[place] * right[place - back]
        sum_ref[half, block_rows(back), lanes] += total


def backward_kernel(
    sizes_ref,
    pixels_ref,
    grad_ref,
    mixed_ref,
    first_ref,
    stat_ref,
    own_proj_ref,
    got_proj_ref,
    own_act_ref,
    got_act_ref,
    own_sum_ref,
    got_sum_ref,
    cols_ref,
    taps_ref,
    turn_ref,
    carry_ref,
    *refs,
    base,
):
    out_ref, pixel_grad_ref, small_ref, sum_ref, channel_sum, cells_ref, low_ref, wide_ref, back_ref = refs[-9:]
    step = pl.program_id(0)
    width = pixels_ref.shape[0]
    full = 2.0 * width

    @pl.when(step == 0)
    def _():
        sum_ref[...] = jnp.zeros_like(sum_ref)
        channel_sum[...] = jnp.zeros_like(channel_sum)

    mask = image_mask(sizes_ref, base + step)
    pixels = pixels_ref[...].astype(f32)
    grad = grad_ref[...].astype(f32)
    masked = pixels * mask
    gain, skip, layer, shift = cols_ref[:, 0:1], cols_ref[:, 2:3], cols_ref[:, 3:4], cols_ref[:, 4:5]

    def gather(row, value):
        channel_sum[row] += value[:, :LANES] + value[:, LANES:]

    masked_grad = grad * mask
    branch = own_proj_ref[...] + got_proj_ref[...].astype(f32) + shift
    out_ref[...] = pixels + mask * layer * branch
    gather(3, masked_grad * branch)
    gather(4, masked_grad)

    scale = stat_ref[1:2, :]
    normed = (mixed_ref[...].astype(f32) - stat_ref[0:1, :]) * scale
    act = own_act_ref[...] + got_act_ref[...].astype(f32)
    gather(0, act * normed)
    gather(1, act)
    plain = (own_sum_ref[0:1, :] + got_sum_ref[0:1, :]) / full
    tilt = (own_sum_ref[1:2, :] + got_sum_ref[1:2, :]) / full
    mixed_low = (scale * (act * gain - plain - normed * tilt)).astype(bf16)
    mixed_grad = mixed_low.astype(f32)
    gather(2, mixed_grad * masked)

    cells_ref[...] = dot(turn_ref[:AREA, :], masked.astype(bf16), NT)
    wide_ref[...] = dot(turn_ref[AREA:, :], mixed_low, NT)
    for start in range(0, width, LANES):
        lanes = slice(start, start + LANES)
        for place, value in enumerate(anticausal(wide_ref, taps_ref, 1, lanes)):
            low_ref[block_rows(place), lanes] = value.astype(bf16)
        correlate(wide_ref, first_ref, sum_ref, 1, lanes)
    back_ref[...] = dot(turn_ref[AREA:, :], low_ref[...])
    for start in range(0, width, LANES):
        lanes = slice(start, start + LANES)
        for place, value in enumerate(anticausal(back_ref, taps_ref, 0, lanes)):
            wide_ref[block_rows(place), lanes] = value
        correlate(back_ref, cells_ref, sum_ref, 0, lanes)
    pixel_grad_ref[...] = grad + mask * (wide_ref[...].T + skip * mixed_grad)

    @pl.when(step == pl.num_programs(0) - 1)
    def _():
        small_ref[...] = carry_ref[...]
        for half in range(2):
            for back in range(S):
                row = TAPS + half * S + back
                small_ref[row : row + 1, :] += jnp.sum(
                    sum_ref[half, block_rows(back), :], axis=0, keepdims=True
                )
        for row in range(5):
            small_ref[ROWS + row : ROWS + row + 1, :] += jnp.sum(channel_sum[row].T, axis=0, keepdims=True)


def backward(sizes, pixels, grad, mixed, first, stat, own, got, cols, taps, turn, carry, part, after):
    own_proj, own_act, own_sum = own
    got_proj, got_act, got_sum = got
    width, total = pixels.shape
    count = total // PARTS
    base = part * (count // AREA)
    column = lambda i, *_: (0, base + i)
    here = lambda i, *_: (0, i)
    fixed = lambda i, *_: (0, 0)
    block = pl.BlockSpec((width, AREA), column)
    local = pl.BlockSpec((width, AREA), here)
    anywhere = pl.BlockSpec(memory_space=pl.ANY)
    grid_spec = pltpu.PrefetchScalarGridSpec(
        num_scalar_prefetch=1,
        grid=(count // AREA,),
        in_specs=[
            block,
            block,
            block,
            pl.BlockSpec((AREA, width), lambda i, *_: (base + i, 0)),
            pl.BlockSpec((8, AREA), column),
            local,
            local,
            local,
            local,
            pl.BlockSpec((8, AREA), here),
            pl.BlockSpec((8, AREA), here),
            pl.BlockSpec(cols.shape, fixed),
            pl.BlockSpec(taps.shape, lambda i, *_: (0, 0, 0)),
            pl.BlockSpec(turn.shape, fixed),
            pl.BlockSpec(carry.shape, fixed),
        ]
        + [anywhere] * len(after),
        out_specs=[block, block, pl.BlockSpec(carry.shape, fixed)],
        scratch_shapes=[
            pltpu.VMEM((2, AREA, width), f32),
            pltpu.VMEM((5, width, LANES), f32),
            pltpu.VMEM((AREA, width), f32),
            pltpu.VMEM((AREA, width), bf16),
            pltpu.VMEM((AREA, width), f32),
            pltpu.VMEM((AREA, width), f32),
        ],
    )
    return pl.pallas_call(
        functools.partial(backward_kernel, base=base),
        grid_spec=grid_spec,
        out_shape=[
            jax.ShapeDtypeStruct((width, total), f32),
            jax.ShapeDtypeStruct((width, total), f32),
            jax.ShapeDtypeStruct(carry.shape, f32),
        ],
        input_output_aliases={16: 0, 17: 1} if part else {},
        compiler_params=params(),
        cost_estimate=cost(10e9 / PARTS, 44e6 / PARTS),
        name="backward_%d" % part,
    )(
        sizes, pixels, grad, mixed, first, stat, own_proj, got_proj, own_act, got_act, own_sum, got_sum, cols, taps, turn, carry, *after
    )


UP_ROW, UP_MASS, DOWN_COL, DOWN_MASS, MIXER_COL, MIXER_MASS, SCALARS = range(7)


def fold(value):
    total = value[:, :LANES]
    for start in range(LANES, value.shape[1], LANES):
        total += value[:, start : start + LANES]
    return total


def to_column(row):
    return jnp.broadcast_to(row, (LANES, row.shape[1])).T


def to_row(columns):
    return jnp.sum(columns.T, axis=0, keepdims=True)


def statistics_kernel(place_ref, *refs):
    stacks = refs[: 8 * CHUNKS]
    up_cols_ref, down_rows_ref = refs[8 * CHUNKS : 8 * CHUNKS + 2]
    up_ref, down_ref, up_cols_new_ref, down_rows_new_ref, stat_ref, rows_acc, mass_acc = refs[8 * CHUNKS + 2 :]
    step = pl.program_id(0)
    quarter, units = stacks[0].shape
    first, second = place_ref[1], place_ref[2]

    @pl.when(step == 0)
    def _():
        stat_ref[...] = jnp.zeros_like(stat_ref)
        rows_acc[...] = jnp.zeros_like(rows_acc)
        mass_acc[...] = jnp.zeros_like(mass_acc)

    def start_of(flip_half, flip_quarter, half, part):
        rows = ((half ^ flip_half) * 2 + (part ^ flip_quarter)) * quarter
        return pl.ds(pl.multiple_of(rows, quarter), quarter)

    for chunk in range(CHUNKS):

        @pl.when(step == chunk)
        def _():
            up_stacks, down_stacks = stacks[8 * chunk : 8 * chunk + 4], stacks[8 * chunk + 4 : 8 * chunk + 8]
            flips = ((0, 0), (0, 1), (1, 0), (1, 1))
            columns = jnp.zeros((1, units), f32)
            for (half, part), ref in zip(flips, up_stacks):
                rows = start_of(half, part, first, second)
                value = ref[...].astype(f32)
                up_ref[rows, :] = value
                square = value * value
                columns += jnp.sum(square, axis=0, keepdims=True)
                rows_acc[rows, :] += fold(square)
            full = 4 * quarter
            columns = DECAY * up_cols_ref[...] + FRESH * (columns / full + EPSILON_SQUARE)
            up_cols_new_ref[...] = columns
            inverse = 1.0 / columns
            for start in range(0, full, quarter):
                value = up_ref[start : start + quarter, :]
                mass_acc[start : start + quarter, :] += fold(value * value * inverse)

            old = down_rows_ref[...]
            for (half, part), ref in zip(flips, down_stacks):
                rows = start_of(half, part, second, first)
                down_ref[rows, :] = ref[...].astype(f32)
            for start in range(0, full, quarter):
                value = down_ref[start : start + quarter, :]
                square = value * value
                stat_ref[DOWN_COL : DOWN_COL + 1, :] += jnp.sum(square, axis=0, keepdims=True)
                mean = jnp.sum(fold(square), axis=1, keepdims=True) / full
                fresh = DECAY * to_column(old[:, start : start + quarter]) + FRESH * (mean + EPSILON_SQUARE)
                down_rows_new_ref[:, start : start + quarter] = fresh.T[0:1, :]
                stat_ref[DOWN_MASS : DOWN_MASS + 1, :] += jnp.sum(
                    square * (1.0 / fresh[:, 0:1]), axis=0, keepdims=True
                )

    @pl.when(step == CHUNKS - 1)
    def _():
        stat_ref[UP_ROW : UP_ROW + 1, :] = to_row(rows_acc[...])
        stat_ref[UP_MASS : UP_MASS + 1, :] = to_row(mass_acc[...])


def statistics(place, stacks, up_cols, down_rows):
    flat = [array for chunk in stacks for group in chunk for array in group]
    quarter, full = flat[0].shape[0], flat[4].shape[1]
    units = flat[0].shape[1]
    hidden_local = units * CHUNKS
    in_vmem = pl.BlockSpec(memory_space=pltpu.VMEM)
    row = pl.BlockSpec((1, units), lambda i: (0, i))
    return pl.pallas_call(
        statistics_kernel,
        grid=(CHUNKS,),
        in_specs=[pl.BlockSpec(memory_space=pltpu.SMEM)] + [in_vmem] * len(flat) + [row, row],
        out_specs=[
            pl.BlockSpec((full, units), lambda i: (0, i)),
            pl.BlockSpec((units, full), lambda i: (i, 0)),
            row,
            row,
            pl.BlockSpec((8, full), lambda i: (0, 0)),
        ],
        out_shape=[
            jax.ShapeDtypeStruct((full, hidden_local), f32),
            jax.ShapeDtypeStruct((hidden_local, full), f32),
            jax.ShapeDtypeStruct((1, hidden_local), f32),
            jax.ShapeDtypeStruct((1, hidden_local), f32),
            jax.ShapeDtypeStruct((8, full), f32),
        ],
        scratch_shapes=[pltpu.VMEM((full, LANES), f32), pltpu.VMEM((full, LANES), f32)],
        compiler_params=params(),
        cost_estimate=cost(1e8, 14e6),
        name="statistics",
    )(place, *flat, up_cols, down_rows)


def small_kernel(
    sum_ref,
    stat_ref,
    square_ref,
    params_ref,
    channel_ref,
    moment_ref,
    bias_ref,
    bias_moment_ref,
    rows_ref,
    down_rows_new_ref,
    mixer_grad_ref,
    rows_new_ref,
    channel_grad_ref,
    moment_new_ref,
    channel_update_ref,
    bias_grad_ref,
    bias_moment_new_ref,
    bias_update_ref,
    out_ref,
    channel_square_ref,
    table_ref,
):
    out_ref[...] = stat_ref[...]
    taps_back(params_ref, sum_ref, table_ref)
    grad = table_ref[...].T
    mixer_grad_ref[...] = grad
    states = grad.shape[1]
    square = grad * grad
    mean = jnp.sum(fold(square), axis=1, keepdims=True) / states
    fresh = DECAY * to_column(rows_ref[...]) + FRESH * (mean + EPSILON_SQUARE)
    rows_new = fresh.T[0:1, :]
    rows_new_ref[...] = rows_new
    out_ref[MIXER_COL : MIXER_COL + 1, :states] = jnp.sum(square, axis=0, keepdims=True)
    out_ref[MIXER_MASS : MIXER_MASS + 1, :states] = jnp.sum(square * (1.0 / fresh[:, 0:1]), axis=0, keepdims=True)

    layer = channel_ref[3:4, :]
    channel_grad_ref[0:4, :] = sum_ref[ROWS : ROWS + 4, :]
    channel_grad_ref[4:5, :] = sum_ref[ROWS + 4 : ROWS + 5, :] * layer
    grad = channel_grad_ref[...]
    moment = DECAY * moment_ref[...] + FRESH * (grad * grad + EPSILON_SQUARE)
    moment_new_ref[...] = moment
    channel_update = grad * lax.rsqrt(moment)
    channel_update_ref[...] = channel_update

    width = layer.shape[1]
    for at in range(bias_grad_ref.shape[1] // width):
        bias_grad_ref[:, at * width : (at + 1) * width] = sum_ref[BIAS + at : BIAS + at + 1, :]
    grad = bias_grad_ref[...]
    moment = DECAY * bias_moment_ref[...] + FRESH * (grad * grad + EPSILON_SQUARE)
    bias_moment_new_ref[...] = moment
    bias_update = grad * lax.rsqrt(moment)
    bias_update_ref[...] = bias_update

    def total(value):
        return jnp.sum(value, keepdims=True)

    channel = channel_ref[...]
    table = params_ref[...]
    bias = bias_ref[...]
    scalars = (
        total(channel_update * channel_update) + total(bias_update * bias_update),
        total(down_rows_new_ref[...]),
        total(rows_new),
        total(square_ref[0:1, :]),
        total(square_ref[1:2, :]),
        total(table * table),
        total(bias * bias),
    )
    for at, value in enumerate(scalars):
        out_ref[SCALARS : SCALARS + 1, at * LANES : (at + 1) * LANES] = jnp.broadcast_to(value, (1, LANES))
    channel_square_ref[...] = jnp.broadcast_to(jnp.sum(channel * channel, axis=1, keepdims=True), (5, LANES))


def small_update(total, stat, square, mixer_params, channel_params, channel_moment, bias, bias_moment, rows, down_rows_new):
    width, states = mixer_params.shape
    shapes = [
        (width, states),
        (1, width),
        channel_params.shape,
        channel_params.shape,
        channel_params.shape,
        bias.shape,
        bias.shape,
        bias.shape,
        (8, 8 * LANES),
        (5, LANES),
    ]
    return pl.pallas_call(
        small_kernel,
        out_shape=[jax.ShapeDtypeStruct(shape, f32) for shape in shapes],
        scratch_shapes=[pltpu.VMEM((states, width), f32)],
        compiler_params=params(),
        cost_estimate=cost(1e7, 2e6),
        name="small_update",
    )(total, stat, square, mixer_params, channel_params, channel_moment, bias, bias_moment, rows, down_rows_new)


def update_kernel(
    stat_ref,
    got_ref,
    channel_square_ref,
    channel_got_ref,
    up_rows_ref,
    down_cols_ref,
    mixer_cols_ref,
    up_cols_new_ref,
    down_rows_new_ref,
    up_grad_ref,
    up_ref,
    up_average_ref,
    down_grad_ref,
    down_ref,
    down_average_ref,
    mixer_grad_ref,
    mixer_ref,
    mixer_average_ref,
    mixer_rows_new_ref,
    channel_ref,
    channel_average_ref,
    channel_update_ref,
    bias_ref,
    bias_average_ref,
    bias_update_ref,
    rms_ref,
    up_rows_new_ref,
    down_cols_new_ref,
    mixer_cols_new_ref,
    up_new_ref,
    up_average_new_ref,
    down_new_ref,
    down_average_new_ref,
    mixer_new_ref,
    mixer_average_new_ref,
    channel_new_ref,
    channel_average_new_ref,
    bias_new_ref,
    bias_average_new_ref,
):
    full, hidden = up_rows_ref.shape[1], 2 * bias_ref.shape[1]
    states = mixer_cols_ref.shape[1]

    def stat(row, size):
        return stat_ref[row : row + 1, :size] + got_ref[row : row + 1, :size]

    def scalar(at):
        return stat(SCALARS, 8 * LANES)[:, at * LANES : at * LANES + 1]

    def total(value):
        return jnp.sum(value, axis=1, keepdims=True)

    up_rows_new = DECAY * up_rows_ref[...] + FRESH * (stat(UP_ROW, full) / hidden + EPSILON_SQUARE)
    down_cols_new = DECAY * down_cols_ref[...] + FRESH * (stat(DOWN_COL, full) / hidden + EPSILON_SQUARE)
    mixer_cols_new = DECAY * mixer_cols_ref[...] + FRESH * (stat(MIXER_COL, states) / full + EPSILON_SQUARE)
    up_mean = total(up_rows_new) / full
    down_mean = scalar(1) / hidden
    mixer_mean = scalar(2) / full
    square = (
        scalar(0)
        + up_mean * total(stat(UP_MASS, full) / up_rows_new)
        + down_mean * total(stat(DOWN_MASS, full) / down_cols_new)
        + mixer_mean * total(stat(MIXER_MASS, states) / mixer_cols_new)
    )
    rms = jnp.sqrt(square / (2 * full * hidden + states * full + 5 * full + hidden))
    factor = LEARN_RATE * CLIP_LEVEL / jnp.maximum(CLIP_LEVEL, rms)

    def rate(squares, size):
        return factor * jnp.maximum(EPSILON_SCALE, jnp.sqrt(squares / size))

    def settle(weight, change, average_ref, new_ref, average_new_ref):
        new = weight - change
        new_ref[...] = new
        average_new_ref[...] = AVERAGE_KEEP * average_ref[...] + (1.0 - AVERAGE_KEEP) * new

    def column(row):
        return to_column(row)[:, 0:1]

    up_speed = rate(scalar(3), full * hidden) * jnp.sqrt(up_mean)
    settle(
        up_ref[...],
        up_grad_ref[...] * column(lax.rsqrt(up_rows_new) * up_speed) * lax.rsqrt(up_cols_new_ref[...]),
        up_average_ref,
        up_new_ref,
        up_average_new_ref,
    )
    down_speed = rate(scalar(4), full * hidden) * jnp.sqrt(down_mean)
    settle(
        down_ref[...],
        down_grad_ref[...] * column(lax.rsqrt(down_rows_new_ref[...]) * down_speed) * lax.rsqrt(down_cols_new),
        down_average_ref,
        down_new_ref,
        down_average_new_ref,
    )

    @pl.when(pl.program_id(0) == 0)
    def _():
        rms_ref[...] = rms
        up_rows_new_ref[...] = up_rows_new
        down_cols_new_ref[...] = down_cols_new
        mixer_cols_new_ref[...] = mixer_cols_new
        mixer_speed = rate(scalar(5), states * full) * jnp.sqrt(mixer_mean)
        settle(
            mixer_ref[...],
            mixer_grad_ref[...]
            * column(lax.rsqrt(mixer_rows_new_ref[...]) * mixer_speed)
            * lax.rsqrt(mixer_cols_new),
            mixer_average_ref,
            mixer_new_ref,
            mixer_average_new_ref,
        )
        channel_square = channel_square_ref[:, 0:1] + channel_got_ref[:, 0:1]
        settle(
            channel_ref[...],
            rate(channel_square, full) * channel_update_ref[...],
            channel_average_ref,
            channel_new_ref,
            channel_average_new_ref,
        )
        settle(
            bias_ref[...],
            rate(scalar(6), hidden) * bias_update_ref[...],
            bias_average_ref,
            bias_new_ref,
            bias_average_new_ref,
        )


def final_update(operands, units):
    up, mixer, channel, bias = operands[10], operands[16], operands[19], operands[22]
    full, hidden_local = up.shape
    fixed = lambda i: (0, 0)
    up_block = pl.BlockSpec((full, units), lambda i: (0, i))
    down_block = pl.BlockSpec((units, full), lambda i: (i, 0))
    row_block = pl.BlockSpec((1, units), lambda i: (0, i))

    def whole(array):
        return pl.BlockSpec(array.shape, fixed)

    in_specs = [whole(array) for array in operands]
    in_specs[7:9] = [row_block, row_block]
    in_specs[9:12] = [up_block] * 3
    in_specs[12:15] = [down_block] * 3
    shapes = [(1, 1), operands[4].shape, operands[5].shape, operands[6].shape]
    shapes += [up.shape] * 2 + [(hidden_local, full)] * 2 + [mixer.shape] * 2 + [channel.shape] * 2 + [bias.shape] * 2
    out_specs = [pl.BlockSpec(shape, fixed) for shape in shapes]
    out_specs[4:8] = [up_block, up_block, down_block, down_block]
    return pl.pallas_call(
        update_kernel,
        grid=(hidden_local // units,),
        in_specs=in_specs,
        out_specs=out_specs,
        out_shape=[jax.ShapeDtypeStruct(shape, f32) for shape in shapes],
        compiler_params=params(),
        cost_estimate=cost(1e8, 48e6),
        name="final_update",
    )(*operands)


def turn_table():
    place = np.arange(AREA)
    swapped = (place % S) * S + place // S
    table = np.concatenate([place[:, None] == place[None, :], swapped[:, None] == place[None, :]])
    return table.astype(ml_dtypes.bfloat16)


def shards(
    pixels,
    image_sizes,
    out_grad,
    up_weight,
    down_weight,
    mixer_params,
    channel_params,
    hidden_bias,
    up_rows,
    up_cols,
    down_rows,
    down_cols,
    mixer_rows,
    mixer_cols,
    channel_moment,
    bias_moment,
    up_average,
    down_average,
    mixer_average,
    channel_average,
    bias_average,
):
    width_local, count = pixels.shape
    hidden_local = up_weight.shape[1]
    index = lax.axis_index("img").astype(jnp.int32)
    place = jnp.stack(
        [lax.axis_index("ch").astype(jnp.int32), index & 1, (index >> 1) & 1, (index >> 2) & (LINE - 1)]
    )

    def exchange(value):
        return lax.ppermute(value, "ch", [(0, 1), (1, 0)])

    def row(value):
        return value.reshape(1, -1)

    other_grad = exchange(out_grad)
    rounded = jnp.concatenate(
        [channel_params[0:2].astype(bf16).astype(f32), channel_params[2:5], jnp.zeros((3, width_local), f32)]
    )
    own_cols = rounded.T
    other_cols = exchange(rounded).T
    turn = jnp.asarray(turn_table())
    taps = mixer_taps(mixer_params)
    mixed, first = mixer_forward(image_sizes, pixels, taps, channel_params, turn)
    other_mixed = exchange(mixed)
    up_low, up_turned, down_low, down_turned, square = weights_low(up_weight, down_weight)
    bias_col = hidden_bias.astype(bf16).astype(f32)[:, None]
    act, low, stat = norm_forward(
        place, image_sizes, mixed, other_mixed, out_grad, other_grad, own_cols, other_cols
    )

    sums, bias_parts = [], []
    earlier = ()
    for chunk in range(CHUNKS):
        values = feed_chunk(chunk, place, act, low, up_turned, down_low, bias_col, earlier)
        earlier = values[0:2]
        bias_parts.append(values[6][0])
        if chunk:
            tokens = [value for value in [each.step((values[0],)) for each in sums] if value is not None]
        sums.append(GradientSum(chunk, place, values[2:4], values[4:6]))
    hidden, slopes = earlier

    def advance(after):
        return [value for value in [each.step((after,)) for each in sums] if value is not None]

    partial = []
    for part in range(PARTS):
        values = hidden_sums(
            place, hidden, slopes, down_turned, up_low, mixed, other_mixed, stat, own_cols, other_cols, part, tokens
        )
        own_proj, send_proj, own_act, send_act, own_sum = values
        partial.append(((own_proj, own_act, own_sum), exchange((send_proj, send_act, own_sum))))
        tokens = advance(own_sum)
    carry = jnp.concatenate(
        [jnp.zeros((BIAS, width_local), f32), jnp.concatenate(bias_parts).reshape(-1, width_local)]
    )
    carry = jnp.pad(carry, ((0, -carry.shape[0] % 8), (0, 0)))
    done = ()
    for part in range(PARTS):
        own, got = partial[part]
        values = backward(
            image_sizes, pixels, out_grad, mixed, first, stat, own, got, own_cols, taps, turn, carry, part, [*done, *tokens]
        )
        done, carry = values[0:2], values[2]
        tokens = advance(carry)
    block_out, pixel_grad = done
    total = small_sum(carry)

    up_sum, down_sum, up_cols_new, down_rows_new, stats = statistics(
        place, [each.stacks for each in sums], row(up_cols), row(down_rows)
    )
    (
        mixer_sum,
        mixer_rows_new,
        channel_sum,
        channel_moment_new,
        channel_update,
        bias_sum,
        bias_moment_new,
        bias_update,
        stats,
        channel_square,
    ) = small_update(
        total,
        jnp.pad(stats, ((0, 0), (0, 8 * LANES - stats.shape[1]))),
        square,
        mixer_params,
        channel_params,
        channel_moment,
        row(hidden_bias),
        row(bias_moment),
        row(mixer_rows),
        down_rows_new,
    )
    got_stats, got_square = exchange((stats, channel_square))
    (
        update_rms,
        up_rows_new,
        down_cols_new,
        mixer_cols_new,
        up_new,
        up_average_new,
        down_new,
        down_average_new,
        mixer_new,
        mixer_average_new,
        channel_new,
        channel_average_new,
        bias_new,
        bias_average_new,
    ) = final_update(
        [
            stats,
            got_stats,
            channel_square,
            got_square,
            row(up_rows),
            row(down_cols),
            row(mixer_cols),
            up_cols_new,
            down_rows_new,
            up_sum,
            up_weight,
            up_average,
            down_sum,
            down_weight,
            down_average,
            mixer_sum,
            mixer_params,
            mixer_average,
            mixer_rows_new,
            channel_params,
            channel_average,
            channel_update,
            row(hidden_bias),
            row(bias_average),
            bias_update,
        ],
        256,
    )
    return (
        block_out,
        pixel_grad,
        update_rms.reshape(()),
        up_sum,
        up_rows_new.reshape(-1),
        up_cols_new.reshape(-1),
        up_new,
        up_average_new,
        down_sum,
        down_rows_new.reshape(-1),
        down_cols_new.reshape(-1),
        down_new,
        down_average_new,
        mixer_sum,
        mixer_rows_new.reshape(-1),
        mixer_cols_new.reshape(-1),
        mixer_new,
        mixer_average_new,
        channel_sum,
        channel_moment_new,
        channel_new,
        channel_average_new,
        bias_sum.reshape(-1),
        bias_moment_new.reshape(-1),
        bias_new.reshape(-1),
        bias_average_new.reshape(-1),
    )


def solution(mesh):
    split = P("ch", "img")
    over_rows, over_cols, over = P("ch", None), P(None, "ch"), P("ch")
    return jax.shard_map(
        shards,
        mesh=mesh,
        in_specs=(
            split,
            P("img", None),
            split,
            over_cols,
            over_rows,
            over_rows,
            over_cols,
            over,
            P(),
            over,
            over,
            P(),
            over,
            P(),
            over_cols,
            over,
            over_cols,
            over_rows,
            over_rows,
            over_cols,
            over,
        ),
        out_specs=(
            split,
            split,
            P(),
            over_cols,
            P(),
            over,
            over_cols,
            over_cols,
            over_rows,
            over,
            P(),
            over_rows,
            over_rows,
            over_rows,
            over,
            P(),
            over_rows,
            over_rows,
            over_cols,
            over_cols,
            over_cols,
            over_cols,
            over,
            over,
            over,
            over,
        ),
        check_vma=False,
    )
```

```python
import functools

import jax
import jax.numpy as jnp
import ml_dtypes
import numpy as np
from jax import lax
from jax.experimental import pallas as pl
from jax.experimental.pallas import tpu as pltpu
from jax.sharding import PartitionSpec as P

S = 16
AREA = S * S
STEP = 10
LANES = 128

EPSILON_NORM = 1e-06
EPSILON_SQUARE = 1e-30
EPSILON_SCALE = 0.001
LEARN_RATE = 0.3
CLIP_LEVEL = 1.0
AVERAGE_KEEP = 0.9
HALF_ROOT = 0.7071067811865476
DENSITY = 0.3989422804014327
DECAY = 1.0 - STEP ** (-0.8)
FRESH = 1.0 - DECAY
ERF_P = 0.3275911
ERF_A = (0.254829592, -0.284496736, 1.421413741, -1.453152027, 1.061405429)
CHUNKS = 2
SUM_PARTS = 2
BACK_PARTS = 4
PLANE = 4
VMEM = 60 * 1024 * 1024

f32 = jnp.float32
bf16 = jnp.bfloat16
NT = (((1,), (1,)), ((), ()))
TN = (((0,), (0,)), ((), ()))
NN = (((1,), (0,)), ((), ()))


def dot(left, right, dims=NN):
    return lax.dot_general(left, right, dims, preferred_element_type=f32)


def params(**extra):
    return pltpu.CompilerParams(vmem_limit_bytes=VMEM, **extra)


def cost(flops, nbytes):
    return pl.CostEstimate(flops=int(flops), bytes_accessed=int(nbytes), transcendentals=0)


def image_mask(sizes_ref, image):
    place = lax.broadcasted_iota(jnp.int32, (1, AREA), 1)
    row, column = lax.shift_right_logical(place, 4), place & (S - 1)
    inside = (row < sizes_ref[image, 0]) & (column < sizes_ref[image, 1])
    return jnp.where(inside, 1.0, 0.0).astype(f32)


def first_power(table, half):
    base = half * 256
    rate = jnp.exp(table[base : base + 64])
    freq = table[base + 64 : base + 128]
    damp = jnp.exp(-rate)
    return (
        rate,
        damp * jnp.cos(freq),
        damp * jnp.sin(freq),
        table[base + 128 : base + 192],
        table[base + 192 : base + 256],
    )


def taps_kernel(params_ref, out_ref):
    table = params_ref[...].T
    for half in range(2):
        _, step_real, step_imag, real, imag = first_power(table, half)
        here_real, here_imag = jnp.ones_like(step_real), jnp.zeros_like(step_real)
        for place in range(S):
            tap = jnp.sum(real * here_real - imag * here_imag, axis=0, keepdims=True)
            out_ref[half, place : place + 1, :] = tap.astype(bf16).astype(f32)
            here_real, here_imag = (
                here_real * step_real - here_imag * step_imag,
                here_real * step_imag + here_imag * step_real,
            )


def mixer_taps(mixer_params):
    width = mixer_params.shape[0]
    return pl.pallas_call(
        taps_kernel,
        out_shape=jax.ShapeDtypeStruct((2, S, width), f32),
        compiler_params=params(),
        name="mixer_taps",
    )(mixer_params)


def taps_back(params_ref, grad_ref, table_ref):
    table = params_ref[...].T
    for half in range(2):
        rate, step_real, step_imag, real, imag = first_power(table, half)
        here_real, here_imag = jnp.ones_like(step_real), jnp.zeros_like(step_real)
        zero = jnp.zeros_like(step_real)
        sum_real, sum_imag, far_real, far_imag = zero, zero, zero, zero
        for place in range(S):
            grad = grad_ref[half * S + place : half * S + place + 1, :]
            wave_real, wave_imag = grad * here_real, grad * here_imag
            sum_real, sum_imag = sum_real + wave_real, sum_imag + wave_imag
            far_real, far_imag = far_real + place * wave_real, far_imag + place * wave_imag
            here_real, here_imag = (
                here_real * step_real - here_imag * step_imag,
                here_real * step_imag + here_imag * step_real,
            )
        base = half * 256
        table_ref[base : base + 64] = -rate * (real * far_real - imag * far_imag)
        table_ref[base + 64 : base + 128] = -(real * far_imag + imag * far_real)
        table_ref[base + 128 : base + 192] = sum_real
        table_ref[base + 192 : base + 256] = -sum_imag


def block_rows(place):
    return slice(place * S, (place + 1) * S)


def causal(source_ref, taps_ref, half, lanes, base=0):
    rows = [source_ref[base + place * S : base + (place + 1) * S, lanes] for place in range(S)]
    for place in range(S):
        total = rows[place] * taps_ref[half, 0:1, lanes]
        for back in range(1, place + 1):
            total += rows[place - back] * taps_ref[half, back : back + 1, lanes]
        yield total


def anticausal(source_ref, taps_ref, half, lanes):
    rows = [source_ref[block_rows(place), lanes] for place in range(S)]
    for place in range(S):
        total = rows[place] * taps_ref[half, 0:1, lanes]
        for ahead in range(1, S - place):
            total += rows[place + ahead] * taps_ref[half, ahead : ahead + 1, lanes]
        yield total


def mixer_kernel(
    sizes_ref, pixels_ref, taps_ref, channel_ref, turn_ref, mixed_ref, first_ref, cells_ref, low_ref, wide_ref, *, per_step
):
    width = pixels_ref.shape[0]
    for part in range(per_step):
        spot = slice(part * AREA, (part + 1) * AREA)
        mask = image_mask(sizes_ref, pl.program_id(0) * per_step + part)
        masked = (pixels_ref[:, spot].astype(f32) * mask).astype(bf16)
        cells, low, wide = cells_ref.at[part], low_ref.at[part], wide_ref.at[part]
        cells[...] = dot(turn_ref[...], masked, NT)
        for start in range(0, width, LANES):
            lanes = slice(start, start + LANES)
            for place, value in enumerate(causal(cells, taps_ref, 0, lanes)):
                low[block_rows(place), lanes] = value.astype(bf16)
        wide[...] = dot(turn_ref[AREA:, :], low[...])
        first_ref[spot, :] = wide[...].astype(bf16)
        for start in range(0, width, LANES):
            lanes = slice(start, start + LANES)
            skip = channel_ref[2:3, lanes]
            for place, value in enumerate(causal(wide, taps_ref, 1, lanes)):
                own = cells[AREA + place * S : AREA + (place + 1) * S, lanes]
                low[block_rows(place), lanes] = (value + skip * own).astype(bf16)
        mixed_ref[:, spot] = dot(low[...], turn_ref[AREA:, :], TN).astype(bf16)


def mixer_forward(sizes, pixels, taps, channel, turn):
    width, count = pixels.shape
    per_step = 2
    span = per_step * AREA
    grid_spec = pltpu.PrefetchScalarGridSpec(
        num_scalar_prefetch=1,
        grid=(count // span,),
        in_specs=[
            pl.BlockSpec((width, span), lambda i, *_: (0, i)),
            pl.BlockSpec(taps.shape, lambda i, *_: (0, 0, 0)),
            pl.BlockSpec(channel.shape, lambda i, *_: (0, 0)),
            pl.BlockSpec(turn.shape, lambda i, *_: (0, 0)),
        ],
        out_specs=[
            pl.BlockSpec((width, span), lambda i, *_: (0, i)),
            pl.BlockSpec((span, width), lambda i, *_: (i, 0)),
        ],
        scratch_shapes=[
            pltpu.VMEM((per_step, 2 * AREA, width), f32),
            pltpu.VMEM((per_step, AREA, width), bf16),
            pltpu.VMEM((per_step, AREA, width), f32),
        ],
    )
    return pl.pallas_call(
        functools.partial(mixer_kernel, per_step=per_step),
        grid_spec=grid_spec,
        out_shape=[
            jax.ShapeDtypeStruct((width, count), bf16),
            jax.ShapeDtypeStruct((count, width), bf16),
        ],
        compiler_params=params(),
        cost_estimate=cost(8e9, 9e6),
        name="mixer_forward",
    )(sizes, pixels, taps, channel, turn)


def norm_kernel(
    place_ref, sizes_ref, own_ref, other_ref, own_grad_ref, other_grad_ref, own_cols_ref, other_cols_ref, act_ref, low_ref, stat_ref, *, per_step
):
    width = 2.0 * own_ref.shape[0]
    mine = place_ref[0]
    for part in range(per_step):
        spot = slice(part * AREA, (part + 1) * AREA)
        mask = image_mask(sizes_ref, pl.program_id(0) * per_step + part)
        own, other = own_ref[:, spot].astype(f32), other_ref[:, spot].astype(f32)
        mean = (jnp.sum(own, axis=0, keepdims=True) + jnp.sum(other, axis=0, keepdims=True)) / width
        own, other = own - mean, other - mean
        spread = (
            jnp.sum(own * own, axis=0, keepdims=True) + jnp.sum(other * other, axis=0, keepdims=True)
        ) / width
        scale = lax.rsqrt(spread + EPSILON_NORM)
        stat_ref[0:1, spot] = mean
        stat_ref[1:2, spot] = scale
        for which, value, grad_ref, cols_ref in (
            (mine, own, own_grad_ref, own_cols_ref),
            (1 - mine, other, other_grad_ref, other_cols_ref),
        ):
            act_ref[which, :, spot] = (
                value * scale * cols_ref[:, 0:1] + cols_ref[:, 1:2]
            ).astype(bf16)
            grad = grad_ref[:, spot].astype(f32)
            low_ref[which, :, spot] = (grad * (mask * cols_ref[:, 3:4])).astype(bf16)


def norm_forward(place, sizes, own, other, own_grad, other_grad, own_cols, other_cols):
    width, count = own.shape
    per_step = 2
    span = per_step * AREA
    block = pl.BlockSpec((width, span), lambda i, *_: (0, i))
    cols = pl.BlockSpec(own_cols.shape, lambda i, *_: (0, 0))
    pair = pl.BlockSpec((2, width, span), lambda i, *_: (0, 0, i))
    grid_spec = pltpu.PrefetchScalarGridSpec(
        num_scalar_prefetch=2,
        grid=(count // span,),
        in_specs=[block, block, block, block, cols, cols],
        out_specs=[pair, pair, pl.BlockSpec((8, span), lambda i, *_: (0, i))],
    )
    return pl.pallas_call(
        functools.partial(norm_kernel, per_step=per_step),
        grid_spec=grid_spec,
        out_shape=[
            jax.ShapeDtypeStruct((2, width, count), bf16),
            jax.ShapeDtypeStruct((2, width, count), bf16),
            jax.ShapeDtypeStruct((8, count), f32),
        ],
        compiler_params=params(),
        cost_estimate=cost(1e9, 26e6),
        name="norm_forward",
    )(place, sizes, own, other, own_grad, other_grad, own_cols, other_cols)


def weights_kernel(up_ref, down_ref, up_low_ref, up_turned_ref, down_low_ref, down_turned_ref, square_ref):
    @pl.when(pl.program_id(0) == 0)
    def _():
        square_ref[...] = jnp.zeros_like(square_ref)

    for row, source_ref, low_ref, turned_ref in (
        (0, up_ref, up_low_ref, up_turned_ref),
        (1, down_ref, down_low_ref, down_turned_ref),
    ):
        value = source_ref[...]
        units = square_ref.shape[1]
        for start in range(0, value.shape[1], units):
            part = value[:, start : start + units]
            square_ref[row : row + 1, :] += jnp.sum(part * part, axis=0, keepdims=True)
        low_ref[...] = value.astype(bf16)
        turned_ref[...] = value.T.astype(bf16)


def weights_low(up, down):
    full, hidden_local = up.shape
    units = 384
    column = lambda i: (0, i)
    row = lambda i: (i, 0)
    return pl.pallas_call(
        weights_kernel,
        grid=(hidden_local // units,),
        in_specs=[pl.BlockSpec((full, units), column), pl.BlockSpec((full // 2, full), row)],
        out_specs=[
            pl.BlockSpec((full, units), column),
            pl.BlockSpec((units, full), row),
            pl.BlockSpec((units, full), row),
            pl.BlockSpec((full, units), column),
            pl.BlockSpec((8, units), lambda i: (0, 0)),
        ],
        out_shape=[
            jax.ShapeDtypeStruct((full, hidden_local), bf16),
            jax.ShapeDtypeStruct((hidden_local, full), bf16),
            jax.ShapeDtypeStruct((hidden_local, full), bf16),
            jax.ShapeDtypeStruct((full, hidden_local), bf16),
            jax.ShapeDtypeStruct((8, units), f32),
        ],
        compiler_params=params(),
        cost_estimate=cost(1e7, 19e6),
        name="weights_low",
    )(up, down)


def gelu_pair(pre):
    bell = jnp.exp(-0.5 * pre * pre)
    base = 1.0 + (ERF_P * HALF_ROOT) * jnp.abs(pre)
    guess = pl.reciprocal(base, approx=True)
    part = guess * (2.0 - base * guess)
    poly = 0.5 * ERF_A[4]
    for factor in ERF_A[3::-1]:
        poly = poly * part + 0.5 * factor
    tail = poly * part * bell
    upper = jnp.where(pre >= 0.0, 1.0 - tail, tail)
    return pre * upper, upper + pre * bell * DENSITY


def split_out(source_ref, digit, part_refs):
    rows = part_refs[0].shape[0]
    for away, ref in enumerate(part_refs):
        start = pl.multiple_of((digit ^ away) * rows, rows)
        ref[...] = source_ref[pl.ds(start, rows), :].astype(ref.dtype)


def chunk_kernel(place_ref, act_ref, low_ref, up_ref, down_ref, bias_ref, *refs):
    hidden_ref, slope_ref, bias_grad_ref = refs[-5 - PLANE : -2 - PLANE]
    part_refs, (grad_acc, bias_acc) = refs[-2 - PLANE : -2], refs[-2:]
    step = pl.program_id(0)

    @pl.when(step == 0)
    def _():
        grad_acc[...] = jnp.zeros_like(grad_acc)
        bias_acc[...] = jnp.zeros_like(bias_acc)

    halves, width, span = act_ref.shape
    units = up_ref.shape[0]
    act = act_ref[...].reshape(halves * width, span)
    low = low_ref[...].reshape(halves * width, span)
    tile = 256
    tiles = [(row, start) for start in range(0, span, tile) for row in range(0, units, tile)]

    def products(row, start):
        rows, spot = slice(row, row + tile), slice(start, start + tile)
        return dot(up_ref[rows, :], act[:, spot]) + bias_ref[rows, :], dot(down_ref[rows, :], low[:, spot])

    ready = products(*tiles[0])
    for at, (row, start) in enumerate(tiles):
        pre, back = ready
        if at + 1 < len(tiles):
            ready = products(*tiles[at + 1])
        rows, spot = slice(row, row + tile), slice(start, start + tile)
        hidden, slope = gelu_pair(pre)
        hidden_ref[rows, spot] = hidden.astype(bf16)
        slope_ref[rows, spot] = (back * slope).astype(bf16)
    slopes = slope_ref[...]
    grad_acc[:units, :] += dot(slopes, act, NT)
    grad_acc[units:, :] += dot(hidden_ref[...], low, NT)
    bias_acc[...] += dot(jnp.ones((S, span), bf16), slopes, NT)

    @pl.when(step == pl.num_programs(0) - 1)
    def _():
        split_out(grad_acc, place_ref[1], part_refs)
        bias_grad_ref[...] = bias_acc[0:8, :]


def feed_chunk(chunk, place, act, low, up_turned, down, bias, earlier):
    halves, width, count = act.shape
    full = halves * width
    hidden_local = down.shape[0]
    units = hidden_local // CHUNKS
    span = 512
    pair = pl.BlockSpec((halves, width, span), lambda i, *_: (0, 0, i))
    weight = pl.BlockSpec((units, full), lambda i, *_: (chunk, 0))
    wide = pl.BlockSpec((units, span), lambda i, *_: (chunk, i))
    whole = lambda i, *_: (0, 0)
    rows = 2 * units // PLANE
    grid_spec = pltpu.PrefetchScalarGridSpec(
        num_scalar_prefetch=1,
        grid=(count // span,),
        in_specs=[pair, pair, weight, weight, pl.BlockSpec((units, 1), lambda i, *_: (chunk, 0))]
        + [pl.BlockSpec(memory_space=pl.ANY)] * len(earlier),
        out_specs=[wide, wide, pl.BlockSpec((8, units), whole)] + [pl.BlockSpec((rows, full), whole)] * PLANE,
        scratch_shapes=[pltpu.VMEM((2 * units, full), f32), pltpu.VMEM((S, units), f32)],
    )
    return pl.pallas_call(
        chunk_kernel,
        grid_spec=grid_spec,
        out_shape=[
            jax.ShapeDtypeStruct((hidden_local, count), bf16),
            jax.ShapeDtypeStruct((hidden_local, count), bf16),
            jax.ShapeDtypeStruct((8, units), f32),
            jax.ShapeDtypeStruct((rows, full), f32),
        ]
        + [jax.ShapeDtypeStruct((rows, full), bf16)] * (PLANE - 1),
        input_output_aliases={6: 0, 7: 1} if earlier else {},
        compiler_params=params(),
        cost_estimate=cost(8 * count * full * units, 4 * count * (full + units)),
        name="feed_chunk_%d" % chunk,
    )(place, act, low, up_turned, down, bias, *earlier)


def across(value, stride):
    size = lax.axis_size("line") * PLANE
    return lax.ppermute(value, ("line", "plane"), [(i, i ^ stride) for i in range(size)])


def small_sum(value):
    for base in (1, PLANE):
        near = value + across(value, base)
        far = across(value, 2 * base) + across(value, 3 * base)
        value = near + far
    stride = PLANE * 4
    while stride < lax.axis_size("line") * PLANE:
        value = value + across(value, stride)
        stride *= 2
    return value


def along(value, axis, away):
    return lax.ppermute(value, axis, [(i, i ^ away) for i in range(lax.axis_size(axis))])


class GradientSum:
    def __init__(self, kept, sends):
        self.kept = kept
        self.got = [along(value, "plane", away) for away, value in enumerate(sends, 1)]

    def add(self):
        total = self.kept
        for value in self.got:
            total = total + value.astype(f32)
        return total

    def to_line(self):
        size = lax.axis_size("line")
        total = self.add()
        parts = total.reshape(size, -1, total.shape[1])

        def part(away):
            return lax.dynamic_index_in_dim(parts, lax.axis_index("line") ^ away, 0, keepdims=False)

        self.kept = part(0)
        self.sends = [part(away).astype(bf16) for away in range(1, size)]
        self.got = [along(value, "line", away) for away, value in enumerate(self.sends, 1)]

    def gather_line(self):
        self.piece = self.add().astype(bf16)
        self.quarter = lax.all_gather(self.piece, "line", axis=0, tiled=True)

    def gather(self):
        self.sum = lax.all_gather(self.add().astype(bf16), ("plane", "line"), axis=0, tiled=True)

    def gather_plane(self):
        self.sum = lax.all_gather(self.quarter, "plane", axis=0, tiled=True)


def sums_kernel(place_ref, hidden_ref, slope_ref, down_ref, up_ref, own_ref, other_ref, stat_ref, own_cols_ref, other_cols_ref, *refs, skipped):
    own_proj_ref, other_proj_ref, own_act_ref, other_act_ref, sum_ref = refs[skipped : skipped + 5]
    total_ref = refs[-1]
    width = own_ref.shape[0]
    mine = place_ref[0]
    own_rows = pl.ds(pl.multiple_of(mine * width, width), width)
    other_rows = pl.ds(pl.multiple_of((1 - mine) * width, width), width)
    total_ref[0] = dot(down_ref[...], hidden_ref[...])
    total_ref[1] = dot(up_ref[...], slope_ref[...])
    own_proj_ref[...] = total_ref[0, own_rows, :]
    other_proj_ref[...] = total_ref[0, other_rows, :].astype(bf16)
    mean, scale = stat_ref[0:1, :], stat_ref[1:2, :]
    sums = []
    for rows, out_ref, value_ref, cols_ref in (
        (own_rows, own_act_ref, own_ref, own_cols_ref),
        (other_rows, other_act_ref, other_ref, other_cols_ref),
    ):
        act = total_ref[1, rows, :]
        out_ref[...] = act.astype(out_ref.dtype)
        act = act * cols_ref[:, 0:1]
        normed = (value_ref[...].astype(f32) - mean) * scale
        sums.append(jnp.sum(act, axis=0, keepdims=True))
        sums.append(jnp.sum(act * normed, axis=0, keepdims=True))
    sum_ref[0:1, :] = sums[0] + sums[2]
    sum_ref[1:2, :] = sums[1] + sums[3]


def hidden_sums(place, hidden, slopes, down_turned, up, own, other, stat, own_cols, other_cols, part, tokens, riders):
    width, total = own.shape
    count = total // SUM_PARTS
    hidden_local = hidden.shape[0]
    span = 512
    base = part * (count // span)
    column = lambda i, *_: (0, base + i)
    out = lambda i, *_: (0, i)
    fixed = lambda i, *_: (0, 0)
    wide = pl.BlockSpec((hidden_local, span), column)
    block = pl.BlockSpec((width, span), column)
    result = pl.BlockSpec((width, span), out)
    cols = pl.BlockSpec(own_cols.shape, fixed)
    grid_spec = pltpu.PrefetchScalarGridSpec(
        num_scalar_prefetch=1,
        grid=(count // span,),
        in_specs=[
            wide,
            wide,
            pl.BlockSpec(down_turned.shape, fixed),
            pl.BlockSpec(up.shape, fixed),
            block,
            block,
            pl.BlockSpec((8, span), column),
            cols,
            cols,
        ]
        + [pl.BlockSpec(memory_space=pl.ANY)] * (len(riders) + len(tokens)),
        out_specs=[result, result, result, result, pl.BlockSpec((8, span), out)]
        + [pl.BlockSpec(memory_space=pl.ANY)] * len(riders),
        scratch_shapes=[pltpu.VMEM((2, 2 * width, span), f32)],
    )
    values = pl.pallas_call(
        functools.partial(sums_kernel, skipped=len(riders) + len(tokens)),
        grid_spec=grid_spec,
        out_shape=[
            jax.ShapeDtypeStruct((width, count), f32),
            jax.ShapeDtypeStruct((width, count), bf16),
            jax.ShapeDtypeStruct((width, count), f32),
            jax.ShapeDtypeStruct((width, count), bf16),
            jax.ShapeDtypeStruct((8, count), f32),
        ]
        + [jax.ShapeDtypeStruct(rider.shape, rider.dtype) for rider in riders],
        input_output_aliases={10 + at: 5 + at for at in range(len(riders))},
        compiler_params=params(),
        cost_estimate=cost(8 * count * width * hidden_local, 4 * count * (hidden_local + 3 * width)),
        name="hidden_sums_%d" % part,
    )(place, hidden, slopes, down_turned, up, own, other, stat, own_cols, other_cols, *riders, *tokens)
    return values[:5], values[5:]


TAPS, ROWS, BIAS = 0, 32, 40


def correlate(left_ref, right_ref, sum_ref, half, lanes):
    left = [left_ref[block_rows(place), lanes] for place in range(S)]
    right = [right_ref[block_rows(place), lanes].astype(f32) for place in range(S)]
    for back in range(S):
        total = left[back] * right[0]
        for place in range(back + 1, S):
            total += left[place] * right[place - back]
        sum_ref[half, block_rows(back), lanes] += total


def backward_kernel(
    sizes_ref,
    pixels_ref,
    grad_ref,
    mixed_ref,
    first_ref,
    stat_ref,
    own_proj_ref,
    got_proj_ref,
    own_act_ref,
    got_act_ref,
    own_sum_ref,
    got_sum_ref,
    cols_ref,
    taps_ref,
    turn_ref,
    carry_ref,
    *refs,
    base,
    skipped,
):
    out_ref, pixel_grad_ref, small_ref = refs[skipped : skipped + 3]
    sum_ref, channel_sum, cells_ref, low_ref, wide_ref, back_ref = refs[-6:]
    step = pl.program_id(0)
    width = pixels_ref.shape[0]
    full = 2.0 * width

    @pl.when(step == 0)
    def _():
        sum_ref[...] = jnp.zeros_like(sum_ref)
        channel_sum[...] = jnp.zeros_like(channel_sum)

    mask = image_mask(sizes_ref, base + step)
    pixels = pixels_ref[...].astype(f32)
    grad = grad_ref[...].astype(f32)
    masked = pixels * mask
    gain, skip, layer, shift = cols_ref[:, 0:1], cols_ref[:, 2:3], cols_ref[:, 3:4], cols_ref[:, 4:5]

    def gather(row, value):
        channel_sum[row] += value[:, :LANES] + value[:, LANES:]

    masked_grad = grad * mask
    branch = own_proj_ref[...] + got_proj_ref[...].astype(f32) + shift
    out_ref[...] = pixels + mask * layer * branch
    gather(3, masked_grad * branch)
    gather(4, masked_grad)

    scale = stat_ref[1:2, :]
    normed = (mixed_ref[...].astype(f32) - stat_ref[0:1, :]) * scale
    act = own_act_ref[...] + got_act_ref[...].astype(f32)
    gather(0, act * normed)
    gather(1, act)
    plain = (own_sum_ref[0:1, :] + got_sum_ref[0:1, :]) / full
    tilt = (own_sum_ref[1:2, :] + got_sum_ref[1:2, :]) / full
    mixed_low = (scale * (act * gain - plain - normed * tilt)).astype(bf16)
    mixed_grad = mixed_low.astype(f32)
    gather(2, mixed_grad * masked)

    cells_ref[...] = dot(turn_ref[:AREA, :], masked.astype(bf16), NT)
    wide_ref[...] = dot(turn_ref[AREA:, :], mixed_low, NT)
    for start in range(0, width, LANES):
        lanes = slice(start, start + LANES)
        for place, value in enumerate(anticausal(wide_ref, taps_ref, 1, lanes)):
            low_ref[block_rows(place), lanes] = value.astype(bf16)
        correlate(wide_ref, first_ref, sum_ref, 1, lanes)
    back_ref[...] = dot(turn_ref[AREA:, :], low_ref[...])
    for start in range(0, width, LANES):
        lanes = slice(start, start + LANES)
        for place, value in enumerate(anticausal(back_ref, taps_ref, 0, lanes)):
            wide_ref[block_rows(place), lanes] = value
        correlate(back_ref, cells_ref, sum_ref, 0, lanes)
    pixel_grad_ref[...] = grad + mask * (wide_ref[...].T + skip * mixed_grad)

    @pl.when(step == pl.num_programs(0) - 1)
    def _():
        small_ref[...] = carry_ref[...]
        for half in range(2):
            for back in range(S):
                row = TAPS + half * S + back
                small_ref[row : row + 1, :] += jnp.sum(
                    sum_ref[half, block_rows(back), :], axis=0, keepdims=True
                )
        for row in range(5):
            small_ref[ROWS + row : ROWS + row + 1, :] += jnp.sum(channel_sum[row].T, axis=0, keepdims=True)


def backward(sizes, pixels, grad, mixed, first, stat, own, got, cols, taps, turn, carry, part, earlier, riders, tokens):
    own_proj, own_act, own_sum = own
    got_proj, got_act, got_sum = got
    width, total = pixels.shape
    count = total // BACK_PARTS
    base = part * (count // AREA)
    inner = base % (own_proj.shape[1] // AREA)
    column = lambda i, *_: (0, base + i)
    here = lambda i, *_: (0, inner + i)
    fixed = lambda i, *_: (0, 0)
    block = pl.BlockSpec((width, AREA), column)
    local = pl.BlockSpec((width, AREA), here)
    anywhere = pl.BlockSpec(memory_space=pl.ANY)
    grid_spec = pltpu.PrefetchScalarGridSpec(
        num_scalar_prefetch=1,
        grid=(count // AREA,),
        in_specs=[
            block,
            block,
            block,
            pl.BlockSpec((AREA, width), lambda i, *_: (base + i, 0)),
            pl.BlockSpec((8, AREA), column),
            local,
            local,
            local,
            local,
            pl.BlockSpec((8, AREA), here),
            pl.BlockSpec((8, AREA), here),
            pl.BlockSpec(cols.shape, fixed),
            pl.BlockSpec(taps.shape, lambda i, *_: (0, 0, 0)),
            pl.BlockSpec(turn.shape, fixed),
            pl.BlockSpec(carry.shape, fixed),
        ]
        + [anywhere] * (len(earlier) + len(riders) + len(tokens)),
        out_specs=[block, block, pl.BlockSpec(carry.shape, fixed)] + [anywhere] * len(riders),
        scratch_shapes=[
            pltpu.VMEM((2, AREA, width), f32),
            pltpu.VMEM((5, width, LANES), f32),
            pltpu.VMEM((AREA, width), f32),
            pltpu.VMEM((AREA, width), bf16),
            pltpu.VMEM((AREA, width), f32),
            pltpu.VMEM((AREA, width), f32),
        ],
    )
    return pl.pallas_call(
        functools.partial(backward_kernel, base=base, skipped=len(earlier) + len(riders) + len(tokens)),
        grid_spec=grid_spec,
        out_shape=[
            jax.ShapeDtypeStruct((width, total), f32),
            jax.ShapeDtypeStruct((width, total), f32),
            jax.ShapeDtypeStruct(carry.shape, f32),
        ]
        + [jax.ShapeDtypeStruct(rider.shape, rider.dtype) for rider in riders],
        input_output_aliases={16 + at: at for at in range(len(earlier))}
        | {16 + len(earlier) + at: 3 + at for at in range(len(riders))},
        compiler_params=params(),
        cost_estimate=cost(10e9 / BACK_PARTS, 44e6 / BACK_PARTS),
        name="backward_%d" % part,
    )(
        sizes, pixels, grad, mixed, first, stat, own_proj, got_proj, own_act, got_act, own_sum, got_sum, cols, taps, turn, carry, *earlier, *riders, *tokens
    )


UP_ROW, UP_MASS, DOWN_COL, DOWN_MASS, MIXER_COL, MIXER_MASS, SCALARS = range(7)


def fold(value):
    total = value[:, :LANES]
    for start in range(LANES, value.shape[1], LANES):
        total += value[:, start : start + LANES]
    return total


def as_row(ref):
    return ref[...].reshape(1, ref.shape[0])


def to_flat(ref, value):
    ref[...] = value.reshape(ref.shape[0])


def to_column(row):
    return jnp.broadcast_to(row, (LANES, row.shape[1])).T


def to_row(columns):
    return jnp.sum(columns.T, axis=0, keepdims=True)


def statistics_kernel(sum_ref, sum_down_ref, up_old_ref, down_old_ref, carry_ref, *refs):
    up_ref, down_ref, up_new_ref, down_new_ref, stat_ref = refs[-5:]
    step = pl.program_id(0)

    @pl.when(step == 0)
    def _():
        stat_ref[...] = carry_ref[...]

    for source_ref, old_ref, new_ref, columns, mass in (
        (sum_ref, up_old_ref, up_new_ref, UP_ROW, UP_MASS),
        (sum_down_ref, down_old_ref, down_new_ref, DOWN_COL, DOWN_MASS),
    ):
        value = source_ref[...].astype(f32)
        if source_ref is sum_ref:
            up_ref[...] = value.T
        else:
            down_ref[...] = value
        square = value * value
        mean = jnp.sum(fold(square), axis=1, keepdims=True) / value.shape[1]
        fresh = DECAY * to_column(old_ref[...]) + FRESH * (mean + EPSILON_SQUARE)
        new_ref[...] = fresh.T[0:1, :]
        stat_ref[columns : columns + 1, : value.shape[1]] += jnp.sum(square, axis=0, keepdims=True)
        stat_ref[mass : mass + 1, : value.shape[1]] += jnp.sum(
            square * (1.0 / fresh[:, 0:1]), axis=0, keepdims=True
        )


def statistics(chunk, total, up_cols, down_rows, carry, earlier):
    units, full = total.shape[0] // 2, total.shape[1]
    hidden_local = up_cols.shape[1]
    rows = 256
    steps = units // rows
    base = chunk * steps
    row = pl.BlockSpec((1, rows), lambda i: (0, base + i))
    fixed = pl.BlockSpec(carry.shape, lambda i: (0, 0))
    return pl.pallas_call(
        statistics_kernel,
        grid=(steps,),
        in_specs=[
            pl.BlockSpec((rows, full), lambda i: (i, 0)),
            pl.BlockSpec((rows, full), lambda i: (steps + i, 0)),
            row,
            row,
            fixed,
        ]
        + [pl.BlockSpec(memory_space=pl.ANY)] * len(earlier),
        out_specs=[
            pl.BlockSpec((full, rows), lambda i: (0, base + i)),
            pl.BlockSpec((rows, full), lambda i: (base + i, 0)),
            row,
            row,
            fixed,
        ],
        out_shape=[
            jax.ShapeDtypeStruct((full, hidden_local), f32),
            jax.ShapeDtypeStruct((hidden_local, full), f32),
            jax.ShapeDtypeStruct((1, hidden_local), f32),
            jax.ShapeDtypeStruct((1, hidden_local), f32),
            jax.ShapeDtypeStruct(carry.shape, f32),
        ],
        input_output_aliases={5 + at: at for at in range(len(earlier))},
        compiler_params=params(),
        cost_estimate=cost(1e8 / CHUNKS, 14e6 / CHUNKS),
        name="statistics_%d" % chunk,
    )(total, total, up_cols, down_rows, carry, *earlier)


def small_kernel(
    sum_ref,
    stat_ref,
    square_ref,
    params_ref,
    channel_ref,
    moment_ref,
    bias_ref,
    bias_moment_ref,
    rows_ref,
    down_rows_new_ref,
    mixer_grad_ref,
    rows_new_ref,
    channel_grad_ref,
    moment_new_ref,
    channel_update_ref,
    bias_grad_ref,
    bias_moment_new_ref,
    bias_update_ref,
    out_ref,
    channel_square_ref,
    table_ref,
):
    out_ref[...] = stat_ref[...]
    taps_back(params_ref, sum_ref, table_ref)
    grad = table_ref[...].T
    mixer_grad_ref[...] = grad
    states = grad.shape[1]
    square = grad * grad
    mean = jnp.sum(fold(square), axis=1, keepdims=True) / states
    fresh = DECAY * to_column(as_row(rows_ref)) + FRESH * (mean + EPSILON_SQUARE)
    rows_new = fresh.T[0:1, :]
    rows_new_ref[...] = rows_new
    out_ref[MIXER_COL : MIXER_COL + 1, :states] = jnp.sum(square, axis=0, keepdims=True)
    out_ref[MIXER_MASS : MIXER_MASS + 1, :states] = jnp.sum(square * (1.0 / fresh[:, 0:1]), axis=0, keepdims=True)

    layer = channel_ref[3:4, :]
    channel_grad_ref[0:4, :] = sum_ref[ROWS : ROWS + 4, :]
    channel_grad_ref[4:5, :] = sum_ref[ROWS + 4 : ROWS + 5, :] * layer
    grad = channel_grad_ref[...]
    moment = DECAY * moment_ref[...] + FRESH * (grad * grad + EPSILON_SQUARE)
    moment_new_ref[...] = moment
    channel_update = grad * lax.rsqrt(moment)
    channel_update_ref[...] = channel_update

    width = layer.shape[1]
    for at in range(bias_grad_ref.shape[1] // width):
        bias_grad_ref[:, at * width : (at + 1) * width] = sum_ref[BIAS + at : BIAS + at + 1, :]
    grad = bias_grad_ref[...]
    moment = DECAY * as_row(bias_moment_ref) + FRESH * (grad * grad + EPSILON_SQUARE)
    bias_moment_new_ref[...] = moment
    bias_update = grad * lax.rsqrt(moment)
    bias_update_ref[...] = bias_update

    def total(value):
        return jnp.sum(value, keepdims=True)

    channel = channel_ref[...]
    table = params_ref[...]
    bias = as_row(bias_ref)
    scalars = (
        total(channel_update * channel_update) + total(bias_update * bias_update),
        total(down_rows_new_ref[...]),
        total(rows_new),
        total(square_ref[0:1, :]),
        total(square_ref[1:2, :]),
        total(table * table),
        total(bias * bias),
    )
    for at, value in enumerate(scalars):
        out_ref[SCALARS : SCALARS + 1, at * LANES : (at + 1) * LANES] = jnp.broadcast_to(value, (1, LANES))
    channel_square_ref[...] = jnp.broadcast_to(jnp.sum(channel * channel, axis=1, keepdims=True), (5, LANES))


def small_update(total, stat, square, mixer_params, channel_params, channel_moment, bias, bias_moment, rows, down_rows_new):
    width, states = mixer_params.shape
    shapes = [
        (width, states),
        (1, width),
        channel_params.shape,
        channel_params.shape,
        channel_params.shape,
        (1, bias.shape[0]),
        (1, bias.shape[0]),
        (1, bias.shape[0]),
        (8, 8 * LANES),
        (5, LANES),
    ]
    return pl.pallas_call(
        small_kernel,
        out_shape=[jax.ShapeDtypeStruct(shape, f32) for shape in shapes],
        scratch_shapes=[pltpu.VMEM((states, width), f32)],
        compiler_params=params(),
        cost_estimate=cost(1e7, 2e6),
        name="small_update",
    )(total, stat, square, mixer_params, channel_params, channel_moment, bias, bias_moment, rows, down_rows_new)


def update_kernel(
    stat_ref,
    got_ref,
    channel_square_ref,
    channel_got_ref,
    up_rows_ref,
    down_cols_ref,
    mixer_cols_ref,
    up_cols_new_ref,
    down_rows_new_ref,
    up_grad_ref,
    up_ref,
    up_average_ref,
    down_grad_ref,
    down_ref,
    down_average_ref,
    mixer_grad_ref,
    mixer_ref,
    mixer_average_ref,
    mixer_rows_new_ref,
    channel_ref,
    channel_average_ref,
    channel_update_ref,
    bias_ref,
    bias_average_ref,
    bias_update_ref,
    bias_grad_ref,
    bias_moment_ref,
    up_cols_all_ref,
    down_rows_all_ref,
    rms_ref,
    up_rows_new_ref,
    down_cols_new_ref,
    mixer_cols_new_ref,
    up_new_ref,
    up_average_new_ref,
    down_new_ref,
    down_average_new_ref,
    mixer_new_ref,
    mixer_average_new_ref,
    channel_new_ref,
    channel_average_new_ref,
    bias_new_ref,
    bias_average_new_ref,
    bias_grad_out_ref,
    bias_moment_out_ref,
    up_cols_out_ref,
    down_rows_out_ref,
    mixer_rows_out_ref,
):
    full, hidden = up_rows_ref.shape[0], 2 * bias_ref.shape[0]
    states = mixer_cols_ref.shape[0]

    def stat(row, size):
        return stat_ref[row : row + 1, :size] + got_ref[row : row + 1, :size]

    def scalar(at):
        return stat(SCALARS, 8 * LANES)[:, at * LANES : at * LANES + 1]

    def total(value):
        return jnp.sum(value, axis=1, keepdims=True)

    up_rows_new = DECAY * as_row(up_rows_ref) + FRESH * (stat(UP_ROW, full) / hidden + EPSILON_SQUARE)
    down_cols_new = DECAY * as_row(down_cols_ref) + FRESH * (stat(DOWN_COL, full) / hidden + EPSILON_SQUARE)
    mixer_cols_new = DECAY * as_row(mixer_cols_ref) + FRESH * (stat(MIXER_COL, states) / full + EPSILON_SQUARE)
    up_mean = total(up_rows_new) / full
    down_mean = scalar(1) / hidden
    mixer_mean = scalar(2) / full
    square = (
        scalar(0)
        + up_mean * total(stat(UP_MASS, full) / up_rows_new)
        + down_mean * total(stat(DOWN_MASS, full) / down_cols_new)
        + mixer_mean * total(stat(MIXER_MASS, states) / mixer_cols_new)
    )
    rms = jnp.sqrt(square / (2 * full * hidden + states * full + 5 * full + hidden))
    factor = LEARN_RATE * CLIP_LEVEL / jnp.maximum(CLIP_LEVEL, rms)

    def rate(squares, size):
        return factor * jnp.maximum(EPSILON_SCALE, jnp.sqrt(squares / size))

    def settle(weight, change, average_ref, new_ref, average_new_ref):
        new = weight - change
        new_ref[...] = new
        average_new_ref[...] = AVERAGE_KEEP * average_ref[...] + (1.0 - AVERAGE_KEEP) * new

    def column(row):
        return to_column(row)[:, 0:1]

    up_speed = rate(scalar(3), full * hidden) * jnp.sqrt(up_mean)
    settle(
        up_ref[...],
        up_grad_ref[...] * column(lax.rsqrt(up_rows_new) * up_speed) * lax.rsqrt(up_cols_new_ref[...]),
        up_average_ref,
        up_new_ref,
        up_average_new_ref,
    )
    down_speed = rate(scalar(4), full * hidden) * jnp.sqrt(down_mean)
    settle(
        down_ref[...],
        down_grad_ref[...] * column(lax.rsqrt(down_rows_new_ref[...]) * down_speed) * lax.rsqrt(down_cols_new),
        down_average_ref,
        down_new_ref,
        down_average_new_ref,
    )

    @pl.when(pl.program_id(0) == 0)
    def _():
        rms_ref[...] = rms
        to_flat(up_rows_new_ref, up_rows_new)
        to_flat(down_cols_new_ref, down_cols_new)
        to_flat(mixer_cols_new_ref, mixer_cols_new)
        to_flat(bias_grad_out_ref, bias_grad_ref[...])
        to_flat(bias_moment_out_ref, bias_moment_ref[...])
        to_flat(up_cols_out_ref, up_cols_all_ref[...])
        to_flat(down_rows_out_ref, down_rows_all_ref[...])
        to_flat(mixer_rows_out_ref, mixer_rows_new_ref[...])
        mixer_speed = rate(scalar(5), states * full) * jnp.sqrt(mixer_mean)
        settle(
            mixer_ref[...],
            mixer_grad_ref[...]
            * column(lax.rsqrt(mixer_rows_new_ref[...]) * mixer_speed)
            * lax.rsqrt(mixer_cols_new),
            mixer_average_ref,
            mixer_new_ref,
            mixer_average_new_ref,
        )
        channel_square = channel_square_ref[:, 0:1] + channel_got_ref[:, 0:1]
        settle(
            channel_ref[...],
            rate(channel_square, full) * channel_update_ref[...],
            channel_average_ref,
            channel_new_ref,
            channel_average_new_ref,
        )
        bias_new = as_row(bias_ref) - rate(scalar(6), hidden) * bias_update_ref[...]
        to_flat(bias_new_ref, bias_new)
        to_flat(
            bias_average_new_ref, AVERAGE_KEEP * as_row(bias_average_ref) + (1.0 - AVERAGE_KEEP) * bias_new
        )


def final_update(operands, units):
    up, mixer, channel, bias = operands[10], operands[16], operands[19], operands[22]
    full, hidden_local = up.shape
    up_block = pl.BlockSpec((full, units), lambda i: (0, i))
    down_block = pl.BlockSpec((units, full), lambda i: (i, 0))
    row_block = pl.BlockSpec((1, units), lambda i: (0, i))

    def whole(array):
        return pl.BlockSpec(array.shape, lambda i: (0,) * len(array.shape))

    in_specs = [whole(array) for array in operands]
    in_specs[7:9] = [row_block, row_block]
    in_specs[9:12] = [up_block] * 3
    in_specs[12:15] = [down_block] * 3
    shapes = [(1, 1), operands[4].shape, operands[5].shape, operands[6].shape]
    shapes += [up.shape] * 2 + [(hidden_local, full)] * 2 + [mixer.shape] * 2 + [channel.shape] * 2 + [bias.shape] * 2
    shapes += [bias.shape] * 4 + [operands[18].shape[1:]]
    out_specs = [whole(jax.ShapeDtypeStruct(shape, f32)) for shape in shapes]
    out_specs[4:8] = [up_block, up_block, down_block, down_block]
    return pl.pallas_call(
        update_kernel,
        grid=(hidden_local // units,),
        in_specs=in_specs,
        out_specs=out_specs,
        out_shape=[jax.ShapeDtypeStruct(shape, f32) for shape in shapes],
        compiler_params=params(),
        cost_estimate=cost(1e8, 48e6),
        name="final_update",
    )(*operands)


def turn_table():
    place = np.arange(AREA)
    swapped = (place % S) * S + place // S
    table = np.concatenate([place[:, None] == place[None, :], swapped[:, None] == place[None, :]])
    return table.astype(ml_dtypes.bfloat16)


def shards(
    pixels,
    image_sizes,
    out_grad,
    up_weight,
    down_weight,
    mixer_params,
    channel_params,
    hidden_bias,
    up_rows,
    up_cols,
    down_rows,
    down_cols,
    mixer_rows,
    mixer_cols,
    channel_moment,
    bias_moment,
    up_average,
    down_average,
    mixer_average,
    channel_average,
    bias_average,
):
    width_local, count = pixels.shape
    hidden_local = up_weight.shape[1]
    place = jnp.stack([lax.axis_index("ch"), lax.axis_index("plane")]).astype(jnp.int32)

    def exchange(value):
        return lax.ppermute(value, "ch", [(0, 1), (1, 0)])

    def row(value):
        return value.reshape(1, -1)

    other_grad = exchange(out_grad)
    rounded = jnp.concatenate(
        [channel_params[0:2].astype(bf16).astype(f32), channel_params[2:5], jnp.zeros((3, width_local), f32)]
    )
    own_cols = rounded.T
    other_cols = exchange(rounded).T
    turn = jnp.asarray(turn_table())
    taps = mixer_taps(mixer_params)
    mixed, first = mixer_forward(image_sizes, pixels, taps, channel_params, turn)
    other_mixed = exchange(mixed)
    up_low, up_turned, down_low, down_turned, square = weights_low(up_weight, down_weight)
    bias_col = hidden_bias.astype(bf16).astype(f32)[:, None]
    act, low, stat = norm_forward(
        place, image_sizes, mixed, other_mixed, out_grad, other_grad, own_cols, other_cols
    )

    sums, bias_parts = [], []
    earlier = ()
    for chunk in range(CHUNKS):
        values = feed_chunk(chunk, place, act, low, up_turned, down_low, bias_col, earlier)
        earlier = values[0:2]
        bias_parts.append(values[2][0])
        sums.append(GradientSum(values[3], values[4:]))
    hidden, slopes = earlier
    partial = []
    early, late = sums
    early.to_line()
    tokens, riders = early.sends, [late.kept, early.kept]
    for part in range(SUM_PARTS):
        values, riders = hidden_sums(
            place, hidden, slopes, down_turned, up_low, mixed, other_mixed, stat, own_cols, other_cols, part, tokens, riders
        )
        own_proj, send_proj, own_act, send_act, own_sum = values
        partial.append(((own_proj, own_act, own_sum), exchange((send_proj, send_act, own_sum))))
        if part == 0:
            early.kept = riders[1]
            early.gather_line()
            tokens, riders = [early.piece], riders[:1]
    (late.kept,) = riders
    late.to_line()
    early.gather_plane()
    carry = jnp.concatenate(
        [jnp.zeros((BIAS, width_local), f32), jnp.concatenate(bias_parts).reshape(-1, width_local)]
    )
    carry = jnp.pad(carry, ((0, -carry.shape[0] % 8), (0, 0)))
    done = ()
    tokens, riders = [early.quarter, *late.sends], [late.kept]
    for part in range(BACK_PARTS):
        own, got = partial[part * SUM_PARTS // BACK_PARTS]
        values = backward(
            image_sizes, pixels, out_grad, mixed, first, stat, own, got, own_cols, taps, turn, carry, part, done, riders, tokens
        )
        done, carry = values[0:2], values[2]
        tokens = []
        if part == 0:
            (late.kept,) = values[3:]
            late.gather()
            riders = []
    block_out, pixel_grad = done
    total = small_sum(carry)

    settled = ()
    stats = jnp.zeros((8, 8 * LANES), f32)
    for chunk in range(CHUNKS):
        values = statistics(chunk, sums[chunk].sum, row(up_cols), row(down_rows), stats, settled)
        settled, stats = values[0:4], values[4]
    up_sum, down_sum, up_cols_new, down_rows_new = settled
    (
        mixer_sum,
        mixer_rows_new,
        channel_sum,
        channel_moment_new,
        channel_update,
        bias_sum,
        bias_moment_new,
        bias_update,
        stats,
        channel_square,
    ) = small_update(
        total,
        stats,
        square,
        mixer_params,
        channel_params,
        channel_moment,
        hidden_bias,
        bias_moment,
        mixer_rows,
        down_rows_new,
    )
    got_stats, got_square = exchange((stats, channel_square))
    (
        update_rms,
        up_rows_new,
        down_cols_new,
        mixer_cols_new,
        up_new,
        up_average_new,
        down_new,
        down_average_new,
        mixer_new,
        mixer_average_new,
        channel_new,
        channel_average_new,
        bias_new,
        bias_average_new,
        bias_sum,
        bias_moment_new,
        up_cols_new,
        down_rows_new,
        mixer_rows_new,
    ) = final_update(
        [
            stats,
            got_stats,
            channel_square,
            got_square,
            up_rows,
            down_cols,
            mixer_cols,
            up_cols_new,
            down_rows_new,
            up_sum,
            up_weight,
            up_average,
            down_sum,
            down_weight,
            down_average,
            mixer_sum,
            mixer_params,
            mixer_average,
            mixer_rows_new,
            channel_params,
            channel_average,
            channel_update,
            hidden_bias,
            bias_average,
            bias_update,
            bias_sum,
            bias_moment_new,
            up_cols_new,
            down_rows_new,
        ],
        128,
    )
    return (
        block_out,
        pixel_grad,
        update_rms.reshape(()),
        up_sum,
        up_rows_new,
        up_cols_new,
        up_new,
        up_average_new,
        down_sum,
        down_rows_new,
        down_cols_new,
        down_new,
        down_average_new,
        mixer_sum,
        mixer_rows_new,
        mixer_cols_new,
        mixer_new,
        mixer_average_new,
        channel_sum,
        channel_moment_new,
        channel_new,
        channel_average_new,
        bias_sum,
        bias_moment_new,
        bias_new,
        bias_average_new,
    )


def solution(mesh):
    mesh = jax.sharding.Mesh(mesh.devices.reshape(-1, PLANE, mesh.shape["ch"]), ("line", "plane", "ch"))
    images = ("line", "plane")
    split = P("ch", images)
    over_rows, over_cols, over = P("ch", None), P(None, "ch"), P("ch")
    return jax.shard_map(
        shards,
        mesh=mesh,
        in_specs=(
            split,
            P(images, None),
            split,
            over_cols,
            over_rows,
            over_rows,
            over_cols,
            over,
            P(),
            over,
            over,
            P(),
            over,
            P(),
            over_cols,
            over,
            over_cols,
            over_rows,
            over_rows,
            over_cols,
            over,
        ),
        out_specs=(
            split,
            split,
            P(),
            over_cols,
            P(),
            over,
            over_cols,
            over_cols,
            over_rows,
            over,
            P(),
            over_rows,
            over_rows,
            over_rows,
            over,
            P(),
            over_rows,
            over_rows,
            over_cols,
            over_cols,
            over_cols,
            over_cols,
            over,
            over,
            over,
            over,
        ),
        check_vma=False,
    )
```

```python
import functools

import jax
import jax.numpy as jnp
import ml_dtypes
import numpy as np
from jax import lax
from jax.experimental import pallas as pl
from jax.experimental.pallas import tpu as pltpu
from jax.sharding import PartitionSpec as P

S = 16
AREA = S * S
STEP = 10
LANES = 128

EPSILON_NORM = 1e-06
EPSILON_SQUARE = 1e-30
EPSILON_SCALE = 0.001
LEARN_RATE = 0.3
CLIP_LEVEL = 1.0
AVERAGE_KEEP = 0.9
HALF_ROOT = 0.7071067811865476
DENSITY = 0.3989422804014327
DECAY = 1.0 - STEP ** (-0.8)
FRESH = 1.0 - DECAY
ERF_P = 0.3275911
ERF_A = (0.254829592, -0.284496736, 1.421413741, -1.453152027, 1.061405429)
CHUNKS = 2
SUM_PARTS = 2
BACK_PARTS = 4
PLANE = 4

f32 = jnp.float32
bf16 = jnp.bfloat16
NT = (((1,), (1,)), ((), ()))
TN = (((0,), (0,)), ((), ()))
NN = (((1,), (0,)), ((), ()))


def dot(left, right, dims=NN):
    return lax.dot_general(left, right, dims, preferred_element_type=f32)


def params(mib=24):
    return pltpu.CompilerParams(vmem_limit_bytes=mib * 1024 * 1024)


def cost(flops, nbytes):
    return pl.CostEstimate(flops=int(flops), bytes_accessed=int(nbytes), transcendentals=0)


def image_mask(sizes_ref, image):
    place = lax.broadcasted_iota(jnp.int32, (1, AREA), 1)
    row, column = lax.shift_right_logical(place, 4), place & (S - 1)
    inside = (row < sizes_ref[image, 0]) & (column < sizes_ref[image, 1])
    return jnp.where(inside, 1.0, 0.0).astype(f32)


def first_power(table, half):
    base = half * 256
    rate = jnp.exp(table[base : base + 64])
    freq = table[base + 64 : base + 128]
    damp = jnp.exp(-rate)
    return (
        rate,
        damp * jnp.cos(freq),
        damp * jnp.sin(freq),
        table[base + 128 : base + 192],
        table[base + 192 : base + 256],
    )


def taps_kernel(params_ref, out_ref):
    table = params_ref[...].T
    for half in range(2):
        _, step_real, step_imag, real, imag = first_power(table, half)
        here_real, here_imag = jnp.ones_like(step_real), jnp.zeros_like(step_real)
        for place in range(S):
            tap = jnp.sum(real * here_real - imag * here_imag, axis=0, keepdims=True)
            out_ref[half, place : place + 1, :] = tap.astype(bf16).astype(f32)
            here_real, here_imag = (
                here_real * step_real - here_imag * step_imag,
                here_real * step_imag + here_imag * step_real,
            )


def mixer_taps(mixer_params):
    width = mixer_params.shape[0]
    return pl.pallas_call(
        taps_kernel,
        out_shape=jax.ShapeDtypeStruct((2, S, width), f32),
        compiler_params=params(),
        name="mixer_taps",
    )(mixer_params)


def taps_back(params_ref, grad_ref, table_ref):
    table = params_ref[...].T
    for half in range(2):
        rate, step_real, step_imag, real, imag = first_power(table, half)
        here_real, here_imag = jnp.ones_like(step_real), jnp.zeros_like(step_real)
        zero = jnp.zeros_like(step_real)
        sum_real, sum_imag, far_real, far_imag = zero, zero, zero, zero
        for place in range(S):
            grad = grad_ref[half * S + place : half * S + place + 1, :]
            wave_real, wave_imag = grad * here_real, grad * here_imag
            sum_real, sum_imag = sum_real + wave_real, sum_imag + wave_imag
            far_real, far_imag = far_real + place * wave_real, far_imag + place * wave_imag
            here_real, here_imag = (
                here_real * step_real - here_imag * step_imag,
                here_real * step_imag + here_imag * step_real,
            )
        base = half * 256
        table_ref[base : base + 64] = -rate * (real * far_real - imag * far_imag)
        table_ref[base + 64 : base + 128] = -(real * far_imag + imag * far_real)
        table_ref[base + 128 : base + 192] = sum_real
        table_ref[base + 192 : base + 256] = -sum_imag


def block_rows(place):
    return slice(place * S, (place + 1) * S)


def causal(source_ref, taps_ref, half, lanes, base=0):
    rows = [source_ref[base + place * S : base + (place + 1) * S, lanes] for place in range(S)]
    for place in range(S):
        total = rows[place] * taps_ref[half, 0:1, lanes]
        for back in range(1, place + 1):
            total += rows[place - back] * taps_ref[half, back : back + 1, lanes]
        yield total


def anticausal(source_ref, taps_ref, half, lanes):
    rows = [source_ref[block_rows(place), lanes] for place in range(S)]
    for place in range(S):
        total = rows[place] * taps_ref[half, 0:1, lanes]
        for ahead in range(1, S - place):
            total += rows[place + ahead] * taps_ref[half, ahead : ahead + 1, lanes]
        yield total


def mixer_kernel(
    sizes_ref, pixels_ref, taps_ref, channel_ref, turn_ref, mixed_ref, first_ref, cells_ref, low_ref, wide_ref, *, per_step
):
    width = pixels_ref.shape[0]
    for part in range(per_step):
        spot = slice(part * AREA, (part + 1) * AREA)
        mask = image_mask(sizes_ref, pl.program_id(0) * per_step + part)
        masked = (pixels_ref[:, spot].astype(f32) * mask).astype(bf16)
        cells, low, wide = cells_ref.at[part], low_ref.at[part], wide_ref.at[part]
        cells[...] = dot(turn_ref[...], masked, NT)
        for start in range(0, width, LANES):
            lanes = slice(start, start + LANES)
            for place, value in enumerate(causal(cells, taps_ref, 0, lanes)):
                low[block_rows(place), lanes] = value.astype(bf16)
        wide[...] = dot(turn_ref[AREA:, :], low[...])
        first_ref[spot, :] = wide[...].astype(bf16)
        for start in range(0, width, LANES):
            lanes = slice(start, start + LANES)
            skip = channel_ref[2:3, lanes]
            for place, value in enumerate(causal(wide, taps_ref, 1, lanes)):
                own = cells[AREA + place * S : AREA + (place + 1) * S, lanes]
                low[block_rows(place), lanes] = (value + skip * own).astype(bf16)
        mixed_ref[:, spot] = dot(low[...], turn_ref[AREA:, :], TN).astype(bf16)


def mixer_forward(sizes, pixels, taps, channel, turn):
    width, count = pixels.shape
    per_step = 2
    span = per_step * AREA
    grid_spec = pltpu.PrefetchScalarGridSpec(
        num_scalar_prefetch=1,
        grid=(count // span,),
        in_specs=[
            pl.BlockSpec((width, span), lambda i, *_: (0, i)),
            pl.BlockSpec(taps.shape, lambda i, *_: (0, 0, 0)),
            pl.BlockSpec(channel.shape, lambda i, *_: (0, 0)),
            pl.BlockSpec(turn.shape, lambda i, *_: (0, 0)),
        ],
        out_specs=[
            pl.BlockSpec((width, span), lambda i, *_: (0, i)),
            pl.BlockSpec((span, width), lambda i, *_: (i, 0)),
        ],
        scratch_shapes=[
            pltpu.VMEM((per_step, 2 * AREA, width), f32),
            pltpu.VMEM((per_step, AREA, width), bf16),
            pltpu.VMEM((per_step, AREA, width), f32),
        ],
    )
    return pl.pallas_call(
        functools.partial(mixer_kernel, per_step=per_step),
        grid_spec=grid_spec,
        out_shape=[
            jax.ShapeDtypeStruct((width, count), bf16),
            jax.ShapeDtypeStruct((count, width), bf16),
        ],
        compiler_params=params(),
        cost_estimate=cost(8e9, 9e6),
        name="mixer_forward",
    )(sizes, pixels, taps, channel, turn)


def norm_kernel(
    place_ref, sizes_ref, own_ref, other_ref, own_grad_ref, other_grad_ref, own_cols_ref, other_cols_ref, act_ref, low_ref, stat_ref, *, per_step
):
    width = 2.0 * own_ref.shape[0]
    mine = place_ref[0]
    for part in range(per_step):
        spot = slice(part * AREA, (part + 1) * AREA)
        mask = image_mask(sizes_ref, pl.program_id(0) * per_step + part)
        own, other = own_ref[:, spot].astype(f32), other_ref[:, spot].astype(f32)
        mean = (jnp.sum(own, axis=0, keepdims=True) + jnp.sum(other, axis=0, keepdims=True)) / width
        own, other = own - mean, other - mean
        spread = (
            jnp.sum(own * own, axis=0, keepdims=True) + jnp.sum(other * other, axis=0, keepdims=True)
        ) / width
        scale = lax.rsqrt(spread + EPSILON_NORM)
        stat_ref[0:1, spot] = mean
        stat_ref[1:2, spot] = scale
        for which, value, grad_ref, cols_ref in (
            (mine, own, own_grad_ref, own_cols_ref),
            (1 - mine, other, other_grad_ref, other_cols_ref),
        ):
            act_ref[which, :, spot] = (
                value * scale * cols_ref[:, 0:1] + cols_ref[:, 1:2]
            ).astype(bf16)
            grad = grad_ref[:, spot].astype(f32)
            low_ref[which, :, spot] = (grad * (mask * cols_ref[:, 3:4])).astype(bf16)


def norm_forward(place, sizes, own, other, own_grad, other_grad, own_cols, other_cols):
    width, count = own.shape
    per_step = 2
    span = per_step * AREA
    block = pl.BlockSpec((width, span), lambda i, *_: (0, i))
    cols = pl.BlockSpec(own_cols.shape, lambda i, *_: (0, 0))
    pair = pl.BlockSpec((2, width, span), lambda i, *_: (0, 0, i))
    grid_spec = pltpu.PrefetchScalarGridSpec(
        num_scalar_prefetch=2,
        grid=(count // span,),
        in_specs=[block, block, block, block, cols, cols],
        out_specs=[pair, pair, pl.BlockSpec((8, span), lambda i, *_: (0, i))],
    )
    return pl.pallas_call(
        functools.partial(norm_kernel, per_step=per_step),
        grid_spec=grid_spec,
        out_shape=[
            jax.ShapeDtypeStruct((2, width, count), bf16),
            jax.ShapeDtypeStruct((2, width, count), bf16),
            jax.ShapeDtypeStruct((8, count), f32),
        ],
        compiler_params=params(),
        cost_estimate=cost(1e9, 26e6),
        name="norm_forward",
    )(place, sizes, own, other, own_grad, other_grad, own_cols, other_cols)


def weights_kernel(up_ref, down_ref, up_low_ref, up_turned_ref, down_low_ref, down_turned_ref, square_ref):
    @pl.when(pl.program_id(0) == 0)
    def _():
        square_ref[...] = jnp.zeros_like(square_ref)

    for row, source_ref, low_ref, turned_ref in (
        (0, up_ref, up_low_ref, up_turned_ref),
        (1, down_ref, down_low_ref, down_turned_ref),
    ):
        value = source_ref[...]
        units = square_ref.shape[1]
        for start in range(0, value.shape[1], units):
            part = value[:, start : start + units]
            square_ref[row : row + 1, :] += jnp.sum(part * part, axis=0, keepdims=True)
        low_ref[...] = value.astype(bf16)
        turned_ref[...] = value.T.astype(bf16)


def weights_low(up, down):
    full, hidden_local = up.shape
    units = 384
    column = lambda i: (0, i)
    row = lambda i: (i, 0)
    return pl.pallas_call(
        weights_kernel,
        grid=(hidden_local // units,),
        in_specs=[pl.BlockSpec((full, units), column), pl.BlockSpec((full // 2, full), row)],
        out_specs=[
            pl.BlockSpec((full, units), column),
            pl.BlockSpec((units, full), row),
            pl.BlockSpec((units, full), row),
            pl.BlockSpec((full, units), column),
            pl.BlockSpec((8, units), lambda i: (0, 0)),
        ],
        out_shape=[
            jax.ShapeDtypeStruct((full, hidden_local), bf16),
            jax.ShapeDtypeStruct((hidden_local, full), bf16),
            jax.ShapeDtypeStruct((hidden_local, full), bf16),
            jax.ShapeDtypeStruct((full, hidden_local), bf16),
            jax.ShapeDtypeStruct((8, units), f32),
        ],
        compiler_params=params(),
        cost_estimate=cost(1e7, 19e6),
        name="weights_low",
    )(up, down)


def gelu_pair(pre):
    bell = jnp.exp(-0.5 * pre * pre)
    base = 1.0 + (ERF_P * HALF_ROOT) * jnp.abs(pre)
    guess = pl.reciprocal(base, approx=True)
    part = guess * (2.0 - base * guess)
    poly = 0.5 * ERF_A[4]
    for factor in ERF_A[3::-1]:
        poly = poly * part + 0.5 * factor
    tail = poly * part * bell
    upper = jnp.where(pre >= 0.0, 1.0 - tail, tail)
    return pre * upper, upper + pre * bell * DENSITY


def split_out(source_ref, digit, part_refs):
    rows = part_refs[0].shape[0]
    for away, ref in enumerate(part_refs):
        start = pl.multiple_of((digit ^ away) * rows, rows)
        ref[...] = source_ref[pl.ds(start, rows), :].astype(ref.dtype)


def chunk_kernel(place_ref, act_ref, low_ref, up_ref, down_ref, bias_ref, *refs):
    hidden_ref, slope_ref, bias_grad_ref = refs[-5 - PLANE : -2 - PLANE]
    part_refs, (grad_acc, bias_acc) = refs[-2 - PLANE : -2], refs[-2:]
    step = pl.program_id(0)

    @pl.when(step == 0)
    def _():
        grad_acc[...] = jnp.zeros_like(grad_acc)
        bias_acc[...] = jnp.zeros_like(bias_acc)

    halves, width, span = act_ref.shape
    units = up_ref.shape[0]
    full = halves * width
    tile = 256
    tiles = [(row, start) for start in range(0, span, tile) for row in range(0, units, tile)]

    def products(row, start):
        rows, spot = slice(row, row + tile), slice(start, start + tile)
        pre = dot(up_ref[rows, :], act_ref[:, :, spot].reshape(full, tile)) + bias_ref[rows, :]
        return pre, dot(down_ref[rows, :], low_ref[:, :, spot].reshape(full, tile))

    ready = products(*tiles[0])
    for at, (row, start) in enumerate(tiles):
        pre, back = ready
        if at + 1 < len(tiles):
            ready = products(*tiles[at + 1])
        rows, spot = slice(row, row + tile), slice(start, start + tile)
        hidden, slope = gelu_pair(pre)
        hidden_ref[rows, spot] = hidden.astype(bf16)
        slope_ref[rows, spot] = (back * slope).astype(bf16)
    grad_acc[:units, :] += dot(slope_ref[...], act_ref[...].reshape(full, span), NT)
    grad_acc[units:, :] += dot(hidden_ref[...], low_ref[...].reshape(full, span), NT)
    bias_acc[...] += dot(jnp.ones((S, span), bf16), slope_ref[...], NT)

    @pl.when(step == pl.num_programs(0) - 1)
    def _():
        split_out(grad_acc, place_ref[1], part_refs)
        bias_grad_ref[...] = bias_acc[0:8, :]


def feed_chunk(chunk, place, act, low, up_turned, down, bias, earlier):
    halves, width, count = act.shape
    full = halves * width
    hidden_local = down.shape[0]
    units = hidden_local // CHUNKS
    span = 512 if chunk == 0 else 1024
    pair = pl.BlockSpec((halves, width, span), lambda i, *_: (0, 0, i))
    weight = pl.BlockSpec((units, full), lambda i, *_: (chunk, 0))
    wide = pl.BlockSpec((units, span), lambda i, *_: (chunk, i))
    whole = lambda i, *_: (0, 0)
    rows = 2 * units // PLANE
    grid_spec = pltpu.PrefetchScalarGridSpec(
        num_scalar_prefetch=1,
        grid=(count // span,),
        in_specs=[pair, pair, weight, weight, pl.BlockSpec((units, 1), lambda i, *_: (chunk, 0))]
        + [pl.BlockSpec(memory_space=pl.ANY)] * len(earlier),
        out_specs=[wide, wide, pl.BlockSpec((8, units), whole)] + [pl.BlockSpec((rows, full), whole)] * PLANE,
        scratch_shapes=[pltpu.VMEM((2 * units, full), f32), pltpu.VMEM((S, units), f32)],
    )
    return pl.pallas_call(
        chunk_kernel,
        grid_spec=grid_spec,
        out_shape=[
            jax.ShapeDtypeStruct((hidden_local, count), bf16),
            jax.ShapeDtypeStruct((hidden_local, count), bf16),
            jax.ShapeDtypeStruct((8, units), f32),
            jax.ShapeDtypeStruct((rows, full), f32),
        ]
        + [jax.ShapeDtypeStruct((rows, full), bf16)] * (PLANE - 1),
        input_output_aliases={6: 0, 7: 1} if earlier else {},
        compiler_params=params(56),
        cost_estimate=cost(8 * count * full * units, 4 * count * (full + units)),
        name="feed_chunk_%d" % chunk,
    )(place, act, low, up_turned, down, bias, *earlier)


def across(value, stride):
    size = lax.axis_size("line") * PLANE
    return lax.ppermute(value, ("line", "plane"), [(i, i ^ stride) for i in range(size)])


class SmallSum:
    def __init__(self, value):
        self.value = value
        self.send(1)

    def send(self, base):
        self.got = [across(self.value, base * away) for away in range(1, 4)]

    def add(self):
        near, *far = self.got
        self.value = (self.value + near) + (far[0] + far[1])

    def finish(self):
        self.add()
        stride = PLANE * 4
        while stride < lax.axis_size("line") * PLANE:
            self.value = self.value + across(self.value, stride)
            stride *= 2
        return self.value


def along(value, axis, away):
    return lax.ppermute(value, axis, [(i, i ^ away) for i in range(lax.axis_size(axis))])


class GradientSum:
    def __init__(self, kept, sends):
        self.kept = kept
        self.got = [along(value, "plane", away) for away, value in enumerate(sends, 1)]

    def add(self):
        total = self.kept
        for value in self.got:
            total = total + value.astype(f32)
        return total

    def to_line(self):
        size = lax.axis_size("line")
        total = self.add()
        parts = total.reshape(size, -1, total.shape[1])

        def part(away):
            return lax.dynamic_index_in_dim(parts, lax.axis_index("line") ^ away, 0, keepdims=False)

        self.kept = part(0)
        self.sends = [part(away).astype(bf16) for away in range(1, size)]
        self.got = [along(value, "line", away) for away, value in enumerate(self.sends, 1)]

    def to_piece(self):
        self.piece = self.add().astype(bf16)

    def gather(self):
        self.to_piece()
        self.sum = lax.all_gather(self.piece, ("plane", "line"), axis=0, tiled=True)

    def gather_line(self):
        self.to_piece()
        size = lax.axis_size("line")
        self.pieces = [self.piece] + [along(self.piece, "line", away) for away in range(1, size)]

    def gather_plane(self):
        self.quarter = jnp.concatenate(self.pieces)
        self.quarters = [self.quarter] + [along(self.quarter, "plane", away) for away in range(1, PLANE)]


def sums_kernel(place_ref, hidden_ref, slope_ref, down_ref, up_ref, own_ref, other_ref, stat_ref, own_cols_ref, other_cols_ref, *refs, skipped, split):
    own_proj_ref, other_proj_ref, own_act_ref, other_act_ref, sum_ref = refs[skipped : skipped + 5]
    width = own_ref.shape[0]
    mine = place_ref[0]
    own_rows = pl.ds(pl.multiple_of(mine * width, width), width)
    other_rows = pl.ds(pl.multiple_of((1 - mine) * width, width), width)
    if split:

        def part(which, rows):
            weight_ref, value_ref = ((down_ref, hidden_ref), (up_ref, slope_ref))[which]
            return dot(weight_ref[rows, :], value_ref[...])

    else:
        total_ref = refs[-1]
        total_ref[0] = dot(down_ref[...], hidden_ref[...])
        total_ref[1] = dot(up_ref[...], slope_ref[...])

        def part(which, rows):
            return total_ref[which, rows, :]

    own_proj_ref[...] = part(0, own_rows)
    other_proj_ref[...] = part(0, other_rows).astype(bf16)
    mean, scale = stat_ref[0:1, :], stat_ref[1:2, :]
    sums = []
    for rows, out_ref, value_ref, cols_ref in (
        (own_rows, own_act_ref, own_ref, own_cols_ref),
        (other_rows, other_act_ref, other_ref, other_cols_ref),
    ):
        act = part(1, rows)
        out_ref[...] = act.astype(out_ref.dtype)
        act = act * cols_ref[:, 0:1]
        normed = (value_ref[...].astype(f32) - mean) * scale
        sums.append(jnp.sum(act, axis=0, keepdims=True))
        sums.append(jnp.sum(act * normed, axis=0, keepdims=True))
    sum_ref[0:1, :] = sums[0] + sums[2]
    sum_ref[1:2, :] = sums[1] + sums[3]


def hidden_sums(place, hidden, slopes, down_turned, up, own, other, stat, own_cols, other_cols, part, tokens, riders):
    width, total = own.shape
    count = total // SUM_PARTS
    hidden_local = hidden.shape[0]
    span = 512
    base = part * (count // span)
    column = lambda i, *_: (0, base + i)
    out = lambda i, *_: (0, i)
    fixed = lambda i, *_: (0, 0)
    wide = pl.BlockSpec((hidden_local, span), column)
    block = pl.BlockSpec((width, span), column)
    result = pl.BlockSpec((width, span), out)
    cols = pl.BlockSpec(own_cols.shape, fixed)
    grid_spec = pltpu.PrefetchScalarGridSpec(
        num_scalar_prefetch=1,
        grid=(count // span,),
        in_specs=[
            wide,
            wide,
            pl.BlockSpec(down_turned.shape, fixed),
            pl.BlockSpec(up.shape, fixed),
            block,
            block,
            pl.BlockSpec((8, span), column),
            cols,
            cols,
        ]
        + [pl.BlockSpec(memory_space=pl.ANY)] * (len(riders) + len(tokens)),
        out_specs=[result, result, result, result, pl.BlockSpec((8, span), out)]
        + [pl.BlockSpec(memory_space=pl.ANY)] * len(riders),
        scratch_shapes=[] if part == 0 else [pltpu.VMEM((2, 2 * width, span), f32)],
    )
    values = pl.pallas_call(
        functools.partial(sums_kernel, skipped=len(riders) + len(tokens), split=part == 0),
        grid_spec=grid_spec,
        out_shape=[
            jax.ShapeDtypeStruct((width, count), f32),
            jax.ShapeDtypeStruct((width, count), bf16),
            jax.ShapeDtypeStruct((width, count), f32),
            jax.ShapeDtypeStruct((width, count), bf16),
            jax.ShapeDtypeStruct((8, count), f32),
        ]
        + [jax.ShapeDtypeStruct(rider.shape, rider.dtype) for rider in riders],
        input_output_aliases={10 + at: 5 + at for at in range(len(riders))},
        compiler_params=params(40),
        cost_estimate=cost(8 * count * width * hidden_local, 4 * count * (hidden_local + 3 * width)),
        name="hidden_sums_%d" % part,
    )(place, hidden, slopes, down_turned, up, own, other, stat, own_cols, other_cols, *riders, *tokens)
    return values[:5], values[5:]


TAPS, ROWS, BIAS = 0, 32, 40


def correlate(left_ref, right_ref, sum_ref, half, lanes):
    left = [left_ref[block_rows(place), lanes] for place in range(S)]
    right = [right_ref[block_rows(place), lanes].astype(f32) for place in range(S)]
    for back in range(S):
        total = left[back] * right[0]
        for place in range(back + 1, S):
            total += left[place] * right[place - back]
        sum_ref[half, block_rows(back), lanes] += total


def backward_kernel(
    sizes_ref,
    pixels_ref,
    grad_ref,
    mixed_ref,
    first_ref,
    stat_ref,
    own_proj_ref,
    got_proj_ref,
    own_act_ref,
    got_act_ref,
    own_sum_ref,
    got_sum_ref,
    cols_ref,
    taps_ref,
    turn_ref,
    carry_ref,
    *refs,
    base,
    skipped,
):
    out_ref, pixel_grad_ref, small_ref = refs[skipped : skipped + 3]
    sum_ref, channel_sum, cells_ref, low_ref, wide_ref, back_ref = refs[-6:]
    step = pl.program_id(0)
    width = pixels_ref.shape[0]
    full = 2.0 * width

    @pl.when(step == 0)
    def _():
        sum_ref[...] = jnp.zeros_like(sum_ref)
        channel_sum[...] = jnp.zeros_like(channel_sum)

    mask = image_mask(sizes_ref, base + step)
    pixels = pixels_ref[...].astype(f32)
    grad = grad_ref[...].astype(f32)
    masked = pixels * mask
    gain, skip, layer, shift = cols_ref[:, 0:1], cols_ref[:, 2:3], cols_ref[:, 3:4], cols_ref[:, 4:5]

    def gather(row, value):
        channel_sum[row] += value[:, :LANES] + value[:, LANES:]

    masked_grad = grad * mask
    branch = own_proj_ref[...] + got_proj_ref[...].astype(f32) + shift
    out_ref[...] = pixels + mask * layer * branch
    gather(3, masked_grad * branch)
    gather(4, masked_grad)

    scale = stat_ref[1:2, :]
    normed = (mixed_ref[...].astype(f32) - stat_ref[0:1, :]) * scale
    act = own_act_ref[...] + got_act_ref[...].astype(f32)
    gather(0, act * normed)
    gather(1, act)
    plain = (own_sum_ref[0:1, :] + got_sum_ref[0:1, :]) / full
    tilt = (own_sum_ref[1:2, :] + got_sum_ref[1:2, :]) / full
    mixed_low = (scale * (act * gain - plain - normed * tilt)).astype(bf16)
    mixed_grad = mixed_low.astype(f32)
    gather(2, mixed_grad * masked)

    cells_ref[...] = dot(turn_ref[:AREA, :], masked.astype(bf16), NT)
    wide_ref[...] = dot(turn_ref[AREA:, :], mixed_low, NT)
    for start in range(0, width, LANES):
        lanes = slice(start, start + LANES)
        for place, value in enumerate(anticausal(wide_ref, taps_ref, 1, lanes)):
            low_ref[block_rows(place), lanes] = value.astype(bf16)
        correlate(wide_ref, first_ref, sum_ref, 1, lanes)
    back_ref[...] = dot(turn_ref[AREA:, :], low_ref[...])
    for start in range(0, width, LANES):
        lanes = slice(start, start + LANES)
        for place, value in enumerate(anticausal(back_ref, taps_ref, 0, lanes)):
            wide_ref[block_rows(place), lanes] = value
        correlate(back_ref, cells_ref, sum_ref, 0, lanes)
    pixel_grad_ref[...] = grad + mask * (wide_ref[...].T + skip * mixed_grad)

    @pl.when(step == pl.num_programs(0) - 1)
    def _():
        small_ref[...] = carry_ref[...]
        for half in range(2):
            for back in range(S):
                row = TAPS + half * S + back
                small_ref[row : row + 1, :] += jnp.sum(
                    sum_ref[half, block_rows(back), :], axis=0, keepdims=True
                )
        for row in range(5):
            small_ref[ROWS + row : ROWS + row + 1, :] += jnp.sum(channel_sum[row].T, axis=0, keepdims=True)


def backward(sizes, pixels, grad, mixed, first, stat, own, got, cols, taps, turn, carry, part, earlier, riders, tokens):
    own_proj, own_act, own_sum = own
    got_proj, got_act, got_sum = got
    width, total = pixels.shape
    count = total // BACK_PARTS
    base = part * (count // AREA)
    inner = base % (own_proj.shape[1] // AREA)
    column = lambda i, *_: (0, base + i)
    here = lambda i, *_: (0, inner + i)
    fixed = lambda i, *_: (0, 0)
    block = pl.BlockSpec((width, AREA), column)
    local = pl.BlockSpec((width, AREA), here)
    anywhere = pl.BlockSpec(memory_space=pl.ANY)
    grid_spec = pltpu.PrefetchScalarGridSpec(
        num_scalar_prefetch=1,
        grid=(count // AREA,),
        in_specs=[
            block,
            block,
            block,
            pl.BlockSpec((AREA, width), lambda i, *_: (base + i, 0)),
            pl.BlockSpec((8, AREA), column),
            local,
            local,
            local,
            local,
            pl.BlockSpec((8, AREA), here),
            pl.BlockSpec((8, AREA), here),
            pl.BlockSpec(cols.shape, fixed),
            pl.BlockSpec(taps.shape, lambda i, *_: (0, 0, 0)),
            pl.BlockSpec(turn.shape, fixed),
            pl.BlockSpec(carry.shape, fixed),
        ]
        + [anywhere] * (len(earlier) + len(riders) + len(tokens)),
        out_specs=[block, block, pl.BlockSpec(carry.shape, fixed)] + [anywhere] * len(riders),
        scratch_shapes=[
            pltpu.VMEM((2, AREA, width), f32),
            pltpu.VMEM((5, width, LANES), f32),
            pltpu.VMEM((AREA, width), f32),
            pltpu.VMEM((AREA, width), bf16),
            pltpu.VMEM((AREA, width), f32),
            pltpu.VMEM((AREA, width), f32),
        ],
    )
    return pl.pallas_call(
        functools.partial(backward_kernel, base=base, skipped=len(earlier) + len(riders) + len(tokens)),
        grid_spec=grid_spec,
        out_shape=[
            jax.ShapeDtypeStruct((width, total), f32),
            jax.ShapeDtypeStruct((width, total), f32),
            jax.ShapeDtypeStruct(carry.shape, f32),
        ]
        + [jax.ShapeDtypeStruct(rider.shape, rider.dtype) for rider in riders],
        input_output_aliases={16 + at: at for at in range(len(earlier))}
        | {16 + len(earlier) + at: 3 + at for at in range(len(riders))},
        compiler_params=params(),
        cost_estimate=cost(10e9 / BACK_PARTS, 44e6 / BACK_PARTS),
        name="backward_%d" % part,
    )(
        sizes, pixels, grad, mixed, first, stat, own_proj, got_proj, own_act, got_act, own_sum, got_sum, cols, taps, turn, carry, *earlier, *riders, *tokens
    )


UP_ROW, UP_MASS, DOWN_COL, DOWN_MASS, MIXER_COL, MIXER_MASS, SCALARS = range(7)


def fold(value):
    total = value[:, :LANES]
    for start in range(LANES, value.shape[1], LANES):
        total += value[:, start : start + LANES]
    return total


def as_row(ref):
    return ref[...].reshape(1, ref.shape[0])


def to_flat(ref, value):
    ref[...] = value.reshape(ref.shape[0])


def to_column(row):
    return jnp.broadcast_to(row, (LANES, row.shape[1])).T


def to_row(columns):
    return jnp.sum(columns.T, axis=0, keepdims=True)


def statistics_kernel(place_ref, *refs, quarters, skipped, line_parts):
    sources, refs = refs[:quarters], refs[quarters:]
    up_old_ref, down_old_ref, carry_ref = refs[:3]
    up_ref, down_ref, up_new_ref, down_new_ref, stat_ref = refs[3 + skipped : 8 + skipped]
    quarter_ref = refs[-1]
    step = pl.program_id(0)
    plane, line = place_ref[1], place_ref[2]
    steps = PLANE // 2

    @pl.when(step == 0)
    def _():
        stat_ref[...] = carry_ref[...]

    for kind, old_ref, new_ref, columns, mass in (
        (0, up_old_ref, up_new_ref, UP_ROW, UP_MASS),
        (1, down_old_ref, down_new_ref, DOWN_COL, DOWN_MASS),
    ):
        if quarters == 2:
            value = sources[kind][...].astype(f32)
        else:
            for away, source_ref in enumerate(sources):

                @pl.when((kind * steps + step) ^ plane == away)
                def _():
                    rows = quarter_ref.shape[0] // line_parts

                    def move(at, _):
                        target = pl.ds(pl.multiple_of(at * rows, rows), rows)
                        source = pl.ds(pl.multiple_of((at ^ line) * rows, rows), rows)
                        quarter_ref[target, :] = source_ref[source, :].astype(f32)
                        return 0

                    lax.fori_loop(0, line_parts, move, 0)

            value = quarter_ref[...]
        if kind == 0:
            up_ref[...] = value.T
        else:
            down_ref[...] = value
        square = value * value
        mean = jnp.sum(fold(square), axis=1, keepdims=True) / value.shape[1]
        fresh = DECAY * to_column(old_ref[...]) + FRESH * (mean + EPSILON_SQUARE)
        new_ref[...] = fresh.T[0:1, :]
        stat_ref[columns : columns + 1, : value.shape[1]] += jnp.sum(square, axis=0, keepdims=True)
        stat_ref[mass : mass + 1, : value.shape[1]] += jnp.sum(
            square * (1.0 / fresh[:, 0:1]), axis=0, keepdims=True
        )


def statistics(chunk, place, sources, up_cols, down_rows, carry, earlier, rider):
    hidden_local = up_cols.shape[1]
    units = hidden_local // CHUNKS
    full = sources[0].shape[1]
    rows = 2 * units // PLANE
    steps = PLANE // 2
    base = chunk * steps
    row = pl.BlockSpec((1, rows), lambda i: (0, base + i))
    anywhere = pl.BlockSpec(memory_space=pl.ANY)
    fixed = pl.BlockSpec(carry.shape, lambda i: (0, 0))
    if len(sources) == 2:
        specs = [
            pl.BlockSpec((rows, full), lambda i: (i, 0)),
            pl.BlockSpec((rows, full), lambda i: (steps + i, 0)),
        ]
    else:
        specs = [pl.BlockSpec((rows, full), lambda i: (0, 0))] * PLANE
    first = 4 + len(sources)
    return pl.pallas_call(
        functools.partial(statistics_kernel, quarters=len(sources), skipped=len(earlier) + 1, line_parts=lax.axis_size("line")),
        grid=(steps,),
        in_specs=[pl.BlockSpec(memory_space=pltpu.SMEM)]
        + specs
        + [row, row, fixed]
        + [anywhere] * (len(earlier) + 1),
        out_specs=[
            pl.BlockSpec((full, rows), lambda i: (0, base + i)),
            pl.BlockSpec((rows, full), lambda i: (base + i, 0)),
            row,
            row,
            fixed,
            anywhere,
        ],
        out_shape=[
            jax.ShapeDtypeStruct((full, hidden_local), f32),
            jax.ShapeDtypeStruct((hidden_local, full), f32),
            jax.ShapeDtypeStruct((1, hidden_local), f32),
            jax.ShapeDtypeStruct((1, hidden_local), f32),
            jax.ShapeDtypeStruct(carry.shape, f32),
            jax.ShapeDtypeStruct(rider.shape, rider.dtype),
        ],
        input_output_aliases={first + at: at for at in range(len(earlier))} | {first + len(earlier): 5},
        scratch_shapes=[pltpu.VMEM((rows, full), f32)],
        compiler_params=params(40),
        cost_estimate=cost(1e8 / CHUNKS, 14e6 / CHUNKS),
        name="statistics_%d" % chunk,
    )(place, *sources, up_cols, down_rows, carry, *earlier, rider)


def small_kernel(
    sum_ref,
    stat_ref,
    square_ref,
    params_ref,
    channel_ref,
    moment_ref,
    bias_ref,
    bias_moment_ref,
    rows_ref,
    down_rows_new_ref,
    mixer_grad_ref,
    rows_new_ref,
    channel_grad_ref,
    moment_new_ref,
    channel_update_ref,
    bias_grad_ref,
    bias_moment_new_ref,
    bias_update_ref,
    out_ref,
    channel_square_ref,
    table_ref,
):
    out_ref[...] = stat_ref[...]
    taps_back(params_ref, sum_ref, table_ref)
    grad = table_ref[...].T
    mixer_grad_ref[...] = grad
    states = grad.shape[1]
    square = grad * grad
    mean = jnp.sum(fold(square), axis=1, keepdims=True) / states
    fresh = DECAY * to_column(as_row(rows_ref)) + FRESH * (mean + EPSILON_SQUARE)
    rows_new = fresh.T[0:1, :]
    rows_new_ref[...] = rows_new
    out_ref[MIXER_COL : MIXER_COL + 1, :states] = jnp.sum(square, axis=0, keepdims=True)
    out_ref[MIXER_MASS : MIXER_MASS + 1, :states] = jnp.sum(square * (1.0 / fresh[:, 0:1]), axis=0, keepdims=True)

    layer = channel_ref[3:4, :]
    channel_grad_ref[0:4, :] = sum_ref[ROWS : ROWS + 4, :]
    channel_grad_ref[4:5, :] = sum_ref[ROWS + 4 : ROWS + 5, :] * layer
    grad = channel_grad_ref[...]
    moment = DECAY * moment_ref[...] + FRESH * (grad * grad + EPSILON_SQUARE)
    moment_new_ref[...] = moment
    channel_update = grad * lax.rsqrt(moment)
    channel_update_ref[...] = channel_update

    width = layer.shape[1]
    for at in range(bias_grad_ref.shape[1] // width):
        bias_grad_ref[:, at * width : (at + 1) * width] = sum_ref[BIAS + at : BIAS + at + 1, :]
    grad = bias_grad_ref[...]
    moment = DECAY * as_row(bias_moment_ref) + FRESH * (grad * grad + EPSILON_SQUARE)
    bias_moment_new_ref[...] = moment
    bias_update = grad * lax.rsqrt(moment)
    bias_update_ref[...] = bias_update

    def total(value):
        return jnp.sum(value, keepdims=True)

    channel = channel_ref[...]
    table = params_ref[...]
    bias = as_row(bias_ref)
    scalars = (
        total(channel_update * channel_update) + total(bias_update * bias_update),
        total(down_rows_new_ref[...]),
        total(rows_new),
        total(square_ref[0:1, :]),
        total(square_ref[1:2, :]),
        total(table * table),
        total(bias * bias),
    )
    for at, value in enumerate(scalars):
        out_ref[SCALARS : SCALARS + 1, at * LANES : (at + 1) * LANES] = jnp.broadcast_to(value, (1, LANES))
    channel_square_ref[...] = jnp.broadcast_to(jnp.sum(channel * channel, axis=1, keepdims=True), (5, LANES))


def small_update(total, stat, square, mixer_params, channel_params, channel_moment, bias, bias_moment, rows, down_rows_new):
    width, states = mixer_params.shape
    shapes = [
        (width, states),
        (1, width),
        channel_params.shape,
        channel_params.shape,
        channel_params.shape,
        (1, bias.shape[0]),
        (1, bias.shape[0]),
        (1, bias.shape[0]),
        (8, 8 * LANES),
        (5, LANES),
    ]
    return pl.pallas_call(
        small_kernel,
        out_shape=[jax.ShapeDtypeStruct(shape, f32) for shape in shapes],
        scratch_shapes=[pltpu.VMEM((states, width), f32)],
        compiler_params=params(),
        cost_estimate=cost(1e7, 2e6),
        name="small_update",
    )(total, stat, square, mixer_params, channel_params, channel_moment, bias, bias_moment, rows, down_rows_new)


def update_kernel(
    stat_ref,
    got_ref,
    channel_square_ref,
    channel_got_ref,
    up_rows_ref,
    down_cols_ref,
    mixer_cols_ref,
    up_cols_new_ref,
    down_rows_new_ref,
    up_grad_ref,
    up_ref,
    up_average_ref,
    down_grad_ref,
    down_ref,
    down_average_ref,
    mixer_grad_ref,
    mixer_ref,
    mixer_average_ref,
    mixer_rows_new_ref,
    channel_ref,
    channel_average_ref,
    channel_update_ref,
    bias_ref,
    bias_average_ref,
    bias_update_ref,
    bias_grad_ref,
    bias_moment_ref,
    up_cols_all_ref,
    down_rows_all_ref,
    rms_ref,
    up_rows_new_ref,
    down_cols_new_ref,
    mixer_cols_new_ref,
    up_new_ref,
    up_average_new_ref,
    down_new_ref,
    down_average_new_ref,
    mixer_new_ref,
    mixer_average_new_ref,
    channel_new_ref,
    channel_average_new_ref,
    bias_new_ref,
    bias_average_new_ref,
    bias_grad_out_ref,
    bias_moment_out_ref,
    up_cols_out_ref,
    down_rows_out_ref,
    mixer_rows_out_ref,
):
    full, hidden = up_rows_ref.shape[0], 2 * bias_ref.shape[0]
    states = mixer_cols_ref.shape[0]

    def stat(row, size):
        return stat_ref[row : row + 1, :size] + got_ref[row : row + 1, :size]

    def scalar(at):
        return stat(SCALARS, 8 * LANES)[:, at * LANES : at * LANES + 1]

    def total(value):
        return jnp.sum(value, axis=1, keepdims=True)

    up_rows_new = DECAY * as_row(up_rows_ref) + FRESH * (stat(UP_ROW, full) / hidden + EPSILON_SQUARE)
    down_cols_new = DECAY * as_row(down_cols_ref) + FRESH * (stat(DOWN_COL, full) / hidden + EPSILON_SQUARE)
    mixer_cols_new = DECAY * as_row(mixer_cols_ref) + FRESH * (stat(MIXER_COL, states) / full + EPSILON_SQUARE)
    up_mean = total(up_rows_new) / full
    down_mean = scalar(1) / hidden
    mixer_mean = scalar(2) / full
    square = (
        scalar(0)
        + up_mean * total(stat(UP_MASS, full) / up_rows_new)
        + down_mean * total(stat(DOWN_MASS, full) / down_cols_new)
        + mixer_mean * total(stat(MIXER_MASS, states) / mixer_cols_new)
    )
    rms = jnp.sqrt(square / (2 * full * hidden + states * full + 5 * full + hidden))
    factor = LEARN_RATE * CLIP_LEVEL / jnp.maximum(CLIP_LEVEL, rms)

    def rate(squares, size):
        return factor * jnp.maximum(EPSILON_SCALE, jnp.sqrt(squares / size))

    def settle(weight, change, average_ref, new_ref, average_new_ref):
        new = weight - change
        new_ref[...] = new
        average_new_ref[...] = AVERAGE_KEEP * average_ref[...] + (1.0 - AVERAGE_KEEP) * new

    def column(row):
        return to_column(row)[:, 0:1]

    up_speed = rate(scalar(3), full * hidden) * jnp.sqrt(up_mean)
    settle(
        up_ref[...],
        up_grad_ref[...] * column(lax.rsqrt(up_rows_new) * up_speed) * lax.rsqrt(up_cols_new_ref[...]),
        up_average_ref,
        up_new_ref,
        up_average_new_ref,
    )
    down_speed = rate(scalar(4), full * hidden) * jnp.sqrt(down_mean)
    settle(
        down_ref[...],
        down_grad_ref[...] * column(lax.rsqrt(down_rows_new_ref[...]) * down_speed) * lax.rsqrt(down_cols_new),
        down_average_ref,
        down_new_ref,
        down_average_new_ref,
    )

    @pl.when(pl.program_id(0) == 0)
    def _():
        rms_ref[...] = rms
        to_flat(up_rows_new_ref, up_rows_new)
        to_flat(down_cols_new_ref, down_cols_new)
        to_flat(mixer_cols_new_ref, mixer_cols_new)
        to_flat(bias_grad_out_ref, bias_grad_ref[...])
        to_flat(bias_moment_out_ref, bias_moment_ref[...])
        to_flat(up_cols_out_ref, up_cols_all_ref[...])
        to_flat(down_rows_out_ref, down_rows_all_ref[...])
        to_flat(mixer_rows_out_ref, mixer_rows_new_ref[...])
        mixer_speed = rate(scalar(5), states * full) * jnp.sqrt(mixer_mean)
        settle(
            mixer_ref[...],
            mixer_grad_ref[...]
            * column(lax.rsqrt(mixer_rows_new_ref[...]) * mixer_speed)
            * lax.rsqrt(mixer_cols_new),
            mixer_average_ref,
            mixer_new_ref,
            mixer_average_new_ref,
        )
        channel_square = channel_square_ref[:, 0:1] + channel_got_ref[:, 0:1]
        settle(
            channel_ref[...],
            rate(channel_square, full) * channel_update_ref[...],
            channel_average_ref,
            channel_new_ref,
            channel_average_new_ref,
        )
        bias_new = as_row(bias_ref) - rate(scalar(6), hidden) * bias_update_ref[...]
        to_flat(bias_new_ref, bias_new)
        to_flat(
            bias_average_new_ref, AVERAGE_KEEP * as_row(bias_average_ref) + (1.0 - AVERAGE_KEEP) * bias_new
        )


def final_update(operands, units):
    up, mixer, channel, bias = operands[10], operands[16], operands[19], operands[22]
    full, hidden_local = up.shape
    up_block = pl.BlockSpec((full, units), lambda i: (0, i))
    down_block = pl.BlockSpec((units, full), lambda i: (i, 0))
    row_block = pl.BlockSpec((1, units), lambda i: (0, i))

    def whole(array):
        return pl.BlockSpec(array.shape, lambda i: (0,) * len(array.shape))

    in_specs = [whole(array) for array in operands]
    in_specs[7:9] = [row_block, row_block]
    in_specs[9:12] = [up_block] * 3
    in_specs[12:15] = [down_block] * 3
    shapes = [(1, 1), operands[4].shape, operands[5].shape, operands[6].shape]
    shapes += [up.shape] * 2 + [(hidden_local, full)] * 2 + [mixer.shape] * 2 + [channel.shape] * 2 + [bias.shape] * 2
    shapes += [bias.shape] * 4 + [operands[18].shape[1:]]
    out_specs = [whole(jax.ShapeDtypeStruct(shape, f32)) for shape in shapes]
    out_specs[4:8] = [up_block, up_block, down_block, down_block]
    return pl.pallas_call(
        update_kernel,
        grid=(hidden_local // units,),
        in_specs=in_specs,
        out_specs=out_specs,
        out_shape=[jax.ShapeDtypeStruct(shape, f32) for shape in shapes],
        compiler_params=params(),
        cost_estimate=cost(1e8, 48e6),
        name="final_update",
    )(*operands)


def turn_table():
    place = np.arange(AREA)
    swapped = (place % S) * S + place // S
    table = np.concatenate([place[:, None] == place[None, :], swapped[:, None] == place[None, :]])
    return table.astype(ml_dtypes.bfloat16)


def shards(
    pixels,
    image_sizes,
    out_grad,
    up_weight,
    down_weight,
    mixer_params,
    channel_params,
    hidden_bias,
    up_rows,
    up_cols,
    down_rows,
    down_cols,
    mixer_rows,
    mixer_cols,
    channel_moment,
    bias_moment,
    up_average,
    down_average,
    mixer_average,
    channel_average,
    bias_average,
):
    width_local, count = pixels.shape
    hidden_local = up_weight.shape[1]
    place = jnp.stack([lax.axis_index(axis) for axis in ("ch", "plane", "line")]).astype(jnp.int32)

    def exchange(value):
        return lax.ppermute(value, "ch", [(0, 1), (1, 0)])

    def row(value):
        return value.reshape(1, -1)

    other_grad = exchange(out_grad)
    rounded = jnp.concatenate(
        [channel_params[0:2].astype(bf16).astype(f32), channel_params[2:5], jnp.zeros((3, width_local), f32)]
    )
    own_cols = rounded.T
    other_cols = exchange(rounded).T
    turn = jnp.asarray(turn_table())
    taps = mixer_taps(mixer_params)
    mixed, first = mixer_forward(image_sizes, pixels, taps, channel_params, turn)
    other_mixed = exchange(mixed)
    up_low, up_turned, down_low, down_turned, square = weights_low(up_weight, down_weight)
    bias_col = hidden_bias.astype(bf16).astype(f32)[:, None]
    act, low, stat = norm_forward(
        place, image_sizes, mixed, other_mixed, out_grad, other_grad, own_cols, other_cols
    )

    sums, bias_parts = [], []
    earlier = ()
    for chunk in range(CHUNKS):
        values = feed_chunk(chunk, place, act, low, up_turned, down_low, bias_col, earlier)
        earlier = values[0:2]
        bias_parts.append(values[2][0])
        sums.append(GradientSum(values[3], values[4:]))
    hidden, slopes = earlier
    partial = []
    early, late = sums
    early.to_line()
    tokens, riders = early.sends, [early.kept, late.kept]
    for part in range(SUM_PARTS):
        values, riders = hidden_sums(
            place, hidden, slopes, down_turned, up_low, mixed, other_mixed, stat, own_cols, other_cols, part, tokens, riders
        )
        own_proj, send_proj, own_act, send_act, own_sum = values
        partial.append(((own_proj, own_act, own_sum), exchange((send_proj, send_act, own_sum))))
        if part == 0:
            early.kept, late.kept = riders
            early.gather()
            late.to_line()
            tokens, riders = [early.piece, *late.sends], [late.kept]
    (late.kept,) = riders
    by_permutes = late.kept.shape[0] % S == 0
    if by_permutes:
        late.gather_line()
    else:
        late.gather()
    carry = jnp.concatenate(
        [jnp.zeros((BIAS, width_local), f32), jnp.concatenate(bias_parts).reshape(-1, width_local)]
    )
    carry = jnp.pad(carry, ((0, -carry.shape[0] % 8), (0, 0)))
    done = ()
    tokens, riders = [late.piece], [late.piece]
    for part in range(BACK_PARTS):
        own, got = partial[part * SUM_PARTS // BACK_PARTS]
        values = backward(
            image_sizes, pixels, out_grad, mixed, first, stat, own, got, own_cols, taps, turn, carry, part, done, riders, tokens
        )
        done, carry = values[0:2], values[2]
        tokens, riders = [], []
        if part == 0 and by_permutes:
            late.pieces[0] = values[3]
            late.gather_plane()
            tokens = [late.quarter]
    block_out, pixel_grad = done

    small = SmallSum(carry)
    stats = jnp.zeros((8, 8 * LANES), f32)
    settled = ()
    for chunk, sources in enumerate(([early.sum] * 2, late.quarters if by_permutes else [late.sum] * 2)):
        values = statistics(chunk, place, sources, row(up_cols), row(down_rows), stats, settled, small.value)
        settled, stats, small.value = values[0:4], values[4], values[5]
        if chunk == 0:
            small.add()
            small.send(PLANE)
    total = small.finish()
    up_sum, down_sum, up_cols_new, down_rows_new = settled
    (
        mixer_sum,
        mixer_rows_new,
        channel_sum,
        channel_moment_new,
        channel_update,
        bias_sum,
        bias_moment_new,
        bias_update,
        stats,
        channel_square,
    ) = small_update(
        total,
        stats,
        square,
        mixer_params,
        channel_params,
        channel_moment,
        hidden_bias,
        bias_moment,
        mixer_rows,
        down_rows_new,
    )
    got_stats, got_square = exchange((stats, channel_square))
    (
        update_rms,
        up_rows_new,
        down_cols_new,
        mixer_cols_new,
        up_new,
        up_average_new,
        down_new,
        down_average_new,
        mixer_new,
        mixer_average_new,
        channel_new,
        channel_average_new,
        bias_new,
        bias_average_new,
        bias_sum,
        bias_moment_new,
        up_cols_new,
        down_rows_new,
        mixer_rows_new,
    ) = final_update(
        [
            stats,
            got_stats,
            channel_square,
            got_square,
            up_rows,
            down_cols,
            mixer_cols,
            up_cols_new,
            down_rows_new,
            up_sum,
            up_weight,
            up_average,
            down_sum,
            down_weight,
            down_average,
            mixer_sum,
            mixer_params,
            mixer_average,
            mixer_rows_new,
            channel_params,
            channel_average,
            channel_update,
            hidden_bias,
            bias_average,
            bias_update,
            bias_sum,
            bias_moment_new,
            up_cols_new,
            down_rows_new,
        ],
        256,
    )
    return (
        block_out,
        pixel_grad,
        update_rms.reshape(()),
        up_sum,
        up_rows_new,
        up_cols_new,
        up_new,
        up_average_new,
        down_sum,
        down_rows_new,
        down_cols_new,
        down_new,
        down_average_new,
        mixer_sum,
        mixer_rows_new,
        mixer_cols_new,
        mixer_new,
        mixer_average_new,
        channel_sum,
        channel_moment_new,
        channel_new,
        channel_average_new,
        bias_sum,
        bias_moment_new,
        bias_new,
        bias_average_new,
    )


def solution(mesh):
    mesh = jax.sharding.Mesh(mesh.devices.reshape(-1, PLANE, mesh.shape["ch"]), ("line", "plane", "ch"))
    images = ("line", "plane")
    split = P("ch", images)
    over_rows, over_cols, over = P("ch", None), P(None, "ch"), P("ch")
    return jax.shard_map(
        shards,
        mesh=mesh,
        in_specs=(
            split,
            P(images, None),
            split,
            over_cols,
            over_rows,
            over_rows,
            over_cols,
            over,
            P(),
            over,
            over,
            P(),
            over,
            P(),
            over_cols,
            over,
            over_cols,
            over_rows,
            over_rows,
            over_cols,
            over,
        ),
        out_specs=(
            split,
            split,
            P(),
            over_cols,
            P(),
            over,
            over_cols,
            over_cols,
            over_rows,
            over,
            P(),
            over_rows,
            over_rows,
            over_rows,
            over,
            P(),
            over_rows,
            over_rows,
            over_cols,
            over_cols,
            over_cols,
            over_cols,
            over,
            over,
            over,
            over,
        ),
        check_vma=False,
    )
```

```python
import functools

import jax
import jax.numpy as jnp
import ml_dtypes
import numpy as np
from jax import lax
from jax.experimental import pallas as pl
from jax.experimental.pallas import tpu as pltpu
from jax.sharding import PartitionSpec as P

S = 16
AREA = S * S
STEP = 10
LANES = 128

EPSILON_NORM = 1e-06
EPSILON_SQUARE = 1e-30
EPSILON_SCALE = 0.001
LEARN_RATE = 0.3
CLIP_LEVEL = 1.0
AVERAGE_KEEP = 0.9
HALF_ROOT = 0.7071067811865476
DENSITY = 0.3989422804014327
LOG2_E = 1.4426950408889634
DECAY = 1.0 - STEP ** (-0.8)
FRESH = 1.0 - DECAY
ERF_P = 0.3275911
ERF_A = (0.254829592, -0.284496736, 1.421413741, -1.453152027, 1.061405429)
CHUNKS = 2
SUM_PARTS = 2
BACK_PARTS = 4
PLANE = 4

f32 = jnp.float32
bf16 = jnp.bfloat16
NT = (((1,), (1,)), ((), ()))
TN = (((0,), (0,)), ((), ()))
NN = (((1,), (0,)), ((), ()))


def dot(left, right, dims=NN):
    return lax.dot_general(left, right, dims, preferred_element_type=f32)


def params(mib=60):
    return pltpu.CompilerParams(vmem_limit_bytes=mib * 1024 * 1024)


def cost(microseconds):
    return pl.CostEstimate(
        flops=int(microseconds * 1e9), bytes_accessed=int(microseconds * 3e6), transcendentals=0
    )


def image_mask(sizes_ref, image):
    place = lax.broadcasted_iota(jnp.int32, (1, AREA), 1)
    row, column = lax.shift_right_logical(place, 4), place & (S - 1)
    size = sizes_ref[pl.ds(image, 1), :]
    inside = (row < size[:, 0:1]) & (column < size[:, 1:2])
    return jnp.where(inside, 1.0, 0.0).astype(f32)


def spread_columns(source_ref, wide_ref):
    for row in range(wide_ref.shape[0]):
        wide_ref[row] = to_column(source_ref[row : row + 1, :])


def wide_column(wide_ref, row, span):
    return jnp.concatenate([wide_ref[row]] * (span // LANES), axis=1)


def first_power(table, half):
    base = half * 256
    rate = jnp.exp(table[base : base + 64])
    freq = table[base + 64 : base + 128]
    damp = jnp.exp(-rate)
    return (
        rate,
        damp * jnp.cos(freq),
        damp * jnp.sin(freq),
        table[base + 128 : base + 192],
        table[base + 192 : base + 256],
    )


def taps_kernel(params_ref, out_ref):
    table = params_ref[...].T
    for half in range(2):
        _, step_real, step_imag, real, imag = first_power(table, half)
        here_real, here_imag = jnp.ones_like(step_real), jnp.zeros_like(step_real)
        for place in range(S):
            tap = jnp.sum(real * here_real - imag * here_imag, axis=0, keepdims=True)
            out_ref[half, place : place + 1, :] = tap.astype(bf16).astype(f32)
            here_real, here_imag = (
                here_real * step_real - here_imag * step_imag,
                here_real * step_imag + here_imag * step_real,
            )


def mixer_taps(mixer_params):
    width = mixer_params.shape[0]
    return pl.pallas_call(
        taps_kernel,
        out_shape=jax.ShapeDtypeStruct((2, S, width), f32),
        compiler_params=params(),
        name="mixer_taps",
    )(mixer_params)


def taps_back(params_ref, grad_ref, table_ref):
    table = params_ref[...].T
    for half in range(2):
        rate, step_real, step_imag, real, imag = first_power(table, half)
        here_real, here_imag = jnp.ones_like(step_real), jnp.zeros_like(step_real)
        zero = jnp.zeros_like(step_real)
        sum_real, sum_imag, far_real, far_imag = zero, zero, zero, zero
        for place in range(S):
            grad = grad_ref[half * S + place : half * S + place + 1, :]
            wave_real, wave_imag = grad * here_real, grad * here_imag
            sum_real, sum_imag = sum_real + wave_real, sum_imag + wave_imag
            far_real, far_imag = far_real + place * wave_real, far_imag + place * wave_imag
            here_real, here_imag = (
                here_real * step_real - here_imag * step_imag,
                here_real * step_imag + here_imag * step_real,
            )
        base = half * 256
        table_ref[base : base + 64] = -rate * (real * far_real - imag * far_imag)
        table_ref[base + 64 : base + 128] = -(real * far_imag + imag * far_real)
        table_ref[base + 128 : base + 192] = sum_real
        table_ref[base + 192 : base + 256] = -sum_imag


def block_rows(place):
    return slice(place * S, (place + 1) * S)


def causal(source_ref, taps_ref, half, lanes, base=0):
    rows = [source_ref[base + place * S : base + (place + 1) * S, lanes] for place in range(S)]
    for place in range(S):
        total = rows[place] * taps_ref[half, 0:1, lanes]
        for back in range(1, place + 1):
            total += rows[place - back] * taps_ref[half, back : back + 1, lanes]
        yield total


def anticausal(source_ref, taps_ref, half, lanes):
    rows = [source_ref[block_rows(place), lanes] for place in range(S)]
    for place in range(S):
        total = rows[place] * taps_ref[half, 0:1, lanes]
        for ahead in range(1, S - place):
            total += rows[place + ahead] * taps_ref[half, ahead : ahead + 1, lanes]
        yield total


def mixer_kernel(
    sizes_ref, pixels_ref, taps_ref, channel_ref, turn_ref, mixed_ref, first_ref, cells_ref, low_ref, wide_ref, *, per_step
):
    width = pixels_ref.shape[0]
    for part in range(per_step):
        spot = slice(part * AREA, (part + 1) * AREA)
        mask = image_mask(sizes_ref, pl.program_id(0) * per_step + part)
        masked = (pixels_ref[:, spot].astype(f32) * mask).astype(bf16)
        cells, low, wide = cells_ref.at[part], low_ref.at[part], wide_ref.at[part]
        cells[...] = dot(turn_ref[...], masked, NT)
        for start in range(0, width, LANES):
            lanes = slice(start, start + LANES)
            for place, value in enumerate(causal(cells, taps_ref, 0, lanes)):
                low[block_rows(place), lanes] = value.astype(bf16)
        wide[...] = dot(turn_ref[AREA:, :], low[...])
        first_ref[spot, :] = wide[...].astype(bf16)
        for start in range(0, width, LANES):
            lanes = slice(start, start + LANES)
            skip = channel_ref[2:3, lanes]
            for place, value in enumerate(causal(wide, taps_ref, 1, lanes)):
                own = cells[AREA + place * S : AREA + (place + 1) * S, lanes]
                low[block_rows(place), lanes] = (value + skip * own).astype(bf16)
        mixed_ref[:, spot] = dot(low[...], turn_ref[AREA:, :], TN).astype(bf16)


def mixer_forward(sizes, pixels, taps, channel, turn):
    width, count = pixels.shape
    per_step = 2
    span = per_step * AREA
    in_specs = [
        pl.BlockSpec(sizes.shape, lambda i: (0, 0)),
        pl.BlockSpec((width, span), lambda i: (0, i)),
        pl.BlockSpec(taps.shape, lambda i: (0, 0, 0)),
        pl.BlockSpec(channel.shape, lambda i: (0, 0)),
        pl.BlockSpec(turn.shape, lambda i: (0, 0)),
    ]
    out_specs = [pl.BlockSpec((width, span), lambda i: (0, i)), pl.BlockSpec((span, width), lambda i: (i, 0))]
    scratch_shapes = [
        pltpu.VMEM((per_step, 2 * AREA, width), f32),
        pltpu.VMEM((per_step, AREA, width), bf16),
        pltpu.VMEM((per_step, AREA, width), f32),
    ]
    return pl.pallas_call(
        functools.partial(mixer_kernel, per_step=per_step),
        grid=(count // span,),
        in_specs=in_specs,
        out_specs=out_specs,
        scratch_shapes=scratch_shapes,
        out_shape=[
            jax.ShapeDtypeStruct((width, count), bf16),
            jax.ShapeDtypeStruct((count, width), bf16),
        ],
        compiler_params=params(),
        cost_estimate=cost(16),
        name="mixer_forward",
    )(sizes, pixels, taps, channel, turn)


def norm_kernel(
    place_ref,
    sizes_ref,
    own_ref,
    other_ref,
    own_grad_ref,
    other_grad_ref,
    own_rows_ref,
    other_rows_ref,
    act_ref,
    low_ref,
    stat_ref,
    own_wide,
    other_wide,
    *,
    per_step,
):
    width = 2.0 * own_ref.shape[0]
    mine = place_ref[0]

    @pl.when(pl.program_id(0) == 0)
    def _():
        spread_columns(own_rows_ref, own_wide)
        spread_columns(other_rows_ref, other_wide)

    for part in range(per_step):
        spot = slice(part * AREA, (part + 1) * AREA)
        mask = image_mask(sizes_ref, pl.program_id(0) * per_step + part)
        own, other = own_ref[:, spot].astype(f32), other_ref[:, spot].astype(f32)
        mean = (jnp.sum(own, axis=0, keepdims=True) + jnp.sum(other, axis=0, keepdims=True)) / width
        own, other = own - mean, other - mean
        spread = (
            jnp.sum(own * own, axis=0, keepdims=True) + jnp.sum(other * other, axis=0, keepdims=True)
        ) / width
        scale = lax.rsqrt(spread + EPSILON_NORM)
        stat_ref[0:1, spot] = mean
        stat_ref[1:2, spot] = scale
        for which, value_ref, grad_ref, wide in (
            (mine, own_ref, own_grad_ref, own_wide),
            (1 - mine, other_ref, other_grad_ref, other_wide),
        ):
            value = (value_ref[:, spot].astype(f32) - mean) * scale
            act_ref[which, :, spot] = (
                value * wide_column(wide, 0, AREA) + wide_column(wide, 1, AREA)
            ).astype(bf16)
            grad = grad_ref[:, spot].astype(f32) * mask
            low_ref[which, :, spot] = (grad * wide_column(wide, 3, AREA)).astype(bf16)


def norm_forward(place, sizes, own, other, own_grad, other_grad, own_rows, other_rows):
    width, count = own.shape
    per_step = 2
    span = per_step * AREA
    block = pl.BlockSpec((width, span), lambda i, *_: (0, i))
    rows = pl.BlockSpec(own_rows.shape, lambda i, *_: (0, 0))
    pair = pl.BlockSpec((2, width, span), lambda i, *_: (0, 0, i))
    grid_spec = pltpu.PrefetchScalarGridSpec(
        num_scalar_prefetch=1,
        grid=(count // span,),
        in_specs=[pl.BlockSpec(sizes.shape, lambda i, *_: (0, 0)), block, block, block, block, rows, rows],
        out_specs=[pair, pair, pl.BlockSpec((8, span), lambda i, *_: (0, i))],
        scratch_shapes=[pltpu.VMEM((5, width, LANES), f32)] * 2,
    )
    return pl.pallas_call(
        functools.partial(norm_kernel, per_step=per_step),
        grid_spec=grid_spec,
        out_shape=[
            jax.ShapeDtypeStruct((2, width, count), bf16),
            jax.ShapeDtypeStruct((2, width, count), bf16),
            jax.ShapeDtypeStruct((8, count), f32),
        ],
        compiler_params=params(),
        cost_estimate=cost(14),
        name="norm_forward",
    )(place, sizes, own, other, own_grad, other_grad, own_rows, other_rows)


def weights_kernel(up_ref, down_ref, up_low_ref, up_turned_ref, down_low_ref, down_turned_ref, square_ref):
    @pl.when(pl.program_id(0) == 0)
    def _():
        square_ref[...] = jnp.zeros_like(square_ref)

    for row, source_ref, low_ref, turned_ref in (
        (0, up_ref, up_low_ref, up_turned_ref),
        (1, down_ref, down_low_ref, down_turned_ref),
    ):
        value = source_ref[...]
        units = square_ref.shape[1]
        for start in range(0, value.shape[1], units):
            part = value[:, start : start + units]
            square_ref[row : row + 1, :] += jnp.sum(part * part, axis=0, keepdims=True)
        low_ref[...] = value.astype(bf16)
        turned_ref[...] = value.T.astype(bf16)


def weights_low(up, down):
    full, hidden_local = up.shape
    units = 384
    column = lambda i: (0, i)
    row = lambda i: (i, 0)
    return pl.pallas_call(
        weights_kernel,
        grid=(hidden_local // units,),
        in_specs=[pl.BlockSpec((full, units), column), pl.BlockSpec((full // 2, full), row)],
        out_specs=[
            pl.BlockSpec((full, units), column),
            pl.BlockSpec((units, full), row),
            pl.BlockSpec((units, full), row),
            pl.BlockSpec((full, units), column),
            pl.BlockSpec((8, units), lambda i: (0, 0)),
        ],
        out_shape=[
            jax.ShapeDtypeStruct((full, hidden_local), bf16),
            jax.ShapeDtypeStruct((hidden_local, full), bf16),
            jax.ShapeDtypeStruct((hidden_local, full), bf16),
            jax.ShapeDtypeStruct((full, hidden_local), bf16),
            jax.ShapeDtypeStruct((8, units), f32),
        ],
        compiler_params=params(),
        cost_estimate=cost(8),
        name="weights_low",
    )(up, down)


def gelu_pair(pre):
    bell = jnp.exp2(pre * pre * (-0.5 * LOG2_E))
    part = pl.reciprocal(1.0 + (ERF_P * HALF_ROOT) * jnp.abs(pre), approx=True)
    poly = 0.5 * ERF_A[4]
    for factor in ERF_A[3::-1]:
        poly = poly * part + 0.5 * factor
    tail = poly * part * bell
    upper = jnp.where(pre >= 0.0, 1.0 - tail, tail)
    return pre * upper, upper + pre * bell * DENSITY


def split_out(source_ref, digit, part_refs):
    rows = part_refs[0].shape[0]
    for away, ref in enumerate(part_refs):
        start = pl.multiple_of((digit ^ away) * rows, rows)
        ref[...] = source_ref[pl.ds(start, rows), :].astype(ref.dtype)


def chunk_kernel(place_ref, act_ref, low_ref, up_ref, down_ref, bias_ref, *refs):
    hidden_ref, slope_ref, bias_grad_ref = refs[-6 - PLANE : -3 - PLANE]
    part_refs, (grad_acc, bias_acc, bias_wide) = refs[-3 - PLANE : -3], refs[-3:]
    step = pl.program_id(0)

    @pl.when(step == 0)
    def _():
        grad_acc[...] = jnp.zeros_like(grad_acc)
        bias_acc[...] = jnp.zeros_like(bias_acc)
        bias_wide[...] = to_column(bias_ref[...].astype(bf16).astype(f32))

    halves, width, span = act_ref.shape
    units = up_ref.shape[0]
    full = halves * width
    tile = 256
    tiles = [(row, start) for start in range(0, span, tile) for row in range(0, units, tile)]

    def products(row, start):
        rows, spot = slice(row, row + tile), slice(start, start + tile)
        pre = dot(up_ref[rows, :], act_ref[:, :, spot].reshape(full, tile))
        pre += jnp.concatenate([bias_wide[rows, :]] * (tile // LANES), axis=1)
        return pre, dot(down_ref[rows, :], low_ref[:, :, spot].reshape(full, tile))

    ready = products(*tiles[0])
    for at, (row, start) in enumerate(tiles):
        pre, back = ready
        if at + 1 < len(tiles):
            ready = products(*tiles[at + 1])
        rows, spot = slice(row, row + tile), slice(start, start + tile)
        hidden, slope = gelu_pair(pre)
        hidden_ref[rows, spot] = hidden.astype(bf16)
        slope_ref[rows, spot] = (back * slope).astype(bf16)
    grad_acc[:units, :] += dot(slope_ref[...], act_ref[...].reshape(full, span), NT)
    grad_acc[units:, :] += dot(hidden_ref[...], low_ref[...].reshape(full, span), NT)
    bias_acc[...] += dot(jnp.ones((S, span), bf16), slope_ref[...], NT)

    @pl.when(step == pl.num_programs(0) - 1)
    def _():
        split_out(grad_acc, place_ref[1], part_refs)
        bias_grad_ref[...] = bias_acc[0:8, :]


def feed_chunk(chunk, place, act, low, up_turned, down, bias, earlier):
    halves, width, count = act.shape
    full = halves * width
    hidden_local = down.shape[0]
    units = hidden_local // CHUNKS
    span = 512
    pair = pl.BlockSpec((halves, width, span), lambda i, *_: (0, 0, i))
    weight = pl.BlockSpec((units, full), lambda i, *_: (chunk, 0))
    wide = pl.BlockSpec((units, span), lambda i, *_: (chunk, i))
    whole = lambda i, *_: (0, 0)
    rows = 2 * units // PLANE
    grid_spec = pltpu.PrefetchScalarGridSpec(
        num_scalar_prefetch=1,
        grid=(count // span,),
        in_specs=[pair, pair, weight, weight, pl.BlockSpec((1, units), lambda i, *_: (0, chunk))]
        + [pl.BlockSpec(memory_space=pl.ANY)] * len(earlier),
        out_specs=[wide, wide, pl.BlockSpec((8, units), whole)] + [pl.BlockSpec((rows, full), whole)] * PLANE,
        scratch_shapes=[pltpu.VMEM((2 * units, full), f32), pltpu.VMEM((S, units), f32), pltpu.VMEM((units, LANES), f32)],
    )
    return pl.pallas_call(
        chunk_kernel,
        grid_spec=grid_spec,
        out_shape=[
            jax.ShapeDtypeStruct((hidden_local, count), bf16),
            jax.ShapeDtypeStruct((hidden_local, count), bf16),
            jax.ShapeDtypeStruct((8, units), f32),
            jax.ShapeDtypeStruct((rows, full), f32),
        ]
        + [jax.ShapeDtypeStruct((rows, full), bf16)] * (PLANE - 1),
        input_output_aliases={6: 0, 7: 1} if earlier else {},
        compiler_params=params(),
        cost_estimate=cost(40),
        name="feed_chunk_%d" % chunk,
    )(place, act, low, up_turned, down, bias, *earlier)


def across(value, stride):
    size = lax.axis_size("line") * PLANE
    return lax.ppermute(value, ("line", "plane"), [(i, i ^ stride) for i in range(size)])


def along(value, axis, away):
    return lax.ppermute(value, axis, [(i, i ^ away) for i in range(lax.axis_size(axis))])


class GradientSum:
    def __init__(self, kept, sends):
        self.kept = kept
        self.got = [along(value, "plane", away) for away, value in enumerate(sends, 1)]

    def add(self):
        total = self.kept
        for value in self.got:
            total = total + value.astype(f32)
        return total

    def to_line(self):
        size = lax.axis_size("line")
        total = self.add()
        parts = total.reshape(size, -1, total.shape[1])

        def part(away):
            return lax.dynamic_index_in_dim(parts, lax.axis_index("line") ^ away, 0, keepdims=False)

        self.kept = part(0)
        self.sends = [part(away).astype(bf16) for away in range(1, size)]
        self.got = [along(value, "line", away) for away, value in enumerate(self.sends, 1)]

    def to_piece(self):
        self.piece = self.add().astype(bf16)

    def gather(self):
        self.to_piece()
        self.sum = lax.all_gather(self.piece, ("plane", "line"), axis=0, tiled=True)

    def gather_line(self):
        self.to_piece()
        size = lax.axis_size("line")
        self.pieces = [self.piece] + [along(self.piece, "line", away) for away in range(1, size)]

    def gather_plane(self):
        self.quarter = jnp.concatenate(self.pieces)
        self.quarters = [self.quarter] + [along(self.quarter, "plane", away) for away in range(1, PLANE)]


EXTRA = 16


def sums_kernel(
    place_ref,
    hidden_ref,
    slope_ref,
    down_ref,
    up_ref,
    own_ref,
    other_ref,
    stat_ref,
    own_rows_ref,
    other_rows_ref,
    *refs,
    skipped,
):
    own_proj_ref, own_act_ref, sum_ref, send_ref = refs[skipped : skipped + 4]
    own_wide, other_wide = refs[-2:]
    width, span = own_ref.shape
    mine = place_ref[0]
    own_rows = pl.ds(pl.multiple_of(mine * width, width), width)
    other_rows = pl.ds(pl.multiple_of((1 - mine) * width, width), width)

    @pl.when(pl.program_id(0) == 0)
    def _():
        spread_columns(own_rows_ref, own_wide)
        spread_columns(other_rows_ref, other_wide)

    own_proj_ref[...] = dot(down_ref[own_rows, :], hidden_ref[...]).astype(bf16)
    send_ref[0:width, :] = dot(down_ref[other_rows, :], hidden_ref[...]).astype(bf16)
    mean, scale = stat_ref[0:1, :], stat_ref[1:2, :]
    sums = []
    for own, rows, value_ref, wide in (
        (True, own_rows, own_ref, own_wide),
        (False, other_rows, other_ref, other_wide),
    ):
        act = dot(up_ref[rows, :], slope_ref[...])
        if own:
            own_act_ref[...] = act
        else:
            send_ref[width : 2 * width, :] = act.astype(bf16)
        act = act * wide_column(wide, 0, span)
        normed = (value_ref[...].astype(f32) - mean) * scale
        sums.append(jnp.sum(act, axis=0, keepdims=True))
        sums.append(jnp.sum(act * normed, axis=0, keepdims=True))
    plain, tilt = sums[0] + sums[2], sums[1] + sums[3]
    sum_ref[0:1, :] = plain
    sum_ref[1:2, :] = tilt
    parts = []
    for value in (plain, tilt):
        high = value.astype(bf16).astype(f32)
        parts += [high, value - high]
    parts.append(jnp.zeros((EXTRA - 4, span), f32))
    send_ref[2 * width :, :] = jnp.concatenate(parts, axis=0).astype(bf16)


def hidden_sums(place, hidden, slopes, down_turned, up, own, other, stat, own_rows, other_rows, part, tokens, riders):
    width, total = own.shape
    count = total // SUM_PARTS
    hidden_local = hidden.shape[0]
    span = 512
    base = part * (count // span)
    column = lambda i, *_: (0, base + i)
    out = lambda i, *_: (0, i)
    fixed = lambda i, *_: (0, 0)
    wide = pl.BlockSpec((hidden_local, span), column)
    block = pl.BlockSpec((width, span), column)
    result = pl.BlockSpec((width, span), out)
    rows = pl.BlockSpec(own_rows.shape, fixed)
    sent = 2 * width + EXTRA
    grid_spec = pltpu.PrefetchScalarGridSpec(
        num_scalar_prefetch=1,
        grid=(count // span,),
        in_specs=[
            wide,
            wide,
            pl.BlockSpec(down_turned.shape, fixed),
            pl.BlockSpec(up.shape, fixed),
            block,
            block,
            pl.BlockSpec((8, span), column),
            rows,
            rows,
        ]
        + [pl.BlockSpec(memory_space=pl.ANY)] * (len(riders) + len(tokens)),
        out_specs=[result, result, pl.BlockSpec((8, span), out), pl.BlockSpec((sent, span), out)]
        + [pl.BlockSpec(memory_space=pl.ANY)] * len(riders),
        scratch_shapes=[pltpu.VMEM((1, width, LANES), f32)] * 2,
    )
    values = pl.pallas_call(
        functools.partial(sums_kernel, skipped=len(riders) + len(tokens)),
        grid_spec=grid_spec,
        out_shape=[
            jax.ShapeDtypeStruct((width, count), bf16),
            jax.ShapeDtypeStruct((width, count), f32),
            jax.ShapeDtypeStruct((8, count), f32),
            jax.ShapeDtypeStruct((sent, count), bf16),
        ]
        + [jax.ShapeDtypeStruct(rider.shape, rider.dtype) for rider in riders],
        input_output_aliases={10 + at: 4 + at for at in range(len(riders))},
        compiler_params=params(),
        cost_estimate=cost(40 / SUM_PARTS * 2),
        name="hidden_sums_%d" % part,
    )(place, hidden, slopes, down_turned, up, own, other, stat, own_rows, other_rows, *riders, *tokens)
    return values[:3], values[3], values[4:]


TAPS, ROWS, BIAS = 0, 32, 40


def correlate(left_ref, right_ref, sum_ref, half, lanes):
    left = [left_ref[block_rows(place), lanes] for place in range(S)]
    right = [right_ref[block_rows(place), lanes].astype(f32) for place in range(S)]
    for back in range(S):
        total = left[back] * right[0]
        for place in range(back + 1, S):
            total += left[place] * right[place - back]
        sum_ref[half, block_rows(back), lanes] += total


def backward_kernel(
    sizes_ref,
    pixels_ref,
    grad_ref,
    mixed_ref,
    first_ref,
    stat_ref,
    own_proj_ref,
    own_act_ref,
    own_sum_ref,
    got_ref,
    rows_ref,
    taps_ref,
    turn_ref,
    carry_ref,
    *refs,
    base,
    skipped,
):
    out_ref, pixel_grad_ref, small_ref = refs[skipped : skipped + 3]
    sum_ref, channel_sum, cells_ref, low_ref, wide_ref, back_ref, columns = refs[-7:]
    step = pl.program_id(0)
    width = pixels_ref.shape[0]
    full = 2.0 * width

    @pl.when(step == 0)
    def _():
        sum_ref[...] = jnp.zeros_like(sum_ref)
        channel_sum[...] = jnp.zeros_like(channel_sum)
        spread_columns(rows_ref, columns)

    mask = image_mask(sizes_ref, base + step)
    pixels = pixels_ref[...].astype(f32)
    grad = grad_ref[...].astype(f32)
    masked = pixels * mask
    gain, skip, layer, shift = (wide_column(columns, row, AREA) for row in (0, 2, 3, 4))

    def gather(row, value):
        channel_sum[row] += value[:, :LANES] + value[:, LANES:]

    masked_grad = grad * mask
    branch = own_proj_ref[...].astype(f32) + got_ref[0:width, :].astype(f32) + shift
    out_ref[...] = pixels + mask * layer * branch
    gather(3, masked_grad * branch)
    gather(4, masked_grad)

    scale = stat_ref[1:2, :]
    normed = (mixed_ref[...].astype(f32) - stat_ref[0:1, :]) * scale
    act = own_act_ref[...] + got_ref[width : 2 * width, :].astype(f32)
    gather(0, act * normed)
    gather(1, act)
    got = got_ref[2 * width :, :].astype(f32)
    plain = (own_sum_ref[0:1, :] + (got[0:1, :] + got[1:2, :])) / full
    tilt = (own_sum_ref[1:2, :] + (got[2:3, :] + got[3:4, :])) / full
    mixed_low = (scale * (act * gain - plain - normed * tilt)).astype(bf16)
    mixed_grad = mixed_low.astype(f32)
    gather(2, mixed_grad * masked)

    cells_ref[...] = dot(turn_ref[:AREA, :], masked.astype(bf16), NT)
    wide_ref[...] = dot(turn_ref[AREA:, :], mixed_low, NT)
    for start in range(0, width, LANES):
        lanes = slice(start, start + LANES)
        for place, value in enumerate(anticausal(wide_ref, taps_ref, 1, lanes)):
            low_ref[block_rows(place), lanes] = value.astype(bf16)
        correlate(wide_ref, first_ref, sum_ref, 1, lanes)
    back_ref[...] = dot(turn_ref[AREA:, :], low_ref[...])
    for start in range(0, width, LANES):
        lanes = slice(start, start + LANES)
        for place, value in enumerate(anticausal(back_ref, taps_ref, 0, lanes)):
            wide_ref[block_rows(place), lanes] = value
        correlate(back_ref, cells_ref, sum_ref, 0, lanes)
    pixel_grad_ref[...] = grad + mask * (wide_ref[...].T + skip * mixed_grad)

    @pl.when(step == pl.num_programs(0) - 1)
    def _():
        small_ref[...] = carry_ref[...]
        for half in range(2):
            for back in range(S):
                row = TAPS + half * S + back
                small_ref[row : row + 1, :] += jnp.sum(
                    sum_ref[half, block_rows(back), :], axis=0, keepdims=True
                )
        for row in range(5):
            small_ref[ROWS + row : ROWS + row + 1, :] += jnp.sum(channel_sum[row].T, axis=0, keepdims=True)


def backward(sizes, pixels, grad, mixed, mid, stat, own, got, rows, taps, turn, carry, part, earlier, riders, tokens):
    own_proj, own_act, own_sum = own
    width, total = pixels.shape
    count = total // BACK_PARTS
    base = part * (count // AREA)
    inner = base % (own_proj.shape[1] // AREA)
    column = lambda i: (0, base + i)
    here = lambda i: (0, inner + i)
    fixed = lambda i: (0, 0)
    block = pl.BlockSpec((width, AREA), column)
    local = pl.BlockSpec((width, AREA), here)
    anywhere = pl.BlockSpec(memory_space=pl.ANY)
    in_specs = [
        pl.BlockSpec(sizes.shape, fixed),
        block,
        block,
        block,
        pl.BlockSpec((AREA, width), lambda i: (base + i, 0)),
        pl.BlockSpec((8, AREA), column),
        local,
        local,
        pl.BlockSpec((8, AREA), here),
        pl.BlockSpec((got.shape[0], AREA), here),
        pl.BlockSpec(rows.shape, fixed),
        pl.BlockSpec(taps.shape, lambda i: (0, 0, 0)),
        pl.BlockSpec(turn.shape, fixed),
        pl.BlockSpec(carry.shape, fixed),
    ]
    in_specs += [anywhere] * (len(earlier) + len(riders) + len(tokens))
    first = 14
    return pl.pallas_call(
        functools.partial(backward_kernel, base=base, skipped=len(earlier) + len(riders) + len(tokens)),
        grid=(count // AREA,),
        in_specs=in_specs,
        out_specs=[block, block, pl.BlockSpec(carry.shape, fixed)] + [anywhere] * len(riders),
        scratch_shapes=[
            pltpu.VMEM((2, AREA, width), f32),
            pltpu.VMEM((5, width, LANES), f32),
            pltpu.VMEM((AREA, width), f32),
            pltpu.VMEM((AREA, width), bf16),
            pltpu.VMEM((AREA, width), f32),
            pltpu.VMEM((AREA, width), f32),
            pltpu.VMEM((5, width, LANES), f32),
        ],
        out_shape=[
            jax.ShapeDtypeStruct((width, total), f32),
            jax.ShapeDtypeStruct((width, total), f32),
            jax.ShapeDtypeStruct(carry.shape, f32),
        ]
        + [jax.ShapeDtypeStruct(rider.shape, rider.dtype) for rider in riders],
        input_output_aliases={first + at: at for at in range(len(earlier))}
        | {first + len(earlier) + at: 3 + at for at in range(len(riders))},
        compiler_params=params(),
        cost_estimate=cost(45 / BACK_PARTS * 2),
        name="backward_%d" % part,
    )(
        sizes, pixels, grad, mixed, mid, stat, own_proj, own_act, own_sum, got, rows, taps, turn, carry, *earlier, *riders, *tokens
    )


UP_ROW, UP_MASS, DOWN_COL, DOWN_MASS, MIXER_COL, MIXER_MASS, SCALARS = range(7)


def fold(value):
    total = value[:, :LANES]
    for start in range(LANES, value.shape[1], LANES):
        total += value[:, start : start + LANES]
    return total


def as_row(ref):
    return ref[...].reshape(1, ref.shape[0])


def to_flat(ref, value):
    ref[...] = value.reshape(ref.shape[0])


def to_column(row):
    return jnp.broadcast_to(row, (LANES, row.shape[1])).T


def to_row(columns):
    return jnp.sum(columns.T, axis=0, keepdims=True)


def statistics_kernel(place_ref, *refs, quarters, skipped, line_parts):
    sources, refs = refs[:quarters], refs[quarters:]
    up_old_ref, down_old_ref, carry_ref = refs[:3]
    up_ref, down_ref, up_new_ref, down_new_ref, stat_ref = refs[3 + skipped : 8 + skipped]
    quarter_ref = refs[-1]
    step = pl.program_id(0)
    plane, line = place_ref[1], place_ref[2]
    steps = PLANE // 2

    @pl.when(step == 0)
    def _():
        stat_ref[...] = carry_ref[...]

    for kind, old_ref, new_ref, columns, mass in (
        (0, up_old_ref, up_new_ref, UP_ROW, UP_MASS),
        (1, down_old_ref, down_new_ref, DOWN_COL, DOWN_MASS),
    ):
        if quarters == 2:
            value = sources[kind][...].astype(f32)
        else:
            for away, source_ref in enumerate(sources):

                @pl.when((kind * steps + step) ^ plane == away)
                def _():
                    rows = quarter_ref.shape[0] // line_parts

                    def move(at, _):
                        target = pl.ds(pl.multiple_of(at * rows, rows), rows)
                        source = pl.ds(pl.multiple_of((at ^ line) * rows, rows), rows)
                        quarter_ref[target, :] = source_ref[source, :].astype(f32)
                        return 0

                    lax.fori_loop(0, line_parts, move, 0)

            value = quarter_ref[...]
        if kind == 0:
            up_ref[...] = value.T
        else:
            down_ref[...] = value
        square = value * value
        mean = jnp.sum(fold(square), axis=1, keepdims=True) / value.shape[1]
        fresh = DECAY * to_column(old_ref[...]) + FRESH * (mean + EPSILON_SQUARE)
        new_ref[...] = fresh.T[0:1, :]
        stat_ref[columns : columns + 1, : value.shape[1]] += jnp.sum(square, axis=0, keepdims=True)
        stat_ref[mass : mass + 1, : value.shape[1]] += jnp.sum(
            square * (1.0 / fresh[:, 0:1]), axis=0, keepdims=True
        )


def statistics(chunk, place, sources, up_cols, down_rows, carry, earlier, rider):
    hidden_local = up_cols.shape[1]
    units = hidden_local // CHUNKS
    full = sources[0].shape[1]
    rows = 2 * units // PLANE
    steps = PLANE // 2
    base = chunk * steps
    row = pl.BlockSpec((1, rows), lambda i: (0, base + i))
    anywhere = pl.BlockSpec(memory_space=pl.ANY)
    fixed = pl.BlockSpec(carry.shape, lambda i: (0, 0))
    if len(sources) == 2:
        specs = [
            pl.BlockSpec((rows, full), lambda i: (i, 0)),
            pl.BlockSpec((rows, full), lambda i: (steps + i, 0)),
        ]
    else:
        specs = [pl.BlockSpec((rows, full), lambda i: (0, 0))] * PLANE
    first = 4 + len(sources)
    return pl.pallas_call(
        functools.partial(statistics_kernel, quarters=len(sources), skipped=len(earlier) + 1, line_parts=lax.axis_size("line")),
        grid=(steps,),
        in_specs=[pl.BlockSpec(memory_space=pltpu.SMEM)]
        + specs
        + [row, row, fixed]
        + [anywhere] * (len(earlier) + 1),
        out_specs=[
            pl.BlockSpec((full, rows), lambda i: (0, base + i)),
            pl.BlockSpec((rows, full), lambda i: (base + i, 0)),
            row,
            row,
            fixed,
            anywhere,
        ],
        out_shape=[
            jax.ShapeDtypeStruct((full, hidden_local), f32),
            jax.ShapeDtypeStruct((hidden_local, full), f32),
            jax.ShapeDtypeStruct((1, hidden_local), f32),
            jax.ShapeDtypeStruct((1, hidden_local), f32),
            jax.ShapeDtypeStruct(carry.shape, f32),
            jax.ShapeDtypeStruct(rider.shape, rider.dtype),
        ],
        input_output_aliases={first + at: at for at in range(len(earlier))} | {first + len(earlier): 5},
        scratch_shapes=[pltpu.VMEM((rows, full), f32)],
        compiler_params=params(),
        cost_estimate=cost(1),
        name="statistics_%d" % chunk,
    )(place, *sources, up_cols, down_rows, carry, *earlier, rider)


def small_kernel(
    sum_ref,
    stat_ref,
    square_ref,
    params_ref,
    channel_ref,
    moment_ref,
    bias_ref,
    bias_moment_ref,
    rows_ref,
    down_rows_new_ref,
    mixer_grad_ref,
    rows_new_ref,
    channel_grad_ref,
    moment_new_ref,
    channel_update_ref,
    bias_grad_ref,
    bias_moment_new_ref,
    bias_update_ref,
    out_ref,
    channel_square_ref,
    table_ref,
):
    out_ref[...] = stat_ref[...]
    taps_back(params_ref, sum_ref, table_ref)
    grad = table_ref[...].T
    mixer_grad_ref[...] = grad
    states = grad.shape[1]
    square = grad * grad
    mean = jnp.sum(fold(square), axis=1, keepdims=True) / states
    fresh = DECAY * to_column(as_row(rows_ref)) + FRESH * (mean + EPSILON_SQUARE)
    rows_new = fresh.T[0:1, :]
    rows_new_ref[...] = rows_new
    out_ref[MIXER_COL : MIXER_COL + 1, :states] = jnp.sum(square, axis=0, keepdims=True)
    out_ref[MIXER_MASS : MIXER_MASS + 1, :states] = jnp.sum(square * (1.0 / fresh[:, 0:1]), axis=0, keepdims=True)

    layer = channel_ref[3:4, :]
    channel_grad_ref[0:4, :] = sum_ref[ROWS : ROWS + 4, :]
    channel_grad_ref[4:5, :] = sum_ref[ROWS + 4 : ROWS + 5, :] * layer
    grad = channel_grad_ref[...]
    moment = DECAY * moment_ref[...] + FRESH * (grad * grad + EPSILON_SQUARE)
    moment_new_ref[...] = moment
    channel_update = grad * lax.rsqrt(moment)
    channel_update_ref[...] = channel_update

    width = layer.shape[1]
    for at in range(bias_grad_ref.shape[1] // width):
        bias_grad_ref[:, at * width : (at + 1) * width] = sum_ref[BIAS + at : BIAS + at + 1, :]
    grad = bias_grad_ref[...]
    moment = DECAY * as_row(bias_moment_ref) + FRESH * (grad * grad + EPSILON_SQUARE)
    bias_moment_new_ref[...] = moment
    bias_update = grad * lax.rsqrt(moment)
    bias_update_ref[...] = bias_update

    def total(value):
        return jnp.sum(value, keepdims=True)

    channel = channel_ref[...]
    table = params_ref[...]
    bias = as_row(bias_ref)
    scalars = (
        total(channel_update * channel_update) + total(bias_update * bias_update),
        total(down_rows_new_ref[...]),
        total(rows_new),
        total(square_ref[0:1, :]),
        total(square_ref[1:2, :]),
        total(table * table),
        total(bias * bias),
    )
    for at, value in enumerate(scalars):
        out_ref[SCALARS : SCALARS + 1, at * LANES : (at + 1) * LANES] = jnp.broadcast_to(value, (1, LANES))
    channel_square_ref[...] = jnp.broadcast_to(jnp.sum(channel * channel, axis=1, keepdims=True), (5, LANES))


def small_update(total, stat, square, mixer_params, channel_params, channel_moment, bias, bias_moment, rows, down_rows_new):
    width, states = mixer_params.shape
    shapes = [
        (width, states),
        (1, width),
        channel_params.shape,
        channel_params.shape,
        channel_params.shape,
        (1, bias.shape[0]),
        (1, bias.shape[0]),
        (1, bias.shape[0]),
        (8, 8 * LANES),
        (5, LANES),
    ]
    return pl.pallas_call(
        small_kernel,
        out_shape=[jax.ShapeDtypeStruct(shape, f32) for shape in shapes],
        scratch_shapes=[pltpu.VMEM((states, width), f32)],
        compiler_params=params(),
        cost_estimate=cost(5),
        name="small_update",
    )(total, stat, square, mixer_params, channel_params, channel_moment, bias, bias_moment, rows, down_rows_new)


def update_kernel(
    stat_ref,
    got_ref,
    channel_square_ref,
    channel_got_ref,
    up_rows_ref,
    down_cols_ref,
    mixer_cols_ref,
    up_cols_new_ref,
    down_rows_new_ref,
    up_grad_ref,
    up_ref,
    up_average_ref,
    down_grad_ref,
    down_ref,
    down_average_ref,
    mixer_grad_ref,
    mixer_ref,
    mixer_average_ref,
    mixer_rows_new_ref,
    channel_ref,
    channel_average_ref,
    channel_update_ref,
    bias_ref,
    bias_average_ref,
    bias_update_ref,
    bias_grad_ref,
    bias_moment_ref,
    up_cols_all_ref,
    down_rows_all_ref,
    rms_ref,
    up_rows_new_ref,
    down_cols_new_ref,
    mixer_cols_new_ref,
    up_new_ref,
    up_average_new_ref,
    down_new_ref,
    down_average_new_ref,
    mixer_new_ref,
    mixer_average_new_ref,
    channel_new_ref,
    channel_average_new_ref,
    bias_new_ref,
    bias_average_new_ref,
    bias_grad_out_ref,
    bias_moment_out_ref,
    up_cols_out_ref,
    down_rows_out_ref,
    mixer_rows_out_ref,
):
    full, hidden = up_rows_ref.shape[0], 2 * bias_ref.shape[0]
    states = mixer_cols_ref.shape[0]

    def stat(row, size):
        return stat_ref[row : row + 1, :size] + got_ref[row : row + 1, :size]

    def scalar(at):
        return stat(SCALARS, 8 * LANES)[:, at * LANES : at * LANES + 1]

    def total(value):
        return jnp.sum(value, axis=1, keepdims=True)

    up_rows_new = DECAY * as_row(up_rows_ref) + FRESH * (stat(UP_ROW, full) / hidden + EPSILON_SQUARE)
    down_cols_new = DECAY * as_row(down_cols_ref) + FRESH * (stat(DOWN_COL, full) / hidden + EPSILON_SQUARE)
    mixer_cols_new = DECAY * as_row(mixer_cols_ref) + FRESH * (stat(MIXER_COL, states) / full + EPSILON_SQUARE)
    up_mean = total(up_rows_new) / full
    down_mean = scalar(1) / hidden
    mixer_mean = scalar(2) / full
    square = (
        scalar(0)
        + up_mean * total(stat(UP_MASS, full) / up_rows_new)
        + down_mean * total(stat(DOWN_MASS, full) / down_cols_new)
        + mixer_mean * total(stat(MIXER_MASS, states) / mixer_cols_new)
    )
    rms = jnp.sqrt(square / (2 * full * hidden + states * full + 5 * full + hidden))
    factor = LEARN_RATE * CLIP_LEVEL / jnp.maximum(CLIP_LEVEL, rms)

    def rate(squares, size):
        return factor * jnp.maximum(EPSILON_SCALE, jnp.sqrt(squares / size))

    def settle(weight, change, average_ref, new_ref, average_new_ref):
        new = weight - change
        new_ref[...] = new
        average_new_ref[...] = AVERAGE_KEEP * average_ref[...] + (1.0 - AVERAGE_KEEP) * new

    def column(row):
        return to_column(row)[:, 0:1]

    up_speed = rate(scalar(3), full * hidden) * jnp.sqrt(up_mean)
    settle(
        up_ref[...],
        up_grad_ref[...] * column(lax.rsqrt(up_rows_new) * up_speed) * lax.rsqrt(up_cols_new_ref[...]),
        up_average_ref,
        up_new_ref,
        up_average_new_ref,
    )
    down_speed = rate(scalar(4), full * hidden) * jnp.sqrt(down_mean)
    settle(
        down_ref[...],
        down_grad_ref[...] * column(lax.rsqrt(down_rows_new_ref[...]) * down_speed) * lax.rsqrt(down_cols_new),
        down_average_ref,
        down_new_ref,
        down_average_new_ref,
    )

    @pl.when(pl.program_id(0) == 0)
    def _():
        rms_ref[...] = rms
        to_flat(up_rows_new_ref, up_rows_new)
        to_flat(down_cols_new_ref, down_cols_new)
        to_flat(mixer_cols_new_ref, mixer_cols_new)
        to_flat(bias_grad_out_ref, bias_grad_ref[...])
        to_flat(bias_moment_out_ref, bias_moment_ref[...])
        to_flat(up_cols_out_ref, up_cols_all_ref[...])
        to_flat(down_rows_out_ref, down_rows_all_ref[...])
        to_flat(mixer_rows_out_ref, mixer_rows_new_ref[...])
        mixer_speed = rate(scalar(5), states * full) * jnp.sqrt(mixer_mean)
        settle(
            mixer_ref[...],
            mixer_grad_ref[...]
            * column(lax.rsqrt(mixer_rows_new_ref[...]) * mixer_speed)
            * lax.rsqrt(mixer_cols_new),
            mixer_average_ref,
            mixer_new_ref,
            mixer_average_new_ref,
        )
        channel_square = channel_square_ref[:, 0:1] + channel_got_ref[:, 0:1]
        settle(
            channel_ref[...],
            rate(channel_square, full) * channel_update_ref[...],
            channel_average_ref,
            channel_new_ref,
            channel_average_new_ref,
        )
        bias_new = as_row(bias_ref) - rate(scalar(6), hidden) * bias_update_ref[...]
        to_flat(bias_new_ref, bias_new)
        to_flat(
            bias_average_new_ref, AVERAGE_KEEP * as_row(bias_average_ref) + (1.0 - AVERAGE_KEEP) * bias_new
        )


def final_update(operands, units):
    up, mixer, channel, bias = operands[10], operands[16], operands[19], operands[22]
    full, hidden_local = up.shape
    up_block = pl.BlockSpec((full, units), lambda i: (0, i))
    down_block = pl.BlockSpec((units, full), lambda i: (i, 0))
    row_block = pl.BlockSpec((1, units), lambda i: (0, i))

    def whole(array):
        return pl.BlockSpec(array.shape, lambda i: (0,) * len(array.shape))

    in_specs = [whole(array) for array in operands]
    in_specs[7:9] = [row_block, row_block]
    in_specs[9:12] = [up_block] * 3
    in_specs[12:15] = [down_block] * 3
    shapes = [(1, 1), operands[4].shape, operands[5].shape, operands[6].shape]
    shapes += [up.shape] * 2 + [(hidden_local, full)] * 2 + [mixer.shape] * 2 + [channel.shape] * 2 + [bias.shape] * 2
    shapes += [bias.shape] * 4 + [operands[18].shape[1:]]
    out_specs = [whole(jax.ShapeDtypeStruct(shape, f32)) for shape in shapes]
    out_specs[4:8] = [up_block, up_block, down_block, down_block]
    return pl.pallas_call(
        update_kernel,
        grid=(hidden_local // units,),
        in_specs=in_specs,
        out_specs=out_specs,
        out_shape=[jax.ShapeDtypeStruct(shape, f32) for shape in shapes],
        compiler_params=params(),
        cost_estimate=cost(19),
        name="final_update",
    )(*operands)


def turn_table():
    place = np.arange(AREA)
    swapped = (place % S) * S + place // S
    table = np.concatenate([place[:, None] == place[None, :], swapped[:, None] == place[None, :]])
    return table.astype(ml_dtypes.bfloat16)


def shards(
    pixels,
    image_sizes,
    out_grad,
    up_weight,
    down_weight,
    mixer_params,
    channel_params,
    hidden_bias,
    up_rows,
    up_cols,
    down_rows,
    down_cols,
    mixer_rows,
    mixer_cols,
    channel_moment,
    bias_moment,
    up_average,
    down_average,
    mixer_average,
    channel_average,
    bias_average,
):
    width_local, count = pixels.shape
    hidden_local = up_weight.shape[1]
    place = jnp.stack([lax.axis_index(axis) for axis in ("ch", "plane", "line")]).astype(jnp.int32)

    def exchange(value):
        return lax.ppermute(value, "ch", [(0, 1), (1, 0)])

    def row(value):
        return value.reshape(1, -1)

    other_grad = exchange(out_grad)
    rounded = jnp.concatenate(
        [channel_params[0:2].astype(bf16).astype(f32), channel_params[2:5], jnp.zeros((3, width_local), f32)]
    )
    others = exchange(rounded)
    turn = jnp.asarray(turn_table())
    taps = mixer_taps(mixer_params)
    mixed, first = mixer_forward(image_sizes, pixels, taps, channel_params, turn)
    other_mixed = exchange(mixed)
    up_low, up_turned, down_low, down_turned, square = weights_low(up_weight, down_weight)
    act, low, stat = norm_forward(
        place, image_sizes, mixed, other_mixed, out_grad, other_grad, rounded, others
    )

    sums, bias_parts = [], []
    earlier = ()
    for chunk in range(CHUNKS):
        values = feed_chunk(chunk, place, act, low, up_turned, down_low, row(hidden_bias), earlier)
        earlier = values[0:2]
        bias_parts.append(values[2][0])
        sums.append(GradientSum(values[3], values[4:]))
    hidden, slopes = earlier
    partial = []
    early, late = sums
    early.to_line()
    tokens, riders = early.sends, [early.kept, late.kept]
    for part in range(SUM_PARTS):
        own, send, riders = hidden_sums(
            place, hidden, slopes, down_turned, up_low, mixed, other_mixed, stat, rounded, others, part, tokens, riders
        )
        if part == 0:
            early.kept, late.kept = riders
            early.gather()
            tokens, riders = [early.piece], [late.kept]
        partial.append((own, exchange(send)))
    carry = jnp.concatenate(
        [jnp.zeros((BIAS, width_local), f32), jnp.concatenate(bias_parts).reshape(-1, width_local)]
    )
    carry = jnp.pad(carry, ((0, -carry.shape[0] % 8), (0, 0)))
    done = ()
    tokens = []
    for part in range(BACK_PARTS):
        own, got = partial[part * SUM_PARTS // BACK_PARTS]
        values = backward(
            image_sizes, pixels, out_grad, mixed, first, stat, own, got, rounded, taps, turn, carry, part, done, riders, tokens
        )
        done, carry = values[0:2], values[2]
        tokens, riders = [], []
        if part == 0:
            (late.kept,) = values[3:]
            late.to_line()
            by_permutes = late.kept.shape[0] % S == 0
            tokens, riders = late.sends, [late.kept]
        elif part == 1:
            (late.kept,) = values[3:]
            if by_permutes:
                late.gather_line()
                tokens, riders = [late.piece], [late.piece]
            else:
                late.gather()
        elif part == 2 and by_permutes:
            late.pieces[0] = values[3]
            late.gather_plane()
            tokens = [late.quarter]
    block_out, pixel_grad = done

    total, stride = carry, 1
    stats = jnp.zeros((8, 8 * LANES), f32)
    settled = ()
    for chunk, sources in enumerate(([early.sum] * 2, late.quarters if by_permutes else [late.sum] * 2)):
        there = across(total, stride)
        values = statistics(chunk, place, sources, row(up_cols), row(down_rows), stats, settled, total)
        settled, stats = values[0:4], values[4]
        total, stride = values[5] + there, 2 * stride
        if chunk == 0:
            total, stride = total + across(total, stride), 2 * stride
    while stride < lax.axis_size("line") * PLANE:
        total, stride = total + across(total, stride), 2 * stride
    up_sum, down_sum, up_cols_new, down_rows_new = settled
    (
        mixer_sum,
        mixer_rows_new,
        channel_sum,
        channel_moment_new,
        channel_update,
        bias_sum,
        bias_moment_new,
        bias_update,
        stats,
        channel_square,
    ) = small_update(
        total,
        stats,
        square,
        mixer_params,
        channel_params,
        channel_moment,
        hidden_bias,
        bias_moment,
        mixer_rows,
        down_rows_new,
    )
    got_stats, got_square = exchange((stats, channel_square))
    (
        update_rms,
        up_rows_new,
        down_cols_new,
        mixer_cols_new,
        up_new,
        up_average_new,
        down_new,
        down_average_new,
        mixer_new,
        mixer_average_new,
        channel_new,
        channel_average_new,
        bias_new,
        bias_average_new,
        bias_sum,
        bias_moment_new,
        up_cols_new,
        down_rows_new,
        mixer_rows_new,
    ) = final_update(
        [
            stats,
            got_stats,
            channel_square,
            got_square,
            up_rows,
            down_cols,
            mixer_cols,
            up_cols_new,
            down_rows_new,
            up_sum,
            up_weight,
            up_average,
            down_sum,
            down_weight,
            down_average,
            mixer_sum,
            mixer_params,
            mixer_average,
            mixer_rows_new,
            channel_params,
            channel_average,
            channel_update,
            hidden_bias,
            bias_average,
            bias_update,
            bias_sum,
            bias_moment_new,
            up_cols_new,
            down_rows_new,
        ],
        256,
    )
    return (
        block_out,
        pixel_grad,
        update_rms.reshape(()),
        up_sum,
        up_rows_new,
        up_cols_new,
        up_new,
        up_average_new,
        down_sum,
        down_rows_new,
        down_cols_new,
        down_new,
        down_average_new,
        mixer_sum,
        mixer_rows_new,
        mixer_cols_new,
        mixer_new,
        mixer_average_new,
        channel_sum,
        channel_moment_new,
        channel_new,
        channel_average_new,
        bias_sum,
        bias_moment_new,
        bias_new,
        bias_average_new,
    )


def solution(mesh):
    mesh = jax.sharding.Mesh(mesh.devices.reshape(-1, PLANE, mesh.shape["ch"]), ("line", "plane", "ch"))
    images = ("line", "plane")
    split = P("ch", images)
    over_rows, over_cols, over = P("ch", None), P(None, "ch"), P("ch")
    return jax.shard_map(
        shards,
        mesh=mesh,
        in_specs=(
            split,
            P(images, None),
            split,
            over_cols,
            over_rows,
            over_rows,
            over_cols,
            over,
            P(),
            over,
            over,
            P(),
            over,
            P(),
            over_cols,
            over,
            over_cols,
            over_rows,
            over_rows,
            over_cols,
            over,
        ),
        out_specs=(
            split,
            split,
            P(),
            over_cols,
            P(),
            over,
            over_cols,
            over_cols,
            over_rows,
            over,
            P(),
            over_rows,
            over_rows,
            over_rows,
            over,
            P(),
            over_rows,
            over_rows,
            over_cols,
            over_cols,
            over_cols,
            over_cols,
            over,
            over,
            over,
            over,
        ),
        check_vma=False,
    )
```

```python
import functools

import jax
import jax.numpy as jnp
import ml_dtypes
import numpy as np
from jax import lax
from jax.experimental import pallas as pl
from jax.experimental.pallas import tpu as pltpu
from jax.sharding import PartitionSpec as P

S = 16
AREA = S * S
STEP = 10
LANES = 128

EPSILON_NORM = 1e-06
EPSILON_SQUARE = 1e-30
EPSILON_SCALE = 0.001
LEARN_RATE = 0.3
CLIP_LEVEL = 1.0
AVERAGE_KEEP = 0.9
HALF_ROOT = 0.7071067811865476
DENSITY = 0.3989422804014327
LOG2_E = 1.4426950408889634
DECAY = 1.0 - STEP ** (-0.8)
FRESH = 1.0 - DECAY
ERF_P = 0.3275911
ERF_A = (0.254829592, -0.284496736, 1.421413741, -1.453152027, 1.061405429)
CHUNKS = 2
SUM_PARTS = 2
BACK_PARTS = 4
PLANE = 4

f32 = jnp.float32
bf16 = jnp.bfloat16
NT = (((1,), (1,)), ((), ()))
TN = (((0,), (0,)), ((), ()))
NN = (((1,), (0,)), ((), ()))


def dot(left, right, dims=NN):
    return lax.dot_general(left, right, dims, preferred_element_type=f32)


def params(mib=60):
    return pltpu.CompilerParams(vmem_limit_bytes=mib * 1024 * 1024)


def cost(microseconds):
    return pl.CostEstimate(
        flops=int(microseconds * 1e9), bytes_accessed=int(microseconds * 3e6), transcendentals=0
    )


def image_mask(sizes_ref, image):
    place = lax.broadcasted_iota(jnp.int32, (1, AREA), 1)
    row, column = lax.shift_right_logical(place, 4), place & (S - 1)
    sizes = sizes_ref[...].astype(f32)
    here = lax.broadcasted_iota(jnp.int32, sizes.shape, 1) == image
    size = jnp.sum(jnp.where(here, sizes, 0.0), axis=1, keepdims=True)
    inside = (row.astype(f32) < size[0:1, :]) & (column.astype(f32) < size[1:2, :])
    return jnp.where(inside, 1.0, 0.0).astype(f32)


def wide_column(wide_ref, row, span):
    return jnp.concatenate([wide_ref[row]] * (span // LANES), axis=1)


def first_power(table, half):
    base = half * 256
    rate = jnp.exp(table[base : base + 64])
    freq = table[base + 64 : base + 128]
    damp = jnp.exp(-rate)
    return (
        rate,
        damp * jnp.cos(freq),
        damp * jnp.sin(freq),
        table[base + 128 : base + 192],
        table[base + 192 : base + 256],
    )


def make_taps(params_ref, out_ref):
    table = params_ref[...].T
    for half in range(2):
        _, step_real, step_imag, real, imag = first_power(table, half)
        here_real, here_imag = jnp.ones_like(step_real), jnp.zeros_like(step_real)
        for place in range(S):
            tap = jnp.sum(real * here_real - imag * here_imag, axis=0, keepdims=True)
            out_ref[half, place : place + 1, :] = tap.astype(bf16).astype(f32)
            here_real, here_imag = (
                here_real * step_real - here_imag * step_imag,
                here_real * step_imag + here_imag * step_real,
            )


def taps_back(params_ref, grad_ref, table_ref):
    table = params_ref[...].T
    for half in range(2):
        rate, step_real, step_imag, real, imag = first_power(table, half)
        here_real, here_imag = jnp.ones_like(step_real), jnp.zeros_like(step_real)
        zero = jnp.zeros_like(step_real)
        sum_real, sum_imag, far_real, far_imag = zero, zero, zero, zero
        for place in range(S):
            grad = grad_ref[half * S + place : half * S + place + 1, :]
            wave_real, wave_imag = grad * here_real, grad * here_imag
            sum_real, sum_imag = sum_real + wave_real, sum_imag + wave_imag
            far_real, far_imag = far_real + place * wave_real, far_imag + place * wave_imag
            here_real, here_imag = (
                here_real * step_real - here_imag * step_imag,
                here_real * step_imag + here_imag * step_real,
            )
        base = half * 256
        table_ref[base : base + 64] = -rate * (real * far_real - imag * far_imag)
        table_ref[base + 64 : base + 128] = -(real * far_imag + imag * far_real)
        table_ref[base + 128 : base + 192] = sum_real
        table_ref[base + 192 : base + 256] = -sum_imag


def block_rows(place):
    return slice(place * S, (place + 1) * S)


def causal(source_ref, taps_ref, half, lanes, base=0):
    rows = [source_ref[base + place * S : base + (place + 1) * S, lanes] for place in range(S)]
    for place in range(S):
        total = rows[place] * taps_ref[half, 0:1, lanes]
        for back in range(1, place + 1):
            total += rows[place - back] * taps_ref[half, back : back + 1, lanes]
        yield total


def anticausal(source_ref, taps_ref, half, lanes):
    rows = [source_ref[block_rows(place), lanes] for place in range(S)]
    for place in range(S):
        total = rows[place] * taps_ref[half, 0:1, lanes]
        for ahead in range(1, S - place):
            total += rows[place + ahead] * taps_ref[half, ahead : ahead + 1, lanes]
        yield total


def mixer_kernel(
    sizes_ref, pixels_ref, params_ref, channel_ref, turn_ref, mixed_ref, first_ref, taps_ref, cells_ref, low_ref, wide_ref, *, per_step
):
    @pl.when(pl.program_id(0) == 0)
    def _():
        make_taps(params_ref, taps_ref)

    width = pixels_ref.shape[0]
    for part in range(per_step):
        spot = slice(part * AREA, (part + 1) * AREA)
        mask = image_mask(sizes_ref, pl.program_id(0) * per_step + part)
        masked = (pixels_ref[:, spot].astype(f32) * mask).astype(bf16)
        cells, low, wide = cells_ref.at[part], low_ref.at[part], wide_ref.at[part]
        cells[...] = dot(turn_ref[...], masked, NT)
        for start in range(0, width, LANES):
            lanes = slice(start, start + LANES)
            for place, value in enumerate(causal(cells, taps_ref, 0, lanes)):
                low[block_rows(place), lanes] = value.astype(bf16)
        wide[...] = dot(turn_ref[AREA:, :], low[...])
        first_ref[spot, :] = wide[...].astype(bf16)
        for start in range(0, width, LANES):
            lanes = slice(start, start + LANES)
            skip = channel_ref[2:3, lanes]
            for place, value in enumerate(causal(wide, taps_ref, 1, lanes)):
                own = cells[AREA + place * S : AREA + (place + 1) * S, lanes]
                low[block_rows(place), lanes] = (value + skip * own).astype(bf16)
        mixed_ref[:, spot] = dot(low[...], turn_ref[AREA:, :], TN).astype(bf16)


def mixer_forward(sizes, pixels, mixer_params, channel, turn):
    width, count = pixels.shape
    per_step = 2
    span = per_step * AREA
    in_specs = [
        pl.BlockSpec(sizes.shape, lambda i: (0, 0)),
        pl.BlockSpec((width, span), lambda i: (0, i)),
        pl.BlockSpec(mixer_params.shape, lambda i: (0, 0)),
        pl.BlockSpec(channel.shape, lambda i: (0, 0)),
        pl.BlockSpec(turn.shape, lambda i: (0, 0)),
    ]
    out_specs = [
        pl.BlockSpec((width, span), lambda i: (0, i)),
        pl.BlockSpec((span, width), lambda i: (i, 0)),
        pl.BlockSpec((2, S, width), lambda i: (0, 0, 0)),
    ]
    scratch_shapes = [
        pltpu.VMEM((per_step, 2 * AREA, width), f32),
        pltpu.VMEM((per_step, AREA, width), bf16),
        pltpu.VMEM((per_step, AREA, width), f32),
    ]
    return pl.pallas_call(
        functools.partial(mixer_kernel, per_step=per_step),
        grid=(count // span,),
        in_specs=in_specs,
        out_specs=out_specs,
        scratch_shapes=scratch_shapes,
        out_shape=[
            jax.ShapeDtypeStruct((width, count), bf16),
            jax.ShapeDtypeStruct((count, width), bf16),
            jax.ShapeDtypeStruct((2, S, width), f32),
        ],
        compiler_params=params(),
        cost_estimate=cost(16),
        name="mixer_forward",
    )(sizes, pixels, mixer_params, channel, turn)


GAIN, SHIFT, LAYER = 0, 1, 3


def normalize(
    step,
    place_ref,
    sizes_ref,
    own_ref,
    other_ref,
    own_grad_ref,
    other_grad_ref,
    own_rows_ref,
    other_rows_ref,
    act_ref,
    low_ref,
    stat_ref,
    own_wide,
    other_wide,
):
    width, span = own_ref.shape
    width = 2.0 * width
    mine = place_ref[0]

    @pl.when(step == 0)
    def _():
        for at, row in enumerate((GAIN, SHIFT, LAYER)):
            own_wide[at] = to_column(own_rows_ref[row : row + 1, :])
            other_wide[at] = to_column(other_rows_ref[row : row + 1, :])

    for part in range(span // AREA):
        spot = slice(part * AREA, (part + 1) * AREA)
        mask = image_mask(sizes_ref, step * (span // AREA) + part)
        own, other = own_ref[:, spot].astype(f32), other_ref[:, spot].astype(f32)
        mean = (jnp.sum(own, axis=0, keepdims=True) + jnp.sum(other, axis=0, keepdims=True)) / width
        own, other = own - mean, other - mean
        spread = (
            jnp.sum(own * own, axis=0, keepdims=True) + jnp.sum(other * other, axis=0, keepdims=True)
        ) / width
        scale = lax.rsqrt(spread + EPSILON_NORM)
        stat_ref[0:1, spot] = mean
        stat_ref[1:2, spot] = scale
        for which, value_ref, grad_ref, wide in (
            (mine, own_ref, own_grad_ref, own_wide),
            (1 - mine, other_ref, other_grad_ref, other_wide),
        ):
            value = (value_ref[:, spot].astype(f32) - mean) * scale
            act_ref[which, :, spot] = (
                value * wide_column(wide, 0, AREA) + wide_column(wide, 1, AREA)
            ).astype(bf16)
            grad = grad_ref[:, spot].astype(f32) * mask
            low_ref[which, :, spot] = (grad * wide_column(wide, 2, AREA)).astype(bf16)


def weights_kernel(up_ref, down_ref, up_low_ref, up_turned_ref, down_low_ref, down_turned_ref, square_ref):
    @pl.when(pl.program_id(0) == 0)
    def _():
        square_ref[...] = jnp.zeros_like(square_ref)

    for row, source_ref, low_ref, turned_ref in (
        (0, up_ref, up_low_ref, up_turned_ref),
        (1, down_ref, down_low_ref, down_turned_ref),
    ):
        value = source_ref[...]
        units = square_ref.shape[1]
        for start in range(0, value.shape[1], units):
            part = value[:, start : start + units]
            square_ref[row : row + 1, :] += jnp.sum(part * part, axis=0, keepdims=True)
        low_ref[...] = value.astype(bf16)
        turned_ref[...] = value.T.astype(bf16)


def weights_low(up, down):
    full, hidden_local = up.shape
    units = 384
    column = lambda i: (0, i)
    row = lambda i: (i, 0)
    return pl.pallas_call(
        weights_kernel,
        grid=(hidden_local // units,),
        in_specs=[pl.BlockSpec((full, units), column), pl.BlockSpec((full // 2, full), row)],
        out_specs=[
            pl.BlockSpec((full, units), column),
            pl.BlockSpec((units, full), row),
            pl.BlockSpec((units, full), row),
            pl.BlockSpec((full, units), column),
            pl.BlockSpec((8, units), lambda i: (0, 0)),
        ],
        out_shape=[
            jax.ShapeDtypeStruct((full, hidden_local), bf16),
            jax.ShapeDtypeStruct((hidden_local, full), bf16),
            jax.ShapeDtypeStruct((hidden_local, full), bf16),
            jax.ShapeDtypeStruct((full, hidden_local), bf16),
            jax.ShapeDtypeStruct((8, units), f32),
        ],
        compiler_params=params(),
        cost_estimate=cost(8),
        name="weights_low",
    )(up, down)


def gelu_pair(pre):
    bell = jnp.exp2(pre * pre * (-0.5 * LOG2_E))
    part = pl.reciprocal(1.0 + (ERF_P * HALF_ROOT) * jnp.abs(pre), approx=True)
    poly = 0.5 * ERF_A[4]
    for factor in ERF_A[3::-1]:
        poly = poly * part + 0.5 * factor
    tail = poly * part * bell
    upper = jnp.where(pre >= 0.0, 1.0 - tail, tail)
    return pre * upper, upper + pre * bell * DENSITY


def split_out(source_ref, digit, part_refs):
    rows = part_refs[0].shape[0]
    for away, ref in enumerate(part_refs):
        start = pl.multiple_of((digit ^ away) * rows, rows)
        ref[...] = source_ref[pl.ds(start, rows), :].astype(ref.dtype)


def chunk_kernel(place_ref, *refs, first):
    step = pl.program_id(0)
    if first:
        ins, (up_ref, down_ref, bias_ref) = refs[:7], refs[7:10]
        refs, outs, wide = refs[10:-5], refs[-5:-2], refs[-2:]
        normalize(step, place_ref, *ins, *outs, *wide)
        act_ref, low_ref, _ = outs
    else:
        act_ref, low_ref, up_ref, down_ref, bias_ref = refs[:5]
        refs = refs[7:]
    hidden_ref, slope_ref, bias_grad_ref = refs[:3]
    part_refs, (grad_acc, bias_acc, bias_wide) = refs[3 : 3 + PLANE], refs[3 + PLANE :]

    @pl.when(step == 0)
    def _():
        grad_acc[...] = jnp.zeros_like(grad_acc)
        bias_acc[...] = jnp.zeros_like(bias_acc)
        bias_wide[...] = to_column(bias_ref[...].astype(bf16).astype(f32))

    halves, width, span = act_ref.shape
    units = up_ref.shape[0]
    full = halves * width
    tile = 256
    tiles = [(row, start) for start in range(0, span, tile) for row in range(0, units, tile)]

    def products(row, start):
        rows, spot = slice(row, row + tile), slice(start, start + tile)
        pre = dot(up_ref[rows, :], act_ref[:, :, spot].reshape(full, tile))
        pre += jnp.concatenate([bias_wide[rows, :]] * (tile // LANES), axis=1)
        return pre, dot(down_ref[rows, :], low_ref[:, :, spot].reshape(full, tile))

    ready = products(*tiles[0])
    for at, (row, start) in enumerate(tiles):
        pre, back = ready
        if at + 1 < len(tiles):
            ready = products(*tiles[at + 1])
        rows, spot = slice(row, row + tile), slice(start, start + tile)
        hidden, slope = gelu_pair(pre)
        hidden_ref[rows, spot] = hidden.astype(bf16)
        slope_ref[rows, spot] = (back * slope).astype(bf16)
    grad_acc[:units, :] += dot(slope_ref[...], act_ref[...].reshape(full, span), NT)
    grad_acc[units:, :] += dot(hidden_ref[...], low_ref[...].reshape(full, span), NT)
    bias_acc[...] += dot(jnp.ones((S, span), bf16), slope_ref[...], NT)

    @pl.when(step == pl.num_programs(0) - 1)
    def _():
        split_out(grad_acc, place_ref[1], part_refs)
        bias_grad_ref[...] = bias_acc[0:8, :]


def feed_chunk(chunk, place, inputs, up_turned, down, bias, earlier):
    hidden_local, full = down.shape
    units = hidden_local // CHUNKS
    width = full // 2
    span = 512
    count = inputs[1].shape[-1]
    pair = pl.BlockSpec((2, width, span), lambda i, *_: (0, 0, i))
    block = pl.BlockSpec((width, span), lambda i, *_: (0, i))
    weight = pl.BlockSpec((units, full), lambda i, *_: (chunk, 0))
    wide = pl.BlockSpec((units, span), lambda i, *_: (chunk, i))
    whole = lambda i, *_: (0, 0)
    rows = 2 * units // PLANE
    in_specs = [pair, pair]
    if chunk == 0:
        small = [pl.BlockSpec(array.shape, whole) for array in (inputs[0], *inputs[-2:])]
        in_specs = [small[0], block, block, block, block, small[1], small[2]]
    in_specs += [weight, weight, pl.BlockSpec((1, units), lambda i, *_: (0, chunk))]
    in_specs += [pl.BlockSpec(memory_space=pl.ANY)] * len(earlier)
    out_specs = [wide, wide, pl.BlockSpec((8, units), whole)] + [pl.BlockSpec((rows, full), whole)] * PLANE
    out_shape = [
        jax.ShapeDtypeStruct((hidden_local, count), bf16),
        jax.ShapeDtypeStruct((hidden_local, count), bf16),
        jax.ShapeDtypeStruct((8, units), f32),
        jax.ShapeDtypeStruct((rows, full), f32),
    ] + [jax.ShapeDtypeStruct((rows, full), bf16)] * (PLANE - 1)
    scratch_shapes = [
        pltpu.VMEM((2 * units, full), f32),
        pltpu.VMEM((S, units), f32),
        pltpu.VMEM((units, LANES), f32),
    ]
    if chunk == 0:
        out_specs += [pair, pair, pl.BlockSpec((8, span), lambda i, *_: (0, i))]
        out_shape += [jax.ShapeDtypeStruct((2, width, count), bf16)] * 2 + [jax.ShapeDtypeStruct((8, count), f32)]
        scratch_shapes += [pltpu.VMEM((3, width, LANES), f32)] * 2

    def body(*refs):
        if chunk == 0:
            made = len(in_specs) + 1 + len(out_specs)
            outs = refs[made - 3 : made]
            refs = (*refs[: made - 3], *refs[made:-2], *outs, *refs[-2:])
        chunk_kernel(*refs, first=chunk == 0)

    return pl.pallas_call(
        body,
        grid_spec=pltpu.PrefetchScalarGridSpec(
            num_scalar_prefetch=1,
            grid=(count // span,),
            in_specs=in_specs,
            out_specs=out_specs,
            scratch_shapes=scratch_shapes,
        ),
        out_shape=out_shape,
        input_output_aliases={6: 0, 7: 1} if earlier else {},
        compiler_params=params(),
        cost_estimate=cost(40),
        name="feed_chunk_%d" % chunk,
    )(place, *inputs, up_turned, down, bias, *earlier)


def across(value, stride):
    size = lax.axis_size("line") * PLANE
    return lax.ppermute(value, ("line", "plane"), [(i, i ^ stride) for i in range(size)])


def along(value, axis, away):
    return lax.ppermute(value, axis, [(i, i ^ away) for i in range(lax.axis_size(axis))])


class GradientSum:
    def __init__(self, kept, sends):
        self.kept = kept
        self.got = [along(value, "plane", away) for away, value in enumerate(sends, 1)]

    def add(self):
        total = self.kept
        for value in self.got:
            total = total + value.astype(f32)
        return total

    def to_line(self):
        size = lax.axis_size("line")
        total = self.add()
        parts = total.reshape(size, -1, total.shape[1])

        def part(away):
            return lax.dynamic_index_in_dim(parts, lax.axis_index("line") ^ away, 0, keepdims=False)

        self.kept = part(0)
        self.sends = [part(away).astype(bf16) for away in range(1, size)]
        self.got = [along(value, "line", away) for away, value in enumerate(self.sends, 1)]

    def to_piece(self):
        self.piece = self.add().astype(bf16)

    def gather(self):
        self.to_piece()
        self.sum = lax.all_gather(self.piece, ("plane", "line"), axis=0, tiled=True)

    def gather_line(self):
        self.to_piece()
        size = lax.axis_size("line")
        self.pieces = [self.piece] + [along(self.piece, "line", away) for away in range(1, size)]

    def gather_plane(self):
        self.quarter = jnp.concatenate(self.pieces)
        self.quarters = [self.quarter] + [along(self.quarter, "plane", away) for away in range(1, PLANE)]


EXTRA = 16


def sums_kernel(
    place_ref,
    hidden_ref,
    slope_ref,
    down_ref,
    up_ref,
    own_ref,
    other_ref,
    stat_ref,
    own_rows_ref,
    other_rows_ref,
    *refs,
    skipped,
):
    own_proj_ref, own_act_ref, sum_ref, send_ref = refs[skipped : skipped + 4]
    own_wide, other_wide = refs[-2:]
    width, span = own_ref.shape
    mine = place_ref[0]
    own_rows = pl.ds(pl.multiple_of(mine * width, width), width)
    other_rows = pl.ds(pl.multiple_of((1 - mine) * width, width), width)

    @pl.when(pl.program_id(0) == 0)
    def _():
        own_wide[0] = to_column(own_rows_ref[0:1, :])
        other_wide[0] = to_column(other_rows_ref[0:1, :])

    own_proj_ref[...] = dot(down_ref[own_rows, :], hidden_ref[...]).astype(bf16)
    send_ref[0:width, :] = dot(down_ref[other_rows, :], hidden_ref[...]).astype(bf16)
    mean, scale = stat_ref[0:1, :], stat_ref[1:2, :]
    sums = []
    for own, rows, value_ref, wide in (
        (True, own_rows, own_ref, own_wide),
        (False, other_rows, other_ref, other_wide),
    ):
        act = dot(up_ref[rows, :], slope_ref[...])
        if own:
            own_act_ref[...] = act
        else:
            send_ref[width : 2 * width, :] = act.astype(bf16)
        act = act * wide_column(wide, 0, span)
        normed = (value_ref[...].astype(f32) - mean) * scale
        sums.append(jnp.sum(act, axis=0, keepdims=True))
        sums.append(jnp.sum(act * normed, axis=0, keepdims=True))
    plain, tilt = sums[0] + sums[2], sums[1] + sums[3]
    sum_ref[0:1, :] = plain
    sum_ref[1:2, :] = tilt
    parts = []
    for value in (plain, tilt):
        high = value.astype(bf16).astype(f32)
        parts += [high, value - high]
    parts.append(jnp.zeros((EXTRA - 4, span), f32))
    send_ref[2 * width :, :] = jnp.concatenate(parts, axis=0).astype(bf16)


def hidden_sums(place, hidden, slopes, down_turned, up, own, other, stat, own_rows, other_rows, part, tokens, riders):
    width, total = own.shape
    count = total // SUM_PARTS
    hidden_local = hidden.shape[0]
    span = 512
    base = part * (count // span)
    column = lambda i, *_: (0, base + i)
    out = lambda i, *_: (0, i)
    fixed = lambda i, *_: (0, 0)
    wide = pl.BlockSpec((hidden_local, span), column)
    block = pl.BlockSpec((width, span), column)
    result = pl.BlockSpec((width, span), out)
    rows = pl.BlockSpec(own_rows.shape, fixed)
    sent = 2 * width + EXTRA
    grid_spec = pltpu.PrefetchScalarGridSpec(
        num_scalar_prefetch=1,
        grid=(count // span,),
        in_specs=[
            wide,
            wide,
            pl.BlockSpec(down_turned.shape, fixed),
            pl.BlockSpec(up.shape, fixed),
            block,
            block,
            pl.BlockSpec((8, span), column),
            rows,
            rows,
        ]
        + [pl.BlockSpec(memory_space=pl.ANY)] * (len(riders) + len(tokens)),
        out_specs=[result, result, pl.BlockSpec((8, span), out), pl.BlockSpec((sent, span), out)]
        + [pl.BlockSpec(memory_space=pl.ANY)] * len(riders),
        scratch_shapes=[pltpu.VMEM((1, width, LANES), f32)] * 2,
    )
    values = pl.pallas_call(
        functools.partial(sums_kernel, skipped=len(riders) + len(tokens)),
        grid_spec=grid_spec,
        out_shape=[
            jax.ShapeDtypeStruct((width, count), bf16),
            jax.ShapeDtypeStruct((width, count), f32),
            jax.ShapeDtypeStruct((8, count), f32),
            jax.ShapeDtypeStruct((sent, count), bf16),
        ]
        + [jax.ShapeDtypeStruct(rider.shape, rider.dtype) for rider in riders],
        input_output_aliases={10 + at: 4 + at for at in range(len(riders))},
        compiler_params=params(),
        cost_estimate=cost(40 / SUM_PARTS * 2),
        name="hidden_sums_%d" % part,
    )(place, hidden, slopes, down_turned, up, own, other, stat, own_rows, other_rows, *riders, *tokens)
    return values[:3], values[3], values[4:]


TAPS, ROWS, BIAS = 0, 32, 40


def correlate(left_ref, right_ref, sum_ref, half, lanes):
    left = [left_ref[block_rows(place), lanes] for place in range(S)]
    right = [right_ref[block_rows(place), lanes].astype(f32) for place in range(S)]
    for back in range(S):
        total = left[back] * right[0]
        for place in range(back + 1, S):
            total += left[place] * right[place - back]
        sum_ref[half, block_rows(back), lanes] += total


def backward_kernel(
    sizes_ref,
    pixels_ref,
    grad_ref,
    mixed_ref,
    first_ref,
    stat_ref,
    own_proj_ref,
    own_act_ref,
    own_sum_ref,
    got_ref,
    rows_ref,
    taps_ref,
    turn_ref,
    *refs,
    base,
    carries,
    skipped,
):
    carry_refs, refs = refs[:carries], refs[carries:]
    out_ref, pixel_grad_ref, small_ref = refs[skipped : skipped + 3]
    sum_ref, channel_sum, cells_ref, low_ref, wide_ref, back_ref, columns = refs[-7:]
    step = pl.program_id(0)
    width = pixels_ref.shape[0]
    full = 2.0 * width

    @pl.when(step == 0)
    def _():
        sum_ref[...] = jnp.zeros_like(sum_ref)
        channel_sum[...] = jnp.zeros_like(channel_sum)
        for row in (0, 2, 3, 4):
            columns[row] = to_column(rows_ref[row : row + 1, :])

    mask = image_mask(sizes_ref, base + step)
    pixels = pixels_ref[...].astype(f32)
    grad = grad_ref[...].astype(f32)
    masked = pixels * mask
    gain, skip, layer, shift = (wide_column(columns, row, AREA) for row in (0, 2, 3, 4))

    def gather(row, value):
        channel_sum[row] += value[:, :LANES] + value[:, LANES:]

    masked_grad = grad * mask
    branch = own_proj_ref[...].astype(f32) + got_ref[0:width, :].astype(f32) + shift
    out_ref[...] = pixels + mask * layer * branch
    gather(3, masked_grad * branch)
    gather(4, masked_grad)

    scale = stat_ref[1:2, :]
    normed = (mixed_ref[...].astype(f32) - stat_ref[0:1, :]) * scale
    act = own_act_ref[...] + got_ref[width : 2 * width, :].astype(f32)
    gather(0, act * normed)
    gather(1, act)
    got = got_ref[2 * width :, :].astype(f32)
    plain = (own_sum_ref[0:1, :] + (got[0:1, :] + got[1:2, :])) / full
    tilt = (own_sum_ref[1:2, :] + (got[2:3, :] + got[3:4, :])) / full
    mixed_low = (scale * (act * gain - plain - normed * tilt)).astype(bf16)
    mixed_grad = mixed_low.astype(f32)
    gather(2, mixed_grad * masked)

    cells_ref[...] = dot(turn_ref[:AREA, :], masked.astype(bf16), NT)
    wide_ref[...] = dot(turn_ref[AREA:, :], mixed_low, NT)
    for start in range(0, width, LANES):
        lanes = slice(start, start + LANES)
        for place, value in enumerate(anticausal(wide_ref, taps_ref, 1, lanes)):
            low_ref[block_rows(place), lanes] = value.astype(bf16)
        correlate(wide_ref, first_ref, sum_ref, 1, lanes)
    back_ref[...] = dot(turn_ref[AREA:, :], low_ref[...])
    for start in range(0, width, LANES):
        lanes = slice(start, start + LANES)
        for place, value in enumerate(anticausal(back_ref, taps_ref, 0, lanes)):
            wide_ref[block_rows(place), lanes] = value
        correlate(back_ref, cells_ref, sum_ref, 0, lanes)
    pixel_grad_ref[...] = grad + mask * (wide_ref[...].T + skip * mixed_grad)

    @pl.when(step == pl.num_programs(0) - 1)
    def _():
        if base > 0:
            small_ref[...] = carry_refs[0][...]
        else:
            small_ref[...] = jnp.zeros_like(small_ref)
            row = BIAS
            for ref in carry_refs:
                for start in range(0, ref.shape[1], width):
                    small_ref[row : row + 1, :] = ref[0:1, start : start + width]
                    row += 1
        for half in range(2):
            for back in range(S):
                row = TAPS + half * S + back
                small_ref[row : row + 1, :] += jnp.sum(
                    sum_ref[half, block_rows(back), :], axis=0, keepdims=True
                )
        for row in range(5):
            small_ref[ROWS + row : ROWS + row + 1, :] += jnp.sum(channel_sum[row].T, axis=0, keepdims=True)


def backward(sizes, pixels, grad, mixed, mid, stat, own, got, rows, taps, turn, carries, part, earlier, riders, tokens):
    own_proj, own_act, own_sum = own
    width, total = pixels.shape
    count = total // BACK_PARTS
    base = part * (count // AREA)
    inner = base % (own_proj.shape[1] // AREA)
    column = lambda i: (0, base + i)
    here = lambda i: (0, inner + i)
    fixed = lambda i: (0, 0)
    block = pl.BlockSpec((width, AREA), column)
    local = pl.BlockSpec((width, AREA), here)
    anywhere = pl.BlockSpec(memory_space=pl.ANY)
    in_specs = [
        pl.BlockSpec(sizes.shape, fixed),
        block,
        block,
        block,
        pl.BlockSpec((AREA, width), lambda i: (base + i, 0)),
        pl.BlockSpec((8, AREA), column),
        local,
        local,
        pl.BlockSpec((8, AREA), here),
        pl.BlockSpec((got.shape[0], AREA), here),
        pl.BlockSpec(rows.shape, fixed),
        pl.BlockSpec(taps.shape, lambda i: (0, 0, 0)),
        pl.BlockSpec(turn.shape, fixed),
    ]
    in_specs += [pl.BlockSpec(carry.shape, fixed) for carry in carries]
    in_specs += [anywhere] * (len(earlier) + len(riders) + len(tokens))
    first = 13 + len(carries)
    small = (BIAS + 8, width)
    return pl.pallas_call(
        functools.partial(backward_kernel, base=base, carries=len(carries), skipped=len(earlier) + len(riders) + len(tokens)),
        grid=(count // AREA,),
        in_specs=in_specs,
        out_specs=[block, block, pl.BlockSpec(small, fixed)] + [anywhere] * len(riders),
        scratch_shapes=[
            pltpu.VMEM((2, AREA, width), f32),
            pltpu.VMEM((5, width, LANES), f32),
            pltpu.VMEM((AREA, width), f32),
            pltpu.VMEM((AREA, width), bf16),
            pltpu.VMEM((AREA, width), f32),
            pltpu.VMEM((AREA, width), f32),
            pltpu.VMEM((5, width, LANES), f32),
        ],
        out_shape=[
            jax.ShapeDtypeStruct((width, total), f32),
            jax.ShapeDtypeStruct((width, total), f32),
            jax.ShapeDtypeStruct(small, f32),
        ]
        + [jax.ShapeDtypeStruct(rider.shape, rider.dtype) for rider in riders],
        input_output_aliases={first + at: at for at in range(len(earlier))}
        | {first + len(earlier) + at: 3 + at for at in range(len(riders))},
        compiler_params=params(),
        cost_estimate=cost(45 / BACK_PARTS * 2),
        name="backward_%d" % part,
    )(
        sizes, pixels, grad, mixed, mid, stat, own_proj, own_act, own_sum, got, rows, taps, turn, *carries, *earlier, *riders, *tokens
    )


UP_ROW, UP_MASS, DOWN_COL, DOWN_MASS, MIXER_COL, MIXER_MASS, SCALARS = range(7)


def fold(value):
    total = value[:, :LANES]
    for start in range(LANES, value.shape[1], LANES):
        total += value[:, start : start + LANES]
    return total


def as_row(ref):
    return ref[...].reshape(1, ref.shape[0])


def to_flat(ref, value):
    ref[...] = value.reshape(ref.shape[0])


def to_column(row):
    return jnp.broadcast_to(row, (LANES, row.shape[1])).T


def to_row(columns):
    return jnp.sum(columns.T, axis=0, keepdims=True)


def statistics_kernel(place_ref, *refs, quarters, skipped, line_parts):
    sources, refs = refs[:quarters], refs[quarters:]
    up_old_ref, down_old_ref, carry_ref = refs[:3]
    up_ref, down_ref, up_new_ref, down_new_ref, stat_ref = refs[3 + skipped : 8 + skipped]
    quarter_ref = refs[-1]
    step = pl.program_id(0)
    plane, line = place_ref[1], place_ref[2]
    steps = PLANE // 2

    @pl.when(step == 0)
    def _():
        stat_ref[...] = carry_ref[...]

    for kind, old_ref, new_ref, columns, mass in (
        (0, up_old_ref, up_new_ref, UP_ROW, UP_MASS),
        (1, down_old_ref, down_new_ref, DOWN_COL, DOWN_MASS),
    ):
        if quarters == 2:
            value = sources[kind][...].astype(f32)
        else:
            for away, source_ref in enumerate(sources):

                @pl.when((kind * steps + step) ^ plane == away)
                def _():
                    rows = quarter_ref.shape[0] // line_parts

                    def move(at, _):
                        target = pl.ds(pl.multiple_of(at * rows, rows), rows)
                        source = pl.ds(pl.multiple_of((at ^ line) * rows, rows), rows)
                        quarter_ref[target, :] = source_ref[source, :].astype(f32)
                        return 0

                    lax.fori_loop(0, line_parts, move, 0)

            value = quarter_ref[...]
        if kind == 0:
            up_ref[...] = value.T
        else:
            down_ref[...] = value
        square = value * value
        mean = jnp.sum(fold(square), axis=1, keepdims=True) / value.shape[1]
        fresh = DECAY * to_column(old_ref[...]) + FRESH * (mean + EPSILON_SQUARE)
        new_ref[...] = fresh.T[0:1, :]
        stat_ref[columns : columns + 1, : value.shape[1]] += jnp.sum(square, axis=0, keepdims=True)
        stat_ref[mass : mass + 1, : value.shape[1]] += jnp.sum(
            square * (1.0 / fresh[:, 0:1]), axis=0, keepdims=True
        )


def statistics(chunk, place, sources, up_cols, down_rows, carry, earlier):
    hidden_local = up_cols.shape[1]
    units = hidden_local // CHUNKS
    full = sources[0].shape[1]
    rows = 2 * units // PLANE
    steps = PLANE // 2
    base = chunk * steps
    row = pl.BlockSpec((1, rows), lambda i: (0, base + i))
    anywhere = pl.BlockSpec(memory_space=pl.ANY)
    fixed = pl.BlockSpec(carry.shape, lambda i: (0, 0))
    if len(sources) == 2:
        specs = [
            pl.BlockSpec((rows, full), lambda i: (i, 0)),
            pl.BlockSpec((rows, full), lambda i: (steps + i, 0)),
        ]
    else:
        specs = [pl.BlockSpec((rows, full), lambda i: (0, 0))] * PLANE
    first = 4 + len(sources)
    return pl.pallas_call(
        functools.partial(statistics_kernel, quarters=len(sources), skipped=len(earlier), line_parts=lax.axis_size("line")),
        grid=(steps,),
        in_specs=[pl.BlockSpec(memory_space=pltpu.SMEM)]
        + specs
        + [row, row, fixed]
        + [anywhere] * len(earlier),
        out_specs=[
            pl.BlockSpec((full, rows), lambda i: (0, base + i)),
            pl.BlockSpec((rows, full), lambda i: (base + i, 0)),
            row,
            row,
            fixed,
        ],
        out_shape=[
            jax.ShapeDtypeStruct((full, hidden_local), f32),
            jax.ShapeDtypeStruct((hidden_local, full), f32),
            jax.ShapeDtypeStruct((1, hidden_local), f32),
            jax.ShapeDtypeStruct((1, hidden_local), f32),
            jax.ShapeDtypeStruct(carry.shape, f32),
        ],
        input_output_aliases={first + at: at for at in range(len(earlier))},
        scratch_shapes=[pltpu.VMEM((rows, full), f32)],
        compiler_params=params(),
        cost_estimate=cost(1),
        name="statistics_%d" % chunk,
    )(place, *sources, up_cols, down_rows, carry, *earlier)


def small_kernel(
    sum_ref,
    stat_ref,
    square_ref,
    params_ref,
    channel_ref,
    moment_ref,
    bias_ref,
    bias_moment_ref,
    rows_ref,
    down_rows_new_ref,
    mixer_grad_ref,
    rows_new_ref,
    channel_grad_ref,
    moment_new_ref,
    channel_update_ref,
    bias_grad_ref,
    bias_moment_new_ref,
    bias_update_ref,
    out_ref,
    channel_square_ref,
    table_ref,
):
    out_ref[...] = stat_ref[...]
    taps_back(params_ref, sum_ref, table_ref)
    grad = table_ref[...].T
    mixer_grad_ref[...] = grad
    states = grad.shape[1]
    square = grad * grad
    mean = jnp.sum(fold(square), axis=1, keepdims=True) / states
    fresh = DECAY * to_column(as_row(rows_ref)) + FRESH * (mean + EPSILON_SQUARE)
    rows_new = fresh.T[0:1, :]
    rows_new_ref[...] = rows_new
    out_ref[MIXER_COL : MIXER_COL + 1, :states] = jnp.sum(square, axis=0, keepdims=True)
    out_ref[MIXER_MASS : MIXER_MASS + 1, :states] = jnp.sum(square * (1.0 / fresh[:, 0:1]), axis=0, keepdims=True)

    layer = channel_ref[3:4, :]
    channel_grad_ref[0:4, :] = sum_ref[ROWS : ROWS + 4, :]
    channel_grad_ref[4:5, :] = sum_ref[ROWS + 4 : ROWS + 5, :] * layer
    grad = channel_grad_ref[...]
    moment = DECAY * moment_ref[...] + FRESH * (grad * grad + EPSILON_SQUARE)
    moment_new_ref[...] = moment
    channel_update = grad * lax.rsqrt(moment)
    channel_update_ref[...] = channel_update

    width = layer.shape[1]
    for at in range(bias_grad_ref.shape[1] // width):
        bias_grad_ref[:, at * width : (at + 1) * width] = sum_ref[BIAS + at : BIAS + at + 1, :]
    grad = bias_grad_ref[...]
    moment = DECAY * as_row(bias_moment_ref) + FRESH * (grad * grad + EPSILON_SQUARE)
    bias_moment_new_ref[...] = moment
    bias_update = grad * lax.rsqrt(moment)
    bias_update_ref[...] = bias_update

    def total(value):
        return jnp.sum(value, keepdims=True)

    channel = channel_ref[...]
    table = params_ref[...]
    bias = as_row(bias_ref)
    scalars = (
        total(channel_update * channel_update) + total(bias_update * bias_update),
        total(down_rows_new_ref[...]),
        total(rows_new),
        total(square_ref[0:1, :]),
        total(square_ref[1:2, :]),
        total(table * table),
        total(bias * bias),
    )
    for at, value in enumerate(scalars):
        out_ref[SCALARS : SCALARS + 1, at * LANES : (at + 1) * LANES] = jnp.broadcast_to(value, (1, LANES))
    channel_square_ref[...] = jnp.broadcast_to(jnp.sum(channel * channel, axis=1, keepdims=True), (5, LANES))


def small_update(total, stat, square, mixer_params, channel_params, channel_moment, bias, bias_moment, rows, down_rows_new):
    width, states = mixer_params.shape
    shapes = [
        (width, states),
        (1, width),
        channel_params.shape,
        channel_params.shape,
        channel_params.shape,
        (1, bias.shape[0]),
        (1, bias.shape[0]),
        (1, bias.shape[0]),
        (8, 8 * LANES),
        (5, LANES),
    ]
    return pl.pallas_call(
        small_kernel,
        out_shape=[jax.ShapeDtypeStruct(shape, f32) for shape in shapes],
        scratch_shapes=[pltpu.VMEM((states, width), f32)],
        compiler_params=params(),
        cost_estimate=cost(5),
        name="small_update",
    )(total, stat, square, mixer_params, channel_params, channel_moment, bias, bias_moment, rows, down_rows_new)


def update_kernel(
    stat_ref,
    got_ref,
    channel_square_ref,
    channel_got_ref,
    up_rows_ref,
    down_cols_ref,
    mixer_cols_ref,
    up_cols_new_ref,
    down_rows_new_ref,
    up_grad_ref,
    up_ref,
    up_average_ref,
    down_grad_ref,
    down_ref,
    down_average_ref,
    mixer_grad_ref,
    mixer_ref,
    mixer_average_ref,
    mixer_rows_new_ref,
    channel_ref,
    channel_average_ref,
    channel_update_ref,
    bias_ref,
    bias_average_ref,
    bias_update_ref,
    bias_grad_ref,
    bias_moment_ref,
    up_cols_all_ref,
    down_rows_all_ref,
    rms_ref,
    up_rows_new_ref,
    down_cols_new_ref,
    mixer_cols_new_ref,
    up_new_ref,
    up_average_new_ref,
    down_new_ref,
    down_average_new_ref,
    mixer_new_ref,
    mixer_average_new_ref,
    channel_new_ref,
    channel_average_new_ref,
    bias_new_ref,
    bias_average_new_ref,
    bias_grad_out_ref,
    bias_moment_out_ref,
    up_cols_out_ref,
    down_rows_out_ref,
    mixer_rows_out_ref,
):
    full, hidden = up_rows_ref.shape[0], 2 * bias_ref.shape[0]
    states = mixer_cols_ref.shape[0]

    def stat(row, size):
        return stat_ref[row : row + 1, :size] + got_ref[row : row + 1, :size]

    def scalar(at):
        return stat(SCALARS, 8 * LANES)[:, at * LANES : at * LANES + 1]

    def total(value):
        return jnp.sum(value, axis=1, keepdims=True)

    up_rows_new = DECAY * as_row(up_rows_ref) + FRESH * (stat(UP_ROW, full) / hidden + EPSILON_SQUARE)
    down_cols_new = DECAY * as_row(down_cols_ref) + FRESH * (stat(DOWN_COL, full) / hidden + EPSILON_SQUARE)
    mixer_cols_new = DECAY * as_row(mixer_cols_ref) + FRESH * (stat(MIXER_COL, states) / full + EPSILON_SQUARE)
    up_mean = total(up_rows_new) / full
    down_mean = scalar(1) / hidden
    mixer_mean = scalar(2) / full
    square = (
        scalar(0)
        + up_mean * total(stat(UP_MASS, full) / up_rows_new)
        + down_mean * total(stat(DOWN_MASS, full) / down_cols_new)
        + mixer_mean * total(stat(MIXER_MASS, states) / mixer_cols_new)
    )
    rms = jnp.sqrt(square / (2 * full * hidden + states * full + 5 * full + hidden))
    factor = LEARN_RATE * CLIP_LEVEL / jnp.maximum(CLIP_LEVEL, rms)

    def rate(squares, size):
        return factor * jnp.maximum(EPSILON_SCALE, jnp.sqrt(squares / size))

    def settle(weight, change, average_ref, new_ref, average_new_ref):
        new = weight - change
        new_ref[...] = new
        average_new_ref[...] = AVERAGE_KEEP * average_ref[...] + (1.0 - AVERAGE_KEEP) * new

    def column(row):
        return to_column(row)[:, 0:1]

    up_speed = rate(scalar(3), full * hidden) * jnp.sqrt(up_mean)
    settle(
        up_ref[...],
        up_grad_ref[...] * column(lax.rsqrt(up_rows_new) * up_speed) * lax.rsqrt(up_cols_new_ref[...]),
        up_average_ref,
        up_new_ref,
        up_average_new_ref,
    )
    down_speed = rate(scalar(4), full * hidden) * jnp.sqrt(down_mean)
    settle(
        down_ref[...],
        down_grad_ref[...] * column(lax.rsqrt(down_rows_new_ref[...]) * down_speed) * lax.rsqrt(down_cols_new),
        down_average_ref,
        down_new_ref,
        down_average_new_ref,
    )

    @pl.when(pl.program_id(0) == 0)
    def _():
        rms_ref[...] = rms
        to_flat(up_rows_new_ref, up_rows_new)
        to_flat(down_cols_new_ref, down_cols_new)
        to_flat(mixer_cols_new_ref, mixer_cols_new)
        to_flat(bias_grad_out_ref, bias_grad_ref[...])
        to_flat(bias_moment_out_ref, bias_moment_ref[...])
        to_flat(up_cols_out_ref, up_cols_all_ref[...])
        to_flat(down_rows_out_ref, down_rows_all_ref[...])
        to_flat(mixer_rows_out_ref, mixer_rows_new_ref[...])
        mixer_speed = rate(scalar(5), states * full) * jnp.sqrt(mixer_mean)
        settle(
            mixer_ref[...],
            mixer_grad_ref[...]
            * column(lax.rsqrt(mixer_rows_new_ref[...]) * mixer_speed)
            * lax.rsqrt(mixer_cols_new),
            mixer_average_ref,
            mixer_new_ref,
            mixer_average_new_ref,
        )
        channel_square = channel_square_ref[:, 0:1] + channel_got_ref[:, 0:1]
        settle(
            channel_ref[...],
            rate(channel_square, full) * channel_update_ref[...],
            channel_average_ref,
            channel_new_ref,
            channel_average_new_ref,
        )
        bias_new = as_row(bias_ref) - rate(scalar(6), hidden) * bias_update_ref[...]
        to_flat(bias_new_ref, bias_new)
        to_flat(
            bias_average_new_ref, AVERAGE_KEEP * as_row(bias_average_ref) + (1.0 - AVERAGE_KEEP) * bias_new
        )


def final_update(operands, units):
    up, mixer, channel, bias = operands[10], operands[16], operands[19], operands[22]
    full, hidden_local = up.shape
    up_block = pl.BlockSpec((full, units), lambda i: (0, i))
    down_block = pl.BlockSpec((units, full), lambda i: (i, 0))
    row_block = pl.BlockSpec((1, units), lambda i: (0, i))

    def whole(array):
        return pl.BlockSpec(array.shape, lambda i: (0,) * len(array.shape))

    in_specs = [whole(array) for array in operands]
    in_specs[7:9] = [row_block, row_block]
    in_specs[9:12] = [up_block] * 3
    in_specs[12:15] = [down_block] * 3
    shapes = [(1, 1), operands[4].shape, operands[5].shape, operands[6].shape]
    shapes += [up.shape] * 2 + [(hidden_local, full)] * 2 + [mixer.shape] * 2 + [channel.shape] * 2 + [bias.shape] * 2
    shapes += [bias.shape] * 4 + [operands[18].shape[1:]]
    out_specs = [whole(jax.ShapeDtypeStruct(shape, f32)) for shape in shapes]
    out_specs[4:8] = [up_block, up_block, down_block, down_block]
    return pl.pallas_call(
        update_kernel,
        grid=(hidden_local // units,),
        in_specs=in_specs,
        out_specs=out_specs,
        out_shape=[jax.ShapeDtypeStruct(shape, f32) for shape in shapes],
        compiler_params=params(),
        cost_estimate=cost(19),
        name="final_update",
    )(*operands)


def turn_table():
    place = np.arange(AREA)
    swapped = (place % S) * S + place // S
    table = np.concatenate([place[:, None] == place[None, :], swapped[:, None] == place[None, :]])
    return table.astype(ml_dtypes.bfloat16)


def shards(
    pixels,
    image_sizes,
    out_grad,
    up_weight,
    down_weight,
    mixer_params,
    channel_params,
    hidden_bias,
    up_rows,
    up_cols,
    down_rows,
    down_cols,
    mixer_rows,
    mixer_cols,
    channel_moment,
    bias_moment,
    up_average,
    down_average,
    mixer_average,
    channel_average,
    bias_average,
):
    width_local, count = pixels.shape
    hidden_local = up_weight.shape[1]
    place = jnp.stack([lax.axis_index(axis) for axis in ("ch", "plane", "line")]).astype(jnp.int32)

    def exchange(value):
        return lax.ppermute(value, "ch", [(0, 1), (1, 0)])

    def row(value):
        return value.reshape(1, -1)

    other_grad = exchange(out_grad)
    rounded = jnp.concatenate(
        [channel_params[0:2].astype(bf16).astype(f32), channel_params[2:5], jnp.zeros((3, width_local), f32)]
    )
    others = exchange(rounded)
    turn = jnp.asarray(turn_table())
    sizes = image_sizes.T
    mixed, first, taps = mixer_forward(sizes, pixels, mixer_params, channel_params, turn)
    other_mixed = exchange(mixed)
    up_low, up_turned, down_low, down_turned, square = weights_low(up_weight, down_weight)
    sums, bias_parts = [], []
    earlier = ()
    inputs = [sizes, mixed, other_mixed, out_grad, other_grad, rounded, others]
    for chunk in range(CHUNKS):
        values = feed_chunk(chunk, place, inputs, up_turned, down_low, row(hidden_bias), earlier)
        earlier = values[0:2]
        if chunk == 0:
            inputs, stat = values[-3:-1], values[-1]
        bias_parts.append(values[2])
        sums.append(GradientSum(values[3], values[4 : 3 + PLANE]))
    hidden, slopes = earlier
    partial = []
    early, late = sums
    early.to_line()
    tokens, riders = early.sends, [early.kept, late.kept]
    for part in range(SUM_PARTS):
        own, send, riders = hidden_sums(
            place, hidden, slopes, down_turned, up_low, mixed, other_mixed, stat, rounded, others, part, tokens, riders
        )
        if part == 0:
            early.kept, late.kept = riders
            early.gather()
            tokens, riders = [early.piece], [late.kept]
        partial.append((own, exchange(send)))
    done = ()
    (late.kept,) = riders
    late.to_line()
    by_permutes = late.kept.shape[0] % S == 0
    tokens, riders = late.sends, [late.kept]
    carries = bias_parts
    for part in range(BACK_PARTS):
        own, got = partial[part * SUM_PARTS // BACK_PARTS]
        values = backward(
            sizes, pixels, out_grad, mixed, first, stat, own, got, rounded, taps, turn, carries, part, done, riders, tokens
        )
        done, carries = values[0:2], values[2:3]
        tokens, riders = [], []
        if part == 0:
            (late.kept,) = values[3:]
            if by_permutes:
                late.gather_line()
                tokens, riders = [late.piece], [late.piece]
            else:
                late.gather()
        elif part == 1 and by_permutes:
            late.pieces[0] = values[3]
            late.gather_plane()
            tokens = [late.quarter]
    (carry,) = carries
    block_out, pixel_grad = done

    total, stride = carry, 1
    while stride < lax.axis_size("line") * PLANE:
        total, stride = total + across(total, stride), 2 * stride
    stats = jnp.zeros((8, 8 * LANES), f32)
    settled = ()
    for chunk, sources in enumerate(([early.sum] * 2, late.quarters if by_permutes else [late.sum] * 2)):
        values = statistics(chunk, place, sources, row(up_cols), row(down_rows), stats, settled)
        settled, stats = values[0:4], values[4]
    up_sum, down_sum, up_cols_new, down_rows_new = settled
    (
        mixer_sum,
        mixer_rows_new,
        channel_sum,
        channel_moment_new,
        channel_update,
        bias_sum,
        bias_moment_new,
        bias_update,
        stats,
        channel_square,
    ) = small_update(
        total,
        stats,
        square,
        mixer_params,
        channel_params,
        channel_moment,
        hidden_bias,
        bias_moment,
        mixer_rows,
        down_rows_new,
    )
    got_stats, got_square = exchange((stats, channel_square))
    (
        update_rms,
        up_rows_new,
        down_cols_new,
        mixer_cols_new,
        up_new,
        up_average_new,
        down_new,
        down_average_new,
        mixer_new,
        mixer_average_new,
        channel_new,
        channel_average_new,
        bias_new,
        bias_average_new,
        bias_sum,
        bias_moment_new,
        up_cols_new,
        down_rows_new,
        mixer_rows_new,
    ) = final_update(
        [
            stats,
            got_stats,
            channel_square,
            got_square,
            up_rows,
            down_cols,
            mixer_cols,
            up_cols_new,
            down_rows_new,
            up_sum,
            up_weight,
            up_average,
            down_sum,
            down_weight,
            down_average,
            mixer_sum,
            mixer_params,
            mixer_average,
            mixer_rows_new,
            channel_params,
            channel_average,
            channel_update,
            hidden_bias,
            bias_average,
            bias_update,
            bias_sum,
            bias_moment_new,
            up_cols_new,
            down_rows_new,
        ],
        256,
    )
    return (
        block_out,
        pixel_grad,
        update_rms.reshape(()),
        up_sum,
        up_rows_new,
        up_cols_new,
        up_new,
        up_average_new,
        down_sum,
        down_rows_new,
        down_cols_new,
        down_new,
        down_average_new,
        mixer_sum,
        mixer_rows_new,
        mixer_cols_new,
        mixer_new,
        mixer_average_new,
        channel_sum,
        channel_moment_new,
        channel_new,
        channel_average_new,
        bias_sum,
        bias_moment_new,
        bias_new,
        bias_average_new,
    )


def solution(mesh):
    mesh = jax.sharding.Mesh(mesh.devices.reshape(-1, PLANE, mesh.shape["ch"]), ("line", "plane", "ch"))
    images = ("line", "plane")
    split = P("ch", images)
    over_rows, over_cols, over = P("ch", None), P(None, "ch"), P("ch")
    return jax.shard_map(
        shards,
        mesh=mesh,
        in_specs=(
            split,
            P(images, None),
            split,
            over_cols,
            over_rows,
            over_rows,
            over_cols,
            over,
            P(),
            over,
            over,
            P(),
            over,
            P(),
            over_cols,
            over,
            over_cols,
            over_rows,
            over_rows,
            over_cols,
            over,
        ),
        out_specs=(
            split,
            split,
            P(),
            over_cols,
            P(),
            over,
            over_cols,
            over_cols,
            over_rows,
            over,
            P(),
            over_rows,
            over_rows,
            over_rows,
            over,
            P(),
            over_rows,
            over_rows,
            over_cols,
            over_cols,
            over_cols,
            over_cols,
            over,
            over,
            over,
            over,
        ),
        check_vma=False,
    )
```

```python
import functools

import jax
import jax.numpy as jnp
import ml_dtypes
import numpy as np
from jax import lax
from jax.experimental import pallas as pl
from jax.experimental.pallas import tpu as pltpu
from jax.sharding import PartitionSpec as P

S = 16
AREA = S * S
STEP = 10
LANES = 128

EPSILON_NORM = 1e-06
EPSILON_SQUARE = 1e-30
EPSILON_SCALE = 0.001
LEARN_RATE = 0.3
CLIP_LEVEL = 1.0
AVERAGE_KEEP = 0.9
HALF_ROOT = 0.7071067811865476
DENSITY = 0.3989422804014327
LOG2_E = 1.4426950408889634
DECAY = 1.0 - STEP ** (-0.8)
FRESH = 1.0 - DECAY
ERF_P = 0.3275911
ERF_A = (0.254829592, -0.284496736, 1.421413741, -1.453152027, 1.061405429)
CHUNKS = 2
SUM_PARTS = 2
BACK_PARTS = ((0, 4), (4, 4), (8, 8))
PLANE = 4

f32 = jnp.float32
bf16 = jnp.bfloat16
NT = (((1,), (1,)), ((), ()))
TN = (((0,), (0,)), ((), ()))
NN = (((1,), (0,)), ((), ()))


def dot(left, right, dims=NN):
    return lax.dot_general(left, right, dims, preferred_element_type=f32)


def params(mib=60):
    return pltpu.CompilerParams(vmem_limit_bytes=mib * 1024 * 1024)


def cost(microseconds):
    return pl.CostEstimate(
        flops=int(microseconds * 1e9), bytes_accessed=int(microseconds * 3e6), transcendentals=0
    )


def image_mask(sizes_ref, image):
    place = lax.broadcasted_iota(jnp.int32, (1, AREA), 1)
    row, column = lax.shift_right_logical(place, 4), place & (S - 1)
    sizes = sizes_ref[...].astype(f32)
    here = lax.broadcasted_iota(jnp.int32, sizes.shape, 1) == image
    size = jnp.sum(jnp.where(here, sizes, 0.0), axis=1, keepdims=True)
    inside = (row.astype(f32) < size[0:1, :]) & (column.astype(f32) < size[1:2, :])
    return jnp.where(inside, 1.0, 0.0).astype(f32)


def wide_column(wide_ref, row, span):
    return jnp.concatenate([wide_ref[row]] * (span // LANES), axis=1)


def first_power(table, half):
    base = half * 256
    rate = jnp.exp(table[base : base + 64])
    freq = table[base + 64 : base + 128]
    damp = jnp.exp(-rate)
    return (
        rate,
        damp * jnp.cos(freq),
        damp * jnp.sin(freq),
        table[base + 128 : base + 192],
        table[base + 192 : base + 256],
    )


def make_taps(params_ref, out_ref):
    table = params_ref[...].T
    for half in range(2):
        _, step_real, step_imag, real, imag = first_power(table, half)
        here_real, here_imag = jnp.ones_like(step_real), jnp.zeros_like(step_real)
        for place in range(S):
            tap = jnp.sum(real * here_real - imag * here_imag, axis=0, keepdims=True)
            out_ref[half, place : place + 1, :] = tap.astype(bf16).astype(f32)
            here_real, here_imag = (
                here_real * step_real - here_imag * step_imag,
                here_real * step_imag + here_imag * step_real,
            )


def taps_back(params_ref, grad_ref, table_ref):
    table = params_ref[...].T
    for half in range(2):
        rate, step_real, step_imag, real, imag = first_power(table, half)
        here_real, here_imag = jnp.ones_like(step_real), jnp.zeros_like(step_real)
        zero = jnp.zeros_like(step_real)
        sum_real, sum_imag, far_real, far_imag = zero, zero, zero, zero
        for place in range(S):
            grad = grad_ref[half * S + place : half * S + place + 1, :]
            wave_real, wave_imag = grad * here_real, grad * here_imag
            sum_real, sum_imag = sum_real + wave_real, sum_imag + wave_imag
            far_real, far_imag = far_real + place * wave_real, far_imag + place * wave_imag
            here_real, here_imag = (
                here_real * step_real - here_imag * step_imag,
                here_real * step_imag + here_imag * step_real,
            )
        base = half * 256
        table_ref[base : base + 64] = -rate * (real * far_real - imag * far_imag)
        table_ref[base + 64 : base + 128] = -(real * far_imag + imag * far_real)
        table_ref[base + 128 : base + 192] = sum_real
        table_ref[base + 192 : base + 256] = -sum_imag


def block_rows(place):
    return slice(place * S, (place + 1) * S)


def causal(source_ref, taps_ref, half, lanes, base=0):
    rows = [source_ref[base + place * S : base + (place + 1) * S, lanes] for place in range(S)]
    for place in range(S):
        total = rows[place] * taps_ref[half, 0:1, lanes]
        for back in range(1, place + 1):
            total += rows[place - back] * taps_ref[half, back : back + 1, lanes]
        yield total


def anticausal(source_ref, taps_ref, half, lanes):
    rows = [source_ref[block_rows(place), lanes] for place in range(S)]
    for place in range(S):
        total = rows[place] * taps_ref[half, 0:1, lanes]
        for ahead in range(1, S - place):
            total += rows[place + ahead] * taps_ref[half, ahead : ahead + 1, lanes]
        yield total


def mixer_kernel(
    sizes_ref, pixels_ref, params_ref, channel_ref, turn_ref, mixed_ref, first_ref, taps_ref, cells_ref, low_ref, wide_ref, *, per_step
):
    @pl.when(pl.program_id(0) == 0)
    def _():
        make_taps(params_ref, taps_ref)

    width = pixels_ref.shape[0]
    for part in range(per_step):
        spot = slice(part * AREA, (part + 1) * AREA)
        mask = image_mask(sizes_ref, pl.program_id(0) * per_step + part)
        masked = (pixels_ref[:, spot].astype(f32) * mask).astype(bf16)
        cells, low, wide = cells_ref.at[part], low_ref.at[part], wide_ref.at[part]
        cells[...] = dot(turn_ref[...], masked, NT)
        for start in range(0, width, LANES):
            lanes = slice(start, start + LANES)
            for place, value in enumerate(causal(cells, taps_ref, 0, lanes)):
                low[block_rows(place), lanes] = value.astype(bf16)
        wide[...] = dot(turn_ref[AREA:, :], low[...])
        first_ref[spot, :] = wide[...].astype(bf16)
        for start in range(0, width, LANES):
            lanes = slice(start, start + LANES)
            skip = channel_ref[2:3, lanes]
            for place, value in enumerate(causal(wide, taps_ref, 1, lanes)):
                own = cells[AREA + place * S : AREA + (place + 1) * S, lanes]
                low[block_rows(place), lanes] = (value + skip * own).astype(bf16)
        mixed_ref[:, spot] = dot(low[...], turn_ref[AREA:, :], TN).astype(bf16)


def mixer_forward(sizes, pixels, mixer_params, channel, turn):
    width, count = pixels.shape
    per_step = 2
    span = per_step * AREA
    in_specs = [
        pl.BlockSpec(sizes.shape, lambda i: (0, 0)),
        pl.BlockSpec((width, span), lambda i: (0, i)),
        pl.BlockSpec(mixer_params.shape, lambda i: (0, 0)),
        pl.BlockSpec(channel.shape, lambda i: (0, 0)),
        pl.BlockSpec(turn.shape, lambda i: (0, 0)),
    ]
    out_specs = [
        pl.BlockSpec((width, span), lambda i: (0, i)),
        pl.BlockSpec((span, width), lambda i: (i, 0)),
        pl.BlockSpec((2, S, width), lambda i: (0, 0, 0)),
    ]
    scratch_shapes = [
        pltpu.VMEM((per_step, 2 * AREA, width), f32),
        pltpu.VMEM((per_step, AREA, width), bf16),
        pltpu.VMEM((per_step, AREA, width), f32),
    ]
    return pl.pallas_call(
        functools.partial(mixer_kernel, per_step=per_step),
        grid=(count // span,),
        in_specs=in_specs,
        out_specs=out_specs,
        scratch_shapes=scratch_shapes,
        out_shape=[
            jax.ShapeDtypeStruct((width, count), bf16),
            jax.ShapeDtypeStruct((count, width), bf16),
            jax.ShapeDtypeStruct((2, S, width), f32),
        ],
        compiler_params=params(),
        cost_estimate=cost(16),
        name="mixer_forward",
    )(sizes, pixels, mixer_params, channel, turn)


GAIN, SHIFT, LAYER = 0, 1, 3


def normalize(
    step,
    place_ref,
    sizes_ref,
    own_ref,
    other_ref,
    own_grad_ref,
    other_grad_ref,
    own_rows_ref,
    other_rows_ref,
    act_ref,
    low_ref,
    stat_ref,
    own_wide,
    other_wide,
):
    width, span = own_ref.shape
    width = 2.0 * width
    mine = place_ref[0]

    @pl.when(step == 0)
    def _():
        for at, row in enumerate((GAIN, SHIFT, LAYER)):
            own_wide[at] = to_column(own_rows_ref[row : row + 1, :])
            other_wide[at] = to_column(other_rows_ref[row : row + 1, :])

    for part in range(span // AREA):
        spot = slice(part * AREA, (part + 1) * AREA)
        mask = image_mask(sizes_ref, step * (span // AREA) + part)
        own, other = own_ref[:, spot].astype(f32), other_ref[:, spot].astype(f32)
        mean = (jnp.sum(own, axis=0, keepdims=True) + jnp.sum(other, axis=0, keepdims=True)) / width
        own, other = own - mean, other - mean
        spread = (
            jnp.sum(own * own, axis=0, keepdims=True) + jnp.sum(other * other, axis=0, keepdims=True)
        ) / width
        scale = lax.rsqrt(spread + EPSILON_NORM)
        stat_ref[0:1, spot] = mean
        stat_ref[1:2, spot] = scale
        for which, value_ref, grad_ref, wide in (
            (mine, own_ref, own_grad_ref, own_wide),
            (1 - mine, other_ref, other_grad_ref, other_wide),
        ):
            value = (value_ref[:, spot].astype(f32) - mean) * scale
            act_ref[which, :, spot] = (
                value * wide_column(wide, 0, AREA) + wide_column(wide, 1, AREA)
            ).astype(bf16)
            grad = grad_ref[:, spot].astype(f32) * mask
            low_ref[which, :, spot] = (grad * wide_column(wide, 2, AREA)).astype(bf16)


def weights_kernel(up_ref, down_ref, up_low_ref, up_turned_ref, down_low_ref, down_turned_ref, square_ref):
    @pl.when(pl.program_id(0) == 0)
    def _():
        square_ref[...] = jnp.zeros_like(square_ref)

    for row, source_ref, low_ref, turned_ref in (
        (0, up_ref, up_low_ref, up_turned_ref),
        (1, down_ref, down_low_ref, down_turned_ref),
    ):
        value = source_ref[...]
        units = square_ref.shape[1]
        for start in range(0, value.shape[1], units):
            part = value[:, start : start + units]
            square_ref[row : row + 1, :] += jnp.sum(part * part, axis=0, keepdims=True)
        low_ref[...] = value.astype(bf16)
        turned_ref[...] = value.T.astype(bf16)


def weights_low(up, down):
    full, hidden_local = up.shape
    units = 384
    column = lambda i: (0, i)
    row = lambda i: (i, 0)
    return pl.pallas_call(
        weights_kernel,
        grid=(hidden_local // units,),
        in_specs=[pl.BlockSpec((full, units), column), pl.BlockSpec((full // 2, full), row)],
        out_specs=[
            pl.BlockSpec((full, units), column),
            pl.BlockSpec((units, full), row),
            pl.BlockSpec((units, full), row),
            pl.BlockSpec((full, units), column),
            pl.BlockSpec((8, units), lambda i: (0, 0)),
        ],
        out_shape=[
            jax.ShapeDtypeStruct((full, hidden_local), bf16),
            jax.ShapeDtypeStruct((hidden_local, full), bf16),
            jax.ShapeDtypeStruct((hidden_local, full), bf16),
            jax.ShapeDtypeStruct((full, hidden_local), bf16),
            jax.ShapeDtypeStruct((8, units), f32),
        ],
        compiler_params=params(),
        cost_estimate=cost(8),
        name="weights_low",
    )(up, down)


def gelu_pair(pre):
    bell = jnp.exp2(pre * pre * (-0.5 * LOG2_E))
    part = pl.reciprocal(1.0 + (ERF_P * HALF_ROOT) * jnp.abs(pre), approx=True)
    poly = 0.5 * ERF_A[4]
    for factor in ERF_A[3::-1]:
        poly = poly * part + 0.5 * factor
    tail = poly * part * bell
    upper = jnp.where(pre >= 0.0, 1.0 - tail, tail)
    return pre * upper, upper + pre * bell * DENSITY


def split_out(source_ref, digit, part_refs):
    rows = part_refs[0].shape[0]
    for away, ref in enumerate(part_refs):
        start = pl.multiple_of((digit ^ away) * rows, rows)
        ref[...] = source_ref[pl.ds(start, rows), :].astype(ref.dtype)


def chunk_kernel(place_ref, *refs, first):
    step = pl.program_id(0)
    if first:
        ins, (up_ref, down_ref, bias_ref) = refs[:7], refs[7:10]
        refs, outs, wide = refs[10:-5], refs[-5:-2], refs[-2:]
        normalize(step, place_ref, *ins, *outs, *wide)
        act_ref, low_ref, _ = outs
    else:
        act_ref, low_ref, up_ref, down_ref, bias_ref = refs[:5]
        refs = refs[7:]
    hidden_ref, slope_ref, bias_grad_ref = refs[:3]
    part_refs, (grad_acc, bias_acc, bias_wide) = refs[3 : 3 + PLANE], refs[3 + PLANE :]

    @pl.when(step == 0)
    def _():
        grad_acc[...] = jnp.zeros_like(grad_acc)
        bias_acc[...] = jnp.zeros_like(bias_acc)
        bias_wide[...] = to_column(bias_ref[...].astype(bf16).astype(f32))

    halves, width, span = act_ref.shape
    units = up_ref.shape[0]
    full = halves * width
    tile = 256
    tiles = [(row, start) for start in range(0, span, tile) for row in range(0, units, tile)]

    def products(row, start):
        rows, spot = slice(row, row + tile), slice(start, start + tile)
        pre = dot(up_ref[rows, :], act_ref[:, :, spot].reshape(full, tile))
        pre += jnp.concatenate([bias_wide[rows, :]] * (tile // LANES), axis=1)
        return pre, dot(down_ref[rows, :], low_ref[:, :, spot].reshape(full, tile))

    ready = products(*tiles[0])
    for at, (row, start) in enumerate(tiles):
        pre, back = ready
        if at + 1 < len(tiles):
            ready = products(*tiles[at + 1])
        rows, spot = slice(row, row + tile), slice(start, start + tile)
        hidden, slope = gelu_pair(pre)
        hidden_ref[rows, spot] = hidden.astype(bf16)
        slope_ref[rows, spot] = (back * slope).astype(bf16)
    grad_acc[:units, :] += dot(slope_ref[...], act_ref[...].reshape(full, span), NT)
    grad_acc[units:, :] += dot(hidden_ref[...], low_ref[...].reshape(full, span), NT)
    bias_acc[...] += dot(jnp.ones((S, span), bf16), slope_ref[...], NT)

    @pl.when(step == pl.num_programs(0) - 1)
    def _():
        split_out(grad_acc, place_ref[1], part_refs)
        bias_grad_ref[...] = bias_acc[0:8, :]


def feed_chunk(chunk, place, inputs, up_turned, down, bias, earlier):
    hidden_local, full = down.shape
    units = hidden_local // CHUNKS
    width = full // 2
    span = 512
    count = inputs[1].shape[-1]
    pair = pl.BlockSpec((2, width, span), lambda i, *_: (0, 0, i))
    block = pl.BlockSpec((width, span), lambda i, *_: (0, i))
    weight = pl.BlockSpec((units, full), lambda i, *_: (chunk, 0))
    wide = pl.BlockSpec((units, span), lambda i, *_: (chunk, i))
    whole = lambda i, *_: (0, 0)
    rows = 2 * units // PLANE
    in_specs = [pair, pair]
    if chunk == 0:
        small = [pl.BlockSpec(array.shape, whole) for array in (inputs[0], *inputs[-2:])]
        in_specs = [small[0], block, block, block, block, small[1], small[2]]
    in_specs += [weight, weight, pl.BlockSpec((1, units), lambda i, *_: (0, chunk))]
    in_specs += [pl.BlockSpec(memory_space=pl.ANY)] * len(earlier)
    out_specs = [wide, wide, pl.BlockSpec((8, units), whole)] + [pl.BlockSpec((rows, full), whole)] * PLANE
    out_shape = [
        jax.ShapeDtypeStruct((hidden_local, count), bf16),
        jax.ShapeDtypeStruct((hidden_local, count), bf16),
        jax.ShapeDtypeStruct((8, units), f32),
        jax.ShapeDtypeStruct((rows, full), f32),
    ] + [jax.ShapeDtypeStruct((rows, full), bf16)] * (PLANE - 1)
    scratch_shapes = [
        pltpu.VMEM((2 * units, full), f32),
        pltpu.VMEM((S, units), f32),
        pltpu.VMEM((units, LANES), f32),
    ]
    if chunk == 0:
        out_specs += [pair, pair, pl.BlockSpec((8, span), lambda i, *_: (0, i))]
        out_shape += [jax.ShapeDtypeStruct((2, width, count), bf16)] * 2 + [jax.ShapeDtypeStruct((8, count), f32)]
        scratch_shapes += [pltpu.VMEM((3, width, LANES), f32)] * 2

    def body(*refs):
        if chunk == 0:
            made = len(in_specs) + 1 + len(out_specs)
            outs = refs[made - 3 : made]
            refs = (*refs[: made - 3], *refs[made:-2], *outs, *refs[-2:])
        chunk_kernel(*refs, first=chunk == 0)

    return pl.pallas_call(
        body,
        grid_spec=pltpu.PrefetchScalarGridSpec(
            num_scalar_prefetch=1,
            grid=(count // span,),
            in_specs=in_specs,
            out_specs=out_specs,
            scratch_shapes=scratch_shapes,
        ),
        out_shape=out_shape,
        input_output_aliases={6: 0, 7: 1} if earlier else {},
        compiler_params=params(),
        cost_estimate=cost(40),
        name="feed_chunk_%d" % chunk,
    )(place, *inputs, up_turned, down, bias, *earlier)


def across(value, stride):
    size = lax.axis_size("line") * PLANE
    return lax.ppermute(value, ("line", "plane"), [(i, i ^ stride) for i in range(size)])


def along(value, axis, away):
    return lax.ppermute(value, axis, [(i, i ^ away) for i in range(lax.axis_size(axis))])


class GradientSum:
    def __init__(self, kept, sends):
        self.kept = kept
        self.got = [along(value, "plane", away) for away, value in enumerate(sends, 1)]

    def add(self):
        total = self.kept
        for value in self.got:
            total = total + value.astype(f32)
        return total

    def to_line(self):
        size = lax.axis_size("line")
        total = self.add()
        parts = total.reshape(size, -1, total.shape[1])

        def part(away):
            return lax.dynamic_index_in_dim(parts, lax.axis_index("line") ^ away, 0, keepdims=False)

        self.kept = part(0)
        self.sends = [part(away).astype(bf16) for away in range(1, size)]
        self.got = [along(value, "line", away) for away, value in enumerate(self.sends, 1)]

    def to_piece(self):
        self.piece = self.add().astype(bf16)

    def gather(self):
        self.to_piece()
        self.sum = lax.all_gather(self.piece, ("plane", "line"), axis=0, tiled=True)

    def gather_line(self):
        self.to_piece()
        size = lax.axis_size("line")
        self.pieces = [self.piece] + [along(self.piece, "line", away) for away in range(1, size)]

    def gather_plane(self):
        self.quarter = jnp.concatenate(self.pieces)
        self.quarters = [self.quarter] + [along(self.quarter, "plane", away) for away in range(1, PLANE)]


EXTRA = 16


def sums_kernel(
    place_ref,
    hidden_ref,
    slope_ref,
    down_ref,
    up_ref,
    own_ref,
    other_ref,
    stat_ref,
    own_rows_ref,
    other_rows_ref,
    *refs,
    skipped,
):
    own_proj_ref, own_act_ref, sum_ref, send_ref = refs[skipped : skipped + 4]
    own_wide, other_wide = refs[-2:]
    width, span = own_ref.shape
    mine = place_ref[0]
    own_rows = pl.ds(pl.multiple_of(mine * width, width), width)
    other_rows = pl.ds(pl.multiple_of((1 - mine) * width, width), width)

    @pl.when(pl.program_id(0) == 0)
    def _():
        own_wide[0] = to_column(own_rows_ref[0:1, :])
        other_wide[0] = to_column(other_rows_ref[0:1, :])

    own_proj_ref[...] = dot(down_ref[own_rows, :], hidden_ref[...]).astype(bf16)
    send_ref[0:width, :] = dot(down_ref[other_rows, :], hidden_ref[...]).astype(bf16)
    mean, scale = stat_ref[0:1, :], stat_ref[1:2, :]
    sums = []
    for own, rows, value_ref, wide in (
        (True, own_rows, own_ref, own_wide),
        (False, other_rows, other_ref, other_wide),
    ):
        act = dot(up_ref[rows, :], slope_ref[...])
        if own:
            own_act_ref[...] = act
        else:
            send_ref[width : 2 * width, :] = act.astype(bf16)
        act = act * wide_column(wide, 0, span)
        normed = (value_ref[...].astype(f32) - mean) * scale
        sums.append(jnp.sum(act, axis=0, keepdims=True))
        sums.append(jnp.sum(act * normed, axis=0, keepdims=True))
    plain, tilt = sums[0] + sums[2], sums[1] + sums[3]
    sum_ref[0:1, :] = plain
    sum_ref[1:2, :] = tilt
    parts = []
    for value in (plain, tilt):
        high = value.astype(bf16).astype(f32)
        parts += [high, value - high]
    parts.append(jnp.zeros((EXTRA - 4, span), f32))
    send_ref[2 * width :, :] = jnp.concatenate(parts, axis=0).astype(bf16)


def hidden_sums(place, hidden, slopes, down_turned, up, own, other, stat, own_rows, other_rows, part, tokens, riders):
    width, total = own.shape
    count = total // SUM_PARTS
    hidden_local = hidden.shape[0]
    span = 512
    base = part * (count // span)
    column = lambda i, *_: (0, base + i)
    out = lambda i, *_: (0, i)
    fixed = lambda i, *_: (0, 0)
    wide = pl.BlockSpec((hidden_local, span), column)
    block = pl.BlockSpec((width, span), column)
    result = pl.BlockSpec((width, span), out)
    rows = pl.BlockSpec(own_rows.shape, fixed)
    sent = 2 * width + EXTRA
    grid_spec = pltpu.PrefetchScalarGridSpec(
        num_scalar_prefetch=1,
        grid=(count // span,),
        in_specs=[
            wide,
            wide,
            pl.BlockSpec(down_turned.shape, fixed),
            pl.BlockSpec(up.shape, fixed),
            block,
            block,
            pl.BlockSpec((8, span), column),
            rows,
            rows,
        ]
        + [pl.BlockSpec(memory_space=pl.ANY)] * (len(riders) + len(tokens)),
        out_specs=[result, result, pl.BlockSpec((8, span), out), pl.BlockSpec((sent, span), out)]
        + [pl.BlockSpec(memory_space=pl.ANY)] * len(riders),
        scratch_shapes=[pltpu.VMEM((1, width, LANES), f32)] * 2,
    )
    values = pl.pallas_call(
        functools.partial(sums_kernel, skipped=len(riders) + len(tokens)),
        grid_spec=grid_spec,
        out_shape=[
            jax.ShapeDtypeStruct((width, count), bf16),
            jax.ShapeDtypeStruct((width, count), f32),
            jax.ShapeDtypeStruct((8, count), f32),
            jax.ShapeDtypeStruct((sent, count), bf16),
        ]
        + [jax.ShapeDtypeStruct(rider.shape, rider.dtype) for rider in riders],
        input_output_aliases={10 + at: 4 + at for at in range(len(riders))},
        compiler_params=params(),
        cost_estimate=cost(40 / SUM_PARTS * 2),
        name="hidden_sums_%d" % part,
    )(place, hidden, slopes, down_turned, up, own, other, stat, own_rows, other_rows, *riders, *tokens)
    return values[:3], values[3], values[4:]


TAPS, ROWS, BIAS = 0, 32, 40
PER_STEP = 2


def correlate(left_ref, right_ref, sum_ref, half, lanes):
    left = [left_ref[block_rows(place), lanes] for place in range(S)]
    right = [right_ref[block_rows(place), lanes].astype(f32) for place in range(S)]
    for back in range(S):
        total = left[back] * right[0]
        for place in range(back + 1, S):
            total += left[place] * right[place - back]
        sum_ref[half, block_rows(back), lanes] += total


def backward_kernel(
    sizes_ref,
    pixels_ref,
    grad_ref,
    mixed_ref,
    first_ref,
    stat_ref,
    own_proj_ref,
    own_act_ref,
    own_sum_ref,
    got_ref,
    rows_ref,
    taps_ref,
    turn_ref,
    *refs,
    base,
    carries,
    skipped,
):
    carry_refs, refs = refs[:carries], refs[carries:]
    out_ref, pixel_grad_ref, small_ref = refs[skipped : skipped + 3]
    sum_ref, channel_sum, cells_ref, low_ref, wide_ref, back_ref, columns = refs[-7:]
    step = pl.program_id(0)
    width = pixels_ref.shape[0]
    full = 2.0 * width

    @pl.when(step == 0)
    def _():
        sum_ref[...] = jnp.zeros_like(sum_ref)
        channel_sum[...] = jnp.zeros_like(channel_sum)
        for row in (0, 2, 3, 4):
            columns[row] = to_column(rows_ref[row : row + 1, :])

    gain, skip, layer, shift = (wide_column(columns, row, AREA) for row in (0, 2, 3, 4))

    def gather(row, value):
        channel_sum[row] += value[:, :LANES] + value[:, LANES:]

    for part in range(PER_STEP):
        spot = slice(part * AREA, (part + 1) * AREA)
        mask = image_mask(sizes_ref, base + step * PER_STEP + part)
        pixels = pixels_ref[:, spot].astype(f32)
        grad = grad_ref[:, spot].astype(f32)
        masked = pixels * mask
        masked_grad = grad * mask
        branch = own_proj_ref[:, spot].astype(f32) + got_ref[0:width, spot].astype(f32) + shift
        out_ref[:, spot] = pixels + mask * layer * branch
        gather(3, masked_grad * branch)
        gather(4, masked_grad)

        scale = stat_ref[1:2, spot]
        normed = (mixed_ref[:, spot].astype(f32) - stat_ref[0:1, spot]) * scale
        act = own_act_ref[:, spot] + got_ref[width : 2 * width, spot].astype(f32)
        gather(0, act * normed)
        gather(1, act)
        got = got_ref[2 * width :, spot].astype(f32)
        plain = (own_sum_ref[0:1, spot] + (got[0:1, :] + got[1:2, :])) / full
        tilt = (own_sum_ref[1:2, spot] + (got[2:3, :] + got[3:4, :])) / full
        mixed_low = (scale * (act * gain - plain - normed * tilt)).astype(bf16)
        mixed_grad = mixed_low.astype(f32)
        gather(2, mixed_grad * masked)

        cells, low, wide, back = cells_ref.at[part], low_ref.at[part], wide_ref.at[part], back_ref.at[part]
        cells[...] = dot(turn_ref[:AREA, :], masked.astype(bf16), NT)
        wide[...] = dot(turn_ref[AREA:, :], mixed_low, NT)
        for start in range(0, width, LANES):
            lanes = slice(start, start + LANES)
            for place, value in enumerate(anticausal(wide, taps_ref, 1, lanes)):
                low[block_rows(place), lanes] = value.astype(bf16)
            correlate(wide, first_ref.at[spot], sum_ref, 1, lanes)
        back[...] = dot(turn_ref[AREA:, :], low[...])
        for start in range(0, width, LANES):
            lanes = slice(start, start + LANES)
            for place, value in enumerate(anticausal(back, taps_ref, 0, lanes)):
                wide[block_rows(place), lanes] = value
            correlate(back, cells, sum_ref, 0, lanes)
        pixel_grad_ref[:, spot] = grad + mask * (wide[...].T + skip * mixed_grad)

    @pl.when(step == pl.num_programs(0) - 1)
    def _():
        if base > 0:
            small_ref[...] = carry_refs[0][...]
        else:
            small_ref[...] = jnp.zeros_like(small_ref)
            row = BIAS
            for ref in carry_refs:
                for start in range(0, ref.shape[1], width):
                    small_ref[row : row + 1, :] = ref[0:1, start : start + width]
                    row += 1
        for half in range(2):
            for back in range(S):
                row = TAPS + half * S + back
                small_ref[row : row + 1, :] += jnp.sum(
                    sum_ref[half, block_rows(back), :], axis=0, keepdims=True
                )
        for row in range(5):
            small_ref[ROWS + row : ROWS + row + 1, :] += jnp.sum(channel_sum[row].T, axis=0, keepdims=True)


def backward(sizes, pixels, grad, mixed, mid, stat, own, got, rows, taps, turn, carries, part, earlier, riders, tokens):
    own_proj, own_act, own_sum = own
    width, total = pixels.shape
    base, count = (at * (total // S) for at in part)
    span = PER_STEP * AREA
    at = base // span
    inner = at % (own_proj.shape[1] // span)
    column = lambda i: (0, at + i)
    here = lambda i: (0, inner + i)
    fixed = lambda i: (0, 0)
    block = pl.BlockSpec((width, span), column)
    local = pl.BlockSpec((width, span), here)
    anywhere = pl.BlockSpec(memory_space=pl.ANY)
    base //= AREA
    in_specs = [
        pl.BlockSpec(sizes.shape, fixed),
        block,
        block,
        block,
        pl.BlockSpec((span, width), lambda i: (at + i, 0)),
        pl.BlockSpec((8, span), column),
        local,
        local,
        pl.BlockSpec((8, span), here),
        pl.BlockSpec((got.shape[0], span), here),
        pl.BlockSpec(rows.shape, fixed),
        pl.BlockSpec(taps.shape, lambda i: (0, 0, 0)),
        pl.BlockSpec(turn.shape, fixed),
    ]
    in_specs += [pl.BlockSpec(carry.shape, fixed) for carry in carries]
    in_specs += [anywhere] * (len(earlier) + len(riders) + len(tokens))
    first = 13 + len(carries)
    small = (BIAS + 8, width)
    return pl.pallas_call(
        functools.partial(backward_kernel, base=base, carries=len(carries), skipped=len(earlier) + len(riders) + len(tokens)),
        grid=(count // span,),
        in_specs=in_specs,
        out_specs=[block, block, pl.BlockSpec(small, fixed)] + [anywhere] * len(riders),
        scratch_shapes=[
            pltpu.VMEM((2, AREA, width), f32),
            pltpu.VMEM((5, width, LANES), f32),
            pltpu.VMEM((PER_STEP, AREA, width), f32),
            pltpu.VMEM((PER_STEP, AREA, width), bf16),
            pltpu.VMEM((PER_STEP, AREA, width), f32),
            pltpu.VMEM((PER_STEP, AREA, width), f32),
            pltpu.VMEM((5, width, LANES), f32),
        ],
        out_shape=[
            jax.ShapeDtypeStruct((width, total), f32),
            jax.ShapeDtypeStruct((width, total), f32),
            jax.ShapeDtypeStruct(small, f32),
        ]
        + [jax.ShapeDtypeStruct(rider.shape, rider.dtype) for rider in riders],
        input_output_aliases={first + at: at for at in range(len(earlier))}
        | {first + len(earlier) + at: 3 + at for at in range(len(riders))},
        compiler_params=params(),
        cost_estimate=cost(90 * part[1] / S),
        name="backward_%d" % base,
    )(
        sizes, pixels, grad, mixed, mid, stat, own_proj, own_act, own_sum, got, rows, taps, turn, *carries, *earlier, *riders, *tokens
    )


UP_ROW, UP_MASS, DOWN_COL, DOWN_MASS, MIXER_COL, MIXER_MASS, SCALARS = range(7)


def fold(value):
    total = value[:, :LANES]
    for start in range(LANES, value.shape[1], LANES):
        total += value[:, start : start + LANES]
    return total


def as_row(ref):
    return ref[...].reshape(1, ref.shape[0])


def to_flat(ref, value):
    ref[...] = value.reshape(ref.shape[0])


def to_column(row):
    return jnp.broadcast_to(row, (LANES, row.shape[1])).T


def to_row(columns):
    return jnp.sum(columns.T, axis=0, keepdims=True)


def statistics_kernel(place_ref, *refs, quarters, skipped, line_parts):
    sources, refs = refs[:quarters], refs[quarters:]
    up_old_ref, down_old_ref, carry_ref = refs[:3]
    up_ref, down_ref, up_new_ref, down_new_ref, stat_ref = refs[3 + skipped : 8 + skipped]
    quarter_ref = refs[-1]
    step = pl.program_id(0)
    plane, line = place_ref[1], place_ref[2]
    steps = PLANE // 2

    @pl.when(step == 0)
    def _():
        stat_ref[...] = carry_ref[...]

    for kind, old_ref, new_ref, columns, mass in (
        (0, up_old_ref, up_new_ref, UP_ROW, UP_MASS),
        (1, down_old_ref, down_new_ref, DOWN_COL, DOWN_MASS),
    ):
        if quarters == 2:
            value = sources[kind][...].astype(f32)
        else:
            for away, source_ref in enumerate(sources):

                @pl.when((kind * steps + step) ^ plane == away)
                def _():
                    rows = quarter_ref.shape[0] // line_parts

                    def move(at, _):
                        target = pl.ds(pl.multiple_of(at * rows, rows), rows)
                        source = pl.ds(pl.multiple_of((at ^ line) * rows, rows), rows)
                        quarter_ref[target, :] = source_ref[source, :].astype(f32)
                        return 0

                    lax.fori_loop(0, line_parts, move, 0)

            value = quarter_ref[...]
        if kind == 0:
            up_ref[...] = value.T
        else:
            down_ref[...] = value
        square = value * value
        mean = jnp.sum(fold(square), axis=1, keepdims=True) / value.shape[1]
        fresh = DECAY * to_column(old_ref[...]) + FRESH * (mean + EPSILON_SQUARE)
        new_ref[...] = fresh.T[0:1, :]
        stat_ref[columns : columns + 1, : value.shape[1]] += jnp.sum(square, axis=0, keepdims=True)
        stat_ref[mass : mass + 1, : value.shape[1]] += jnp.sum(
            square * (1.0 / fresh[:, 0:1]), axis=0, keepdims=True
        )


def statistics(chunk, place, sources, up_cols, down_rows, carry, earlier, rider, tokens):
    hidden_local = up_cols.shape[1]
    units = hidden_local // CHUNKS
    full = sources[0].shape[1]
    rows = 2 * units // PLANE
    steps = PLANE // 2
    base = chunk * steps
    row = pl.BlockSpec((1, rows), lambda i: (0, base + i))
    anywhere = pl.BlockSpec(memory_space=pl.ANY)
    fixed = pl.BlockSpec(carry.shape, lambda i: (0, 0))
    if len(sources) == 2:
        specs = [
            pl.BlockSpec((rows, full), lambda i: (i, 0)),
            pl.BlockSpec((rows, full), lambda i: (steps + i, 0)),
        ]
    else:
        specs = [pl.BlockSpec((rows, full), lambda i: (0, 0))] * PLANE
    first = 4 + len(sources)
    return pl.pallas_call(
        functools.partial(statistics_kernel, quarters=len(sources), skipped=len(earlier) + 1 + len(tokens), line_parts=lax.axis_size("line")),
        grid=(steps,),
        in_specs=[pl.BlockSpec(memory_space=pltpu.SMEM)]
        + specs
        + [row, row, fixed]
        + [anywhere] * (len(earlier) + 1 + len(tokens)),
        out_specs=[
            pl.BlockSpec((full, rows), lambda i: (0, base + i)),
            pl.BlockSpec((rows, full), lambda i: (base + i, 0)),
            row,
            row,
            fixed,
            anywhere,
        ],
        out_shape=[
            jax.ShapeDtypeStruct((full, hidden_local), f32),
            jax.ShapeDtypeStruct((hidden_local, full), f32),
            jax.ShapeDtypeStruct((1, hidden_local), f32),
            jax.ShapeDtypeStruct((1, hidden_local), f32),
            jax.ShapeDtypeStruct(carry.shape, f32),
            jax.ShapeDtypeStruct(rider.shape, rider.dtype),
        ],
        input_output_aliases={first + at: at for at in range(len(earlier))} | {first + len(earlier): 5},
        scratch_shapes=[pltpu.VMEM((rows, full), f32)],
        compiler_params=params(),
        cost_estimate=cost(20),
        name="statistics_%d" % chunk,
    )(place, *sources, up_cols, down_rows, carry, *earlier, rider, *tokens)


def small_kernel(
    sum_ref,
    stat_ref,
    square_ref,
    params_ref,
    channel_ref,
    moment_ref,
    bias_ref,
    bias_moment_ref,
    rows_ref,
    down_rows_new_ref,
    mixer_grad_ref,
    rows_new_ref,
    channel_grad_ref,
    moment_new_ref,
    channel_update_ref,
    bias_grad_ref,
    bias_moment_new_ref,
    bias_update_ref,
    out_ref,
    channel_square_ref,
    table_ref,
):
    out_ref[...] = stat_ref[...]
    taps_back(params_ref, sum_ref, table_ref)
    grad = table_ref[...].T
    mixer_grad_ref[...] = grad
    states = grad.shape[1]
    square = grad * grad
    mean = jnp.sum(fold(square), axis=1, keepdims=True) / states
    fresh = DECAY * to_column(as_row(rows_ref)) + FRESH * (mean + EPSILON_SQUARE)
    rows_new = fresh.T[0:1, :]
    rows_new_ref[...] = rows_new
    out_ref[MIXER_COL : MIXER_COL + 1, :states] = jnp.sum(square, axis=0, keepdims=True)
    out_ref[MIXER_MASS : MIXER_MASS + 1, :states] = jnp.sum(square * (1.0 / fresh[:, 0:1]), axis=0, keepdims=True)

    layer = channel_ref[3:4, :]
    channel_grad_ref[0:4, :] = sum_ref[ROWS : ROWS + 4, :]
    channel_grad_ref[4:5, :] = sum_ref[ROWS + 4 : ROWS + 5, :] * layer
    grad = channel_grad_ref[...]
    moment = DECAY * moment_ref[...] + FRESH * (grad * grad + EPSILON_SQUARE)
    moment_new_ref[...] = moment
    channel_update = grad * lax.rsqrt(moment)
    channel_update_ref[...] = channel_update

    width = layer.shape[1]
    for at in range(bias_grad_ref.shape[1] // width):
        bias_grad_ref[:, at * width : (at + 1) * width] = sum_ref[BIAS + at : BIAS + at + 1, :]
    grad = bias_grad_ref[...]
    moment = DECAY * as_row(bias_moment_ref) + FRESH * (grad * grad + EPSILON_SQUARE)
    bias_moment_new_ref[...] = moment
    bias_update = grad * lax.rsqrt(moment)
    bias_update_ref[...] = bias_update

    def total(value):
        return jnp.sum(value, keepdims=True)

    channel = channel_ref[...]
    table = params_ref[...]
    bias = as_row(bias_ref)
    scalars = (
        total(channel_update * channel_update) + total(bias_update * bias_update),
        total(down_rows_new_ref[...]),
        total(rows_new),
        total(square_ref[0:1, :]),
        total(square_ref[1:2, :]),
        total(table * table),
        total(bias * bias),
    )
    for at, value in enumerate(scalars):
        out_ref[SCALARS : SCALARS + 1, at * LANES : (at + 1) * LANES] = jnp.broadcast_to(value, (1, LANES))
    channel_square_ref[...] = jnp.broadcast_to(jnp.sum(channel * channel, axis=1, keepdims=True), (5, LANES))


def small_update(total, stat, square, mixer_params, channel_params, channel_moment, bias, bias_moment, rows, down_rows_new):
    width, states = mixer_params.shape
    shapes = [
        (width, states),
        (1, width),
        channel_params.shape,
        channel_params.shape,
        channel_params.shape,
        (1, bias.shape[0]),
        (1, bias.shape[0]),
        (1, bias.shape[0]),
        (8, 8 * LANES),
        (5, LANES),
    ]
    return pl.pallas_call(
        small_kernel,
        out_shape=[jax.ShapeDtypeStruct(shape, f32) for shape in shapes],
        scratch_shapes=[pltpu.VMEM((states, width), f32)],
        compiler_params=params(),
        cost_estimate=cost(5),
        name="small_update",
    )(total, stat, square, mixer_params, channel_params, channel_moment, bias, bias_moment, rows, down_rows_new)


def update_kernel(
    stat_ref,
    got_ref,
    channel_square_ref,
    channel_got_ref,
    up_rows_ref,
    down_cols_ref,
    mixer_cols_ref,
    up_cols_new_ref,
    down_rows_new_ref,
    up_grad_ref,
    up_ref,
    up_average_ref,
    down_grad_ref,
    down_ref,
    down_average_ref,
    mixer_grad_ref,
    mixer_ref,
    mixer_average_ref,
    mixer_rows_new_ref,
    channel_ref,
    channel_average_ref,
    channel_update_ref,
    bias_ref,
    bias_average_ref,
    bias_update_ref,
    bias_grad_ref,
    bias_moment_ref,
    up_cols_all_ref,
    down_rows_all_ref,
    rms_ref,
    up_rows_new_ref,
    down_cols_new_ref,
    mixer_cols_new_ref,
    up_new_ref,
    up_average_new_ref,
    down_new_ref,
    down_average_new_ref,
    mixer_new_ref,
    mixer_average_new_ref,
    channel_new_ref,
    channel_average_new_ref,
    bias_new_ref,
    bias_average_new_ref,
    bias_grad_out_ref,
    bias_moment_out_ref,
    up_cols_out_ref,
    down_rows_out_ref,
    mixer_rows_out_ref,
    left_ref,
):
    full, hidden = up_rows_ref.shape[0], 2 * bias_ref.shape[0]
    states = mixer_cols_ref.shape[0]

    def stat(row, size):
        return stat_ref[row : row + 1, :size] + got_ref[row : row + 1, :size]

    def scalar(at):
        return stat(SCALARS, 8 * LANES)[:, at * LANES : at * LANES + 1]

    def total(value):
        return jnp.sum(value, axis=1, keepdims=True)

    up_rows_new = DECAY * as_row(up_rows_ref) + FRESH * (stat(UP_ROW, full) / hidden + EPSILON_SQUARE)
    down_cols_new = DECAY * as_row(down_cols_ref) + FRESH * (stat(DOWN_COL, full) / hidden + EPSILON_SQUARE)
    mixer_cols_new = DECAY * as_row(mixer_cols_ref) + FRESH * (stat(MIXER_COL, states) / full + EPSILON_SQUARE)
    up_mean = total(up_rows_new) / full
    down_mean = scalar(1) / hidden
    mixer_mean = scalar(2) / full
    square = (
        scalar(0)
        + up_mean * total(stat(UP_MASS, full) / up_rows_new)
        + down_mean * total(stat(DOWN_MASS, full) / down_cols_new)
        + mixer_mean * total(stat(MIXER_MASS, states) / mixer_cols_new)
    )
    rms = jnp.sqrt(square / (2 * full * hidden + states * full + 5 * full + hidden))
    factor = LEARN_RATE * CLIP_LEVEL / jnp.maximum(CLIP_LEVEL, rms)

    def rate(squares, size):
        return factor * jnp.maximum(EPSILON_SCALE, jnp.sqrt(squares / size))

    def settle(weight, change, average_ref, new_ref, average_new_ref):
        new = weight - change
        new_ref[...] = new
        average_new_ref[...] = AVERAGE_KEEP * average_ref[...] + (1.0 - AVERAGE_KEEP) * new

    def column(row):
        return to_column(row)[:, 0:1]

    up_speed = rate(scalar(3), full * hidden) * jnp.sqrt(up_mean)
    rows = up_ref.shape[0]
    left_ref[...] = lax.rsqrt(up_rows_new) * up_speed
    here = pl.ds(pl.multiple_of(pl.program_id(0) * rows, rows), rows)
    settle(
        up_ref[...],
        up_grad_ref[...] * column(left_ref[:, here]) * lax.rsqrt(up_cols_new_ref[...]),
        up_average_ref,
        up_new_ref,
        up_average_new_ref,
    )
    down_speed = rate(scalar(4), full * hidden) * jnp.sqrt(down_mean)
    settle(
        down_ref[...],
        down_grad_ref[...] * column(lax.rsqrt(down_rows_new_ref[...]) * down_speed) * lax.rsqrt(down_cols_new),
        down_average_ref,
        down_new_ref,
        down_average_new_ref,
    )

    @pl.when(pl.program_id(0) == 0)
    def _():
        rms_ref[...] = rms
        to_flat(up_rows_new_ref, up_rows_new)
        to_flat(down_cols_new_ref, down_cols_new)
        to_flat(mixer_cols_new_ref, mixer_cols_new)
        to_flat(bias_grad_out_ref, bias_grad_ref[...])
        to_flat(bias_moment_out_ref, bias_moment_ref[...])
        to_flat(up_cols_out_ref, up_cols_all_ref[...])
        to_flat(down_rows_out_ref, down_rows_all_ref[...])
        to_flat(mixer_rows_out_ref, mixer_rows_new_ref[...])
        mixer_speed = rate(scalar(5), states * full) * jnp.sqrt(mixer_mean)
        settle(
            mixer_ref[...],
            mixer_grad_ref[...]
            * column(lax.rsqrt(mixer_rows_new_ref[...]) * mixer_speed)
            * lax.rsqrt(mixer_cols_new),
            mixer_average_ref,
            mixer_new_ref,
            mixer_average_new_ref,
        )
        channel_square = channel_square_ref[:, 0:1] + channel_got_ref[:, 0:1]
        settle(
            channel_ref[...],
            rate(channel_square, full) * channel_update_ref[...],
            channel_average_ref,
            channel_new_ref,
            channel_average_new_ref,
        )
        bias_new = as_row(bias_ref) - rate(scalar(6), hidden) * bias_update_ref[...]
        to_flat(bias_new_ref, bias_new)
        to_flat(
            bias_average_new_ref, AVERAGE_KEEP * as_row(bias_average_ref) + (1.0 - AVERAGE_KEEP) * bias_new
        )


def final_update(operands, units):
    up, mixer, channel, bias = operands[10], operands[16], operands[19], operands[22]
    full, hidden_local = up.shape
    steps = hidden_local // units
    up_block = pl.BlockSpec((full // steps, hidden_local), lambda i: (i, 0))
    down_block = pl.BlockSpec((units, full), lambda i: (i, 0))
    row_block = pl.BlockSpec((1, units), lambda i: (0, i))

    def whole(array):
        return pl.BlockSpec(array.shape, lambda i: (0,) * len(array.shape))

    in_specs = [whole(array) for array in operands]
    in_specs[8] = row_block
    in_specs[9:12] = [up_block] * 3
    in_specs[12:15] = [down_block] * 3
    shapes = [(1, 1), operands[4].shape, operands[5].shape, operands[6].shape]
    shapes += [up.shape] * 2 + [(hidden_local, full)] * 2 + [mixer.shape] * 2 + [channel.shape] * 2 + [bias.shape] * 2
    shapes += [bias.shape] * 4 + [operands[18].shape[1:]]
    out_specs = [whole(jax.ShapeDtypeStruct(shape, f32)) for shape in shapes]
    out_specs[4:8] = [up_block, up_block, down_block, down_block]
    return pl.pallas_call(
        update_kernel,
        grid=(steps,),
        in_specs=in_specs,
        out_specs=out_specs,
        out_shape=[jax.ShapeDtypeStruct(shape, f32) for shape in shapes],
        scratch_shapes=[pltpu.VMEM((1, full), f32)],
        compiler_params=params(),
        cost_estimate=cost(19),
        name="final_update",
    )(*operands)


def turn_table():
    place = np.arange(AREA)
    swapped = (place % S) * S + place // S
    table = np.concatenate([place[:, None] == place[None, :], swapped[:, None] == place[None, :]])
    return table.astype(ml_dtypes.bfloat16)


def shards(
    pixels,
    image_sizes,
    out_grad,
    up_weight,
    down_weight,
    mixer_params,
    channel_params,
    hidden_bias,
    up_rows,
    up_cols,
    down_rows,
    down_cols,
    mixer_rows,
    mixer_cols,
    channel_moment,
    bias_moment,
    up_average,
    down_average,
    mixer_average,
    channel_average,
    bias_average,
):
    width_local, count = pixels.shape
    hidden_local = up_weight.shape[1]
    place = jnp.stack([lax.axis_index(axis) for axis in ("ch", "plane", "line")]).astype(jnp.int32)

    def exchange(value):
        return lax.ppermute(value, "ch", [(0, 1), (1, 0)])

    def row(value):
        return value.reshape(1, -1)

    other_grad = exchange(out_grad)
    rounded = jnp.concatenate(
        [channel_params[0:2].astype(bf16).astype(f32), channel_params[2:5], jnp.zeros((3, width_local), f32)]
    )
    others = exchange(rounded)
    turn = jnp.asarray(turn_table())
    sizes = image_sizes.T
    mixed, first, taps = mixer_forward(sizes, pixels, mixer_params, channel_params, turn)
    other_mixed = exchange(mixed)
    up_low, up_turned, down_low, down_turned, square = weights_low(up_weight, down_weight)
    sums, bias_parts = [], []
    earlier = ()
    inputs = [sizes, mixed, other_mixed, out_grad, other_grad, rounded, others]
    for chunk in range(CHUNKS):
        values = feed_chunk(chunk, place, inputs, up_turned, down_low, row(hidden_bias), earlier)
        earlier = values[0:2]
        if chunk == 0:
            inputs, stat = values[-3:-1], values[-1]
        bias_parts.append(values[2])
        sums.append(GradientSum(values[3], values[4 : 3 + PLANE]))
    hidden, slopes = earlier
    partial = []
    early, late = sums
    early.to_line()
    tokens, riders = early.sends, [early.kept, late.kept]
    for part in range(SUM_PARTS):
        own, send, riders = hidden_sums(
            place, hidden, slopes, down_turned, up_low, mixed, other_mixed, stat, rounded, others, part, tokens, riders
        )
        if part == 0:
            early.kept, late.kept = riders
            early.gather()
            tokens, riders = [early.piece], [late.kept]
        partial.append((own, exchange(send)))
    done = ()
    (late.kept,) = riders
    late.to_line()
    by_permutes = late.kept.shape[0] % S == 0
    tokens, riders = late.sends, [late.kept]
    carries = bias_parts
    for at, part in enumerate(BACK_PARTS):
        own, got = partial[part[0] * SUM_PARTS // S]
        values = backward(
            sizes, pixels, out_grad, mixed, first, stat, own, got, rounded, taps, turn, carries, part, done, riders, tokens
        )
        done, carries = values[0:2], values[2:3]
        tokens, riders = [], []
        if at == 0:
            (late.kept,) = values[3:]
            if by_permutes:
                late.gather_line()
                tokens, riders = [late.piece], [late.piece]
            else:
                late.gather()
        elif at == 1 and by_permutes:
            late.pieces[0] = values[3]
            late.gather_plane()
            tokens = [late.quarter]
    (carry,) = carries
    block_out, pixel_grad = done

    total, stride = carry, 1
    stats = jnp.zeros((8, 8 * LANES), f32)
    settled = ()
    for chunk, sources in enumerate(([early.sum] * 2, late.quarters if by_permutes else [late.sum] * 2)):
        there = [across(total, stride * away) for away in (1, 2, 3)]
        tokens = late.quarters[1:] if by_permutes and chunk == 0 else []
        values = statistics(chunk, place, sources, row(up_cols), row(down_rows), stats, settled, total, tokens)
        settled, stats = values[0:4], values[4]
        total, stride = (values[5] + there[0]) + (there[1] + there[2]), 4 * stride
    while stride < lax.axis_size("line") * PLANE:
        total, stride = total + across(total, stride), 2 * stride
    up_sum, down_sum, up_cols_new, down_rows_new = settled
    (
        mixer_sum,
        mixer_rows_new,
        channel_sum,
        channel_moment_new,
        channel_update,
        bias_sum,
        bias_moment_new,
        bias_update,
        stats,
        channel_square,
    ) = small_update(
        total,
        stats,
        square,
        mixer_params,
        channel_params,
        channel_moment,
        hidden_bias,
        bias_moment,
        mixer_rows,
        down_rows_new,
    )
    got_stats, got_square = exchange((stats, channel_square))
    (
        update_rms,
        up_rows_new,
        down_cols_new,
        mixer_cols_new,
        up_new,
        up_average_new,
        down_new,
        down_average_new,
        mixer_new,
        mixer_average_new,
        channel_new,
        channel_average_new,
        bias_new,
        bias_average_new,
        bias_sum,
        bias_moment_new,
        up_cols_new,
        down_rows_new,
        mixer_rows_new,
    ) = final_update(
        [
            stats,
            got_stats,
            channel_square,
            got_square,
            up_rows,
            down_cols,
            mixer_cols,
            up_cols_new,
            down_rows_new,
            up_sum,
            up_weight,
            up_average,
            down_sum,
            down_weight,
            down_average,
            mixer_sum,
            mixer_params,
            mixer_average,
            mixer_rows_new,
            channel_params,
            channel_average,
            channel_update,
            hidden_bias,
            bias_average,
            bias_update,
            bias_sum,
            bias_moment_new,
            up_cols_new,
            down_rows_new,
        ],
        256,
    )
    return (
        block_out,
        pixel_grad,
        update_rms.reshape(()),
        up_sum,
        up_rows_new,
        up_cols_new,
        up_new,
        up_average_new,
        down_sum,
        down_rows_new,
        down_cols_new,
        down_new,
        down_average_new,
        mixer_sum,
        mixer_rows_new,
        mixer_cols_new,
        mixer_new,
        mixer_average_new,
        channel_sum,
        channel_moment_new,
        channel_new,
        channel_average_new,
        bias_sum,
        bias_moment_new,
        bias_new,
        bias_average_new,
    )


def solution(mesh):
    mesh = jax.sharding.Mesh(mesh.devices.reshape(-1, PLANE, mesh.shape["ch"]), ("line", "plane", "ch"))
    images = ("line", "plane")
    split = P("ch", images)
    over_rows, over_cols, over = P("ch", None), P(None, "ch"), P("ch")
    return jax.shard_map(
        shards,
        mesh=mesh,
        in_specs=(
            split,
            P(images, None),
            split,
            over_cols,
            over_rows,
            over_rows,
            over_cols,
            over,
            P(),
            over,
            over,
            P(),
            over,
            P(),
            over_cols,
            over,
            over_cols,
            over_rows,
            over_rows,
            over_cols,
            over,
        ),
        out_specs=(
            split,
            split,
            P(),
            over_cols,
            P(),
            over,
            over_cols,
            over_cols,
            over_rows,
            over,
            P(),
            over_rows,
            over_rows,
            over_rows,
            over,
            P(),
            over_rows,
            over_rows,
            over_cols,
            over_cols,
            over_cols,
            over_cols,
            over,
            over,
            over,
            over,
        ),
        check_vma=False,
    )
```

```python
import functools

import jax
import jax.numpy as jnp
import ml_dtypes
import numpy as np
from jax import lax
from jax.experimental import pallas as pl
from jax.experimental.pallas import tpu as pltpu
from jax.sharding import PartitionSpec as P

S = 16
AREA = S * S
STEP = 10
LANES = 128

EPSILON_NORM = 1e-06
EPSILON_SQUARE = 1e-30
EPSILON_SCALE = 0.001
LEARN_RATE = 0.3
CLIP_LEVEL = 1.0
AVERAGE_KEEP = 0.9
HALF_ROOT = 0.7071067811865476
DENSITY = 0.3989422804014327
LOG2_E = 1.4426950408889634
DECAY = 1.0 - STEP ** (-0.8)
FRESH = 1.0 - DECAY
ERF_P = 0.3275911
ERF_A = (0.254829592, -0.284496736, 1.421413741, -1.453152027, 1.061405429)
CHUNKS = 2
SUM_PARTS = 2
BACK_PARTS = ((0, 8), (8, 8))
PLANE = 4

f32 = jnp.float32
bf16 = jnp.bfloat16
NT = (((1,), (1,)), ((), ()))
TN = (((0,), (0,)), ((), ()))
NN = (((1,), (0,)), ((), ()))


def dot(left, right, dims=NN):
    return lax.dot_general(left, right, dims, preferred_element_type=f32)


def params(mib=60):
    return pltpu.CompilerParams(vmem_limit_bytes=mib * 1024 * 1024)


def cost(microseconds):
    return pl.CostEstimate(
        flops=int(microseconds * 1e9), bytes_accessed=int(microseconds * 3e6), transcendentals=0
    )


def image_mask(sizes_ref, image):
    place = lax.broadcasted_iota(jnp.int32, (1, AREA), 1)
    row, column = lax.shift_right_logical(place, 4), place & (S - 1)
    sizes = sizes_ref[...].astype(f32)
    here = lax.broadcasted_iota(jnp.int32, sizes.shape, 1) == image
    size = jnp.sum(jnp.where(here, sizes, 0.0), axis=1, keepdims=True)
    inside = (row.astype(f32) < size[0:1, :]) & (column.astype(f32) < size[1:2, :])
    return jnp.where(inside, 1.0, 0.0).astype(f32)


def wide_column(wide_ref, row, span):
    return jnp.concatenate([wide_ref[row]] * (span // LANES), axis=1)


def first_power(table, half):
    base = half * 256
    rate = jnp.exp(table[base : base + 64])
    freq = table[base + 64 : base + 128]
    damp = jnp.exp(-rate)
    return (
        rate,
        damp * jnp.cos(freq),
        damp * jnp.sin(freq),
        table[base + 128 : base + 192],
        table[base + 192 : base + 256],
    )


def make_taps(params_ref, out_ref):
    table = params_ref[...].T
    for half in range(2):
        _, step_real, step_imag, real, imag = first_power(table, half)
        here_real, here_imag = jnp.ones_like(step_real), jnp.zeros_like(step_real)
        for place in range(S):
            tap = jnp.sum(real * here_real - imag * here_imag, axis=0, keepdims=True)
            out_ref[half, place : place + 1, :] = tap.astype(bf16).astype(f32)
            here_real, here_imag = (
                here_real * step_real - here_imag * step_imag,
                here_real * step_imag + here_imag * step_real,
            )


def taps_back(params_ref, grad_ref, table_ref):
    table = params_ref[...].T
    for half in range(2):
        rate, step_real, step_imag, real, imag = first_power(table, half)
        here_real, here_imag = jnp.ones_like(step_real), jnp.zeros_like(step_real)
        zero = jnp.zeros_like(step_real)
        sum_real, sum_imag, far_real, far_imag = zero, zero, zero, zero
        for place in range(S):
            grad = grad_ref[half * S + place : half * S + place + 1, :]
            wave_real, wave_imag = grad * here_real, grad * here_imag
            sum_real, sum_imag = sum_real + wave_real, sum_imag + wave_imag
            far_real, far_imag = far_real + place * wave_real, far_imag + place * wave_imag
            here_real, here_imag = (
                here_real * step_real - here_imag * step_imag,
                here_real * step_imag + here_imag * step_real,
            )
        base = half * 256
        table_ref[base : base + 64] = -rate * (real * far_real - imag * far_imag)
        table_ref[base + 64 : base + 128] = -(real * far_imag + imag * far_real)
        table_ref[base + 128 : base + 192] = sum_real
        table_ref[base + 192 : base + 256] = -sum_imag


def block_rows(place):
    return slice(place * S, (place + 1) * S)


def causal(source_ref, taps_ref, half, lanes, base=0):
    rows = [source_ref[base + place * S : base + (place + 1) * S, lanes] for place in range(S)]
    for place in range(S):
        total = rows[place] * taps_ref[half, 0:1, lanes]
        for back in range(1, place + 1):
            total += rows[place - back] * taps_ref[half, back : back + 1, lanes]
        yield total


def anticausal(source_ref, taps_ref, half, lanes):
    rows = [source_ref[block_rows(place), lanes] for place in range(S)]
    for place in range(S):
        total = rows[place] * taps_ref[half, 0:1, lanes]
        for ahead in range(1, S - place):
            total += rows[place + ahead] * taps_ref[half, ahead : ahead + 1, lanes]
        yield total


def mixer_kernel(
    sizes_ref, pixels_ref, params_ref, channel_ref, turn_ref, mixed_ref, first_ref, taps_ref, cells_ref, low_ref, wide_ref, *, per_step
):
    @pl.when(pl.program_id(0) == 0)
    def _():
        make_taps(params_ref, taps_ref)

    width = pixels_ref.shape[0]
    for part in range(per_step):
        spot = slice(part * AREA, (part + 1) * AREA)
        mask = image_mask(sizes_ref, pl.program_id(0) * per_step + part)
        masked = (pixels_ref[:, spot].astype(f32) * mask).astype(bf16)
        cells, low, wide = cells_ref.at[part], low_ref.at[part], wide_ref.at[part]
        cells[...] = dot(turn_ref[...], masked, NT)
        for start in range(0, width, LANES):
            lanes = slice(start, start + LANES)
            for place, value in enumerate(causal(cells, taps_ref, 0, lanes)):
                low[block_rows(place), lanes] = value.astype(bf16)
        wide[...] = dot(turn_ref[AREA:, :], low[...])
        first_ref[spot, :] = wide[...].astype(bf16)
        for start in range(0, width, LANES):
            lanes = slice(start, start + LANES)
            skip = channel_ref[2:3, lanes]
            for place, value in enumerate(causal(wide, taps_ref, 1, lanes)):
                own = cells[AREA + place * S : AREA + (place + 1) * S, lanes]
                low[block_rows(place), lanes] = (value + skip * own).astype(bf16)
        mixed_ref[:, spot] = dot(low[...], turn_ref[AREA:, :], TN).astype(bf16)


def mixer_forward(sizes, pixels, mixer_params, channel, turn):
    width, count = pixels.shape
    per_step = 2
    span = per_step * AREA
    in_specs = [
        pl.BlockSpec(sizes.shape, lambda i: (0, 0)),
        pl.BlockSpec((width, span), lambda i: (0, i)),
        pl.BlockSpec(mixer_params.shape, lambda i: (0, 0)),
        pl.BlockSpec(channel.shape, lambda i: (0, 0)),
        pl.BlockSpec(turn.shape, lambda i: (0, 0)),
    ]
    out_specs = [
        pl.BlockSpec((width, span), lambda i: (0, i)),
        pl.BlockSpec((span, width), lambda i: (i, 0)),
        pl.BlockSpec((2, S, width), lambda i: (0, 0, 0)),
    ]
    scratch_shapes = [
        pltpu.VMEM((per_step, 2 * AREA, width), f32),
        pltpu.VMEM((per_step, AREA, width), bf16),
        pltpu.VMEM((per_step, AREA, width), f32),
    ]
    return pl.pallas_call(
        functools.partial(mixer_kernel, per_step=per_step),
        grid=(count // span,),
        in_specs=in_specs,
        out_specs=out_specs,
        scratch_shapes=scratch_shapes,
        out_shape=[
            jax.ShapeDtypeStruct((width, count), bf16),
            jax.ShapeDtypeStruct((count, width), bf16),
            jax.ShapeDtypeStruct((2, S, width), f32),
        ],
        compiler_params=params(),
        cost_estimate=cost(16),
        name="mixer_forward",
    )(sizes, pixels, mixer_params, channel, turn)


GAIN, SHIFT, LAYER = 0, 1, 3


def normalize(
    step,
    place_ref,
    sizes_ref,
    own_ref,
    other_ref,
    own_grad_ref,
    other_grad_ref,
    own_rows_ref,
    other_rows_ref,
    act_ref,
    low_ref,
    stat_ref,
    own_wide,
    other_wide,
):
    width, span = own_ref.shape
    width = 2.0 * width
    mine = place_ref[0]

    @pl.when(step == 0)
    def _():
        for at, row in enumerate((GAIN, SHIFT, LAYER)):
            own_wide[at] = to_column(own_rows_ref[row : row + 1, :])
            other_wide[at] = to_column(other_rows_ref[row : row + 1, :])

    for part in range(span // AREA):
        spot = slice(part * AREA, (part + 1) * AREA)
        mask = image_mask(sizes_ref, step * (span // AREA) + part)
        own, other = own_ref[:, spot].astype(f32), other_ref[:, spot].astype(f32)
        mean = (jnp.sum(own, axis=0, keepdims=True) + jnp.sum(other, axis=0, keepdims=True)) / width
        own, other = own - mean, other - mean
        spread = (
            jnp.sum(own * own, axis=0, keepdims=True) + jnp.sum(other * other, axis=0, keepdims=True)
        ) / width
        scale = lax.rsqrt(spread + EPSILON_NORM)
        stat_ref[0:1, spot] = mean
        stat_ref[1:2, spot] = scale
        for which, value_ref, grad_ref, wide in (
            (mine, own_ref, own_grad_ref, own_wide),
            (1 - mine, other_ref, other_grad_ref, other_wide),
        ):
            value = (value_ref[:, spot].astype(f32) - mean) * scale
            act_ref[which, :, spot] = (
                value * wide_column(wide, 0, AREA) + wide_column(wide, 1, AREA)
            ).astype(bf16)
            grad = grad_ref[:, spot].astype(f32) * mask
            low_ref[which, :, spot] = (grad * wide_column(wide, 2, AREA)).astype(bf16)


def weights_kernel(up_ref, down_ref, up_low_ref, up_turned_ref, down_low_ref, down_turned_ref, square_ref):
    @pl.when(pl.program_id(0) == 0)
    def _():
        square_ref[...] = jnp.zeros_like(square_ref)

    for row, source_ref, low_ref, turned_ref in (
        (0, up_ref, up_low_ref, up_turned_ref),
        (1, down_ref, down_low_ref, down_turned_ref),
    ):
        value = source_ref[...]
        units = square_ref.shape[1]
        for start in range(0, value.shape[1], units):
            part = value[:, start : start + units]
            square_ref[row : row + 1, :] += jnp.sum(part * part, axis=0, keepdims=True)
        low_ref[...] = value.astype(bf16)
        turned_ref[...] = value.T.astype(bf16)


def weights_low(up, down):
    full, hidden_local = up.shape
    units = 384
    column = lambda i: (0, i)
    row = lambda i: (i, 0)
    return pl.pallas_call(
        weights_kernel,
        grid=(hidden_local // units,),
        in_specs=[pl.BlockSpec((full, units), column), pl.BlockSpec((full // 2, full), row)],
        out_specs=[
            pl.BlockSpec((full, units), column),
            pl.BlockSpec((units, full), row),
            pl.BlockSpec((units, full), row),
            pl.BlockSpec((full, units), column),
            pl.BlockSpec((8, units), lambda i: (0, 0)),
        ],
        out_shape=[
            jax.ShapeDtypeStruct((full, hidden_local), bf16),
            jax.ShapeDtypeStruct((hidden_local, full), bf16),
            jax.ShapeDtypeStruct((hidden_local, full), bf16),
            jax.ShapeDtypeStruct((full, hidden_local), bf16),
            jax.ShapeDtypeStruct((8, units), f32),
        ],
        compiler_params=params(),
        cost_estimate=cost(8),
        name="weights_low",
    )(up, down)


def gelu_pair(pre):
    bell = jnp.exp2(pre * pre * (-0.5 * LOG2_E))
    part = pl.reciprocal(1.0 + (ERF_P * HALF_ROOT) * jnp.abs(pre), approx=True)
    poly = 0.5 * ERF_A[4]
    for factor in ERF_A[3::-1]:
        poly = poly * part + 0.5 * factor
    tail = poly * part * bell
    upper = jnp.where(pre >= 0.0, 1.0 - tail, tail)
    return pre * upper, upper + pre * bell * DENSITY


def split_out(source_ref, digit, part_refs):
    rows = part_refs[0].shape[0]
    for away, ref in enumerate(part_refs):
        start = pl.multiple_of((digit ^ away) * rows, rows)
        ref[...] = source_ref[pl.ds(start, rows), :].astype(ref.dtype)


def chunk_kernel(place_ref, *refs, first):
    step = pl.program_id(0)
    if first:
        ins, (up_ref, down_ref, bias_ref) = refs[:7], refs[7:10]
        refs, outs, wide = refs[10:-5], refs[-5:-2], refs[-2:]
        normalize(step, place_ref, *ins, *outs, *wide)
        act_ref, low_ref, _ = outs
    else:
        act_ref, low_ref, up_ref, down_ref, bias_ref = refs[:5]
        refs = refs[7:]
    hidden_ref, slope_ref, bias_grad_ref = refs[:3]
    part_refs, (grad_acc, bias_acc, bias_wide) = refs[3 : 3 + PLANE], refs[3 + PLANE :]

    @pl.when(step == 0)
    def _():
        grad_acc[...] = jnp.zeros_like(grad_acc)
        bias_acc[...] = jnp.zeros_like(bias_acc)
        bias_wide[...] = to_column(bias_ref[...].astype(bf16).astype(f32))

    halves, width, span = act_ref.shape
    units = up_ref.shape[0]
    full = halves * width
    tile = 256
    tiles = [(row, start) for start in range(0, span, tile) for row in range(0, units, tile)]

    def products(row, start):
        rows, spot = slice(row, row + tile), slice(start, start + tile)
        pre = dot(up_ref[rows, :], act_ref[:, :, spot].reshape(full, tile))
        pre += jnp.concatenate([bias_wide[rows, :]] * (tile // LANES), axis=1)
        return pre, dot(down_ref[rows, :], low_ref[:, :, spot].reshape(full, tile))

    ready = products(*tiles[0])
    for at, (row, start) in enumerate(tiles):
        pre, back = ready
        if at + 1 < len(tiles):
            ready = products(*tiles[at + 1])
        rows, spot = slice(row, row + tile), slice(start, start + tile)
        hidden, slope = gelu_pair(pre)
        hidden_ref[rows, spot] = hidden.astype(bf16)
        slope_ref[rows, spot] = (back * slope).astype(bf16)
    grad_acc[:units, :] += dot(slope_ref[...], act_ref[...].reshape(full, span), NT)
    grad_acc[units:, :] += dot(hidden_ref[...], low_ref[...].reshape(full, span), NT)
    bias_acc[...] += dot(jnp.ones((S, span), bf16), slope_ref[...], NT)

    @pl.when(step == pl.num_programs(0) - 1)
    def _():
        split_out(grad_acc, place_ref[1], part_refs)
        bias_grad_ref[...] = bias_acc[0:8, :]


def feed_chunk(chunk, place, inputs, up_turned, down, bias, earlier):
    hidden_local, full = down.shape
    units = hidden_local // CHUNKS
    width = full // 2
    span = 512
    count = inputs[1].shape[-1]
    pair = pl.BlockSpec((2, width, span), lambda i, *_: (0, 0, i))
    block = pl.BlockSpec((width, span), lambda i, *_: (0, i))
    weight = pl.BlockSpec((units, full), lambda i, *_: (chunk, 0))
    wide = pl.BlockSpec((units, span), lambda i, *_: (chunk, i))
    whole = lambda i, *_: (0, 0)
    rows = 2 * units // PLANE
    in_specs = [pair, pair]
    if chunk == 0:
        small = [pl.BlockSpec(array.shape, whole) for array in (inputs[0], *inputs[-2:])]
        in_specs = [small[0], block, block, block, block, small[1], small[2]]
    in_specs += [weight, weight, pl.BlockSpec((1, units), lambda i, *_: (0, chunk))]
    in_specs += [pl.BlockSpec(memory_space=pl.ANY)] * len(earlier)
    out_specs = [wide, wide, pl.BlockSpec((8, units), whole)] + [pl.BlockSpec((rows, full), whole)] * PLANE
    out_shape = [
        jax.ShapeDtypeStruct((hidden_local, count), bf16),
        jax.ShapeDtypeStruct((hidden_local, count), bf16),
        jax.ShapeDtypeStruct((8, units), f32),
        jax.ShapeDtypeStruct((rows, full), f32),
    ] + [jax.ShapeDtypeStruct((rows, full), bf16)] * (PLANE - 1)
    scratch_shapes = [
        pltpu.VMEM((2 * units, full), f32),
        pltpu.VMEM((S, units), f32),
        pltpu.VMEM((units, LANES), f32),
    ]
    if chunk == 0:
        out_specs += [pair, pair, pl.BlockSpec((8, span), lambda i, *_: (0, i))]
        out_shape += [jax.ShapeDtypeStruct((2, width, count), bf16)] * 2 + [jax.ShapeDtypeStruct((8, count), f32)]
        scratch_shapes += [pltpu.VMEM((3, width, LANES), f32)] * 2

    def body(*refs):
        if chunk == 0:
            made = len(in_specs) + 1 + len(out_specs)
            outs = refs[made - 3 : made]
            refs = (*refs[: made - 3], *refs[made:-2], *outs, *refs[-2:])
        chunk_kernel(*refs, first=chunk == 0)

    return pl.pallas_call(
        body,
        grid_spec=pltpu.PrefetchScalarGridSpec(
            num_scalar_prefetch=1,
            grid=(count // span,),
            in_specs=in_specs,
            out_specs=out_specs,
            scratch_shapes=scratch_shapes,
        ),
        out_shape=out_shape,
        input_output_aliases={6: 0, 7: 1} if earlier else {},
        compiler_params=params(),
        cost_estimate=cost(40),
        name="feed_chunk_%d" % chunk,
    )(place, *inputs, up_turned, down, bias, *earlier)


def across(value, stride):
    size = lax.axis_size("line") * PLANE
    return lax.ppermute(value, ("line", "plane"), [(i, i ^ stride) for i in range(size)])


def along(value, axis, away):
    return lax.ppermute(value, axis, [(i, i ^ away) for i in range(lax.axis_size(axis))])


class GradientSum:
    def __init__(self, kept, sends):
        self.kept = kept
        self.got = [along(value, "plane", away) for away, value in enumerate(sends, 1)]

    def add(self):
        total = self.kept
        for value in self.got:
            total = total + value.astype(f32)
        return total

    def to_line(self):
        size = lax.axis_size("line")
        total = self.add()
        parts = total.reshape(size, -1, total.shape[1])

        def part(away):
            return lax.dynamic_index_in_dim(parts, lax.axis_index("line") ^ away, 0, keepdims=False)

        self.kept = part(0)
        self.sends = [part(away).astype(bf16) for away in range(1, size)]
        self.got = [along(value, "line", away) for away, value in enumerate(self.sends, 1)]

    def to_piece(self):
        self.piece = self.add().astype(bf16)

    def gather(self):
        self.to_piece()
        self.sum = lax.all_gather(self.piece, ("plane", "line"), axis=0, tiled=True)

    def gather_line(self):
        self.to_piece()
        size = lax.axis_size("line")
        self.pieces = [self.piece] + [along(self.piece, "line", away) for away in range(1, size)]

    def gather_plane(self):
        self.quarter = jnp.concatenate(self.pieces)
        self.quarters = [self.quarter] + [along(self.quarter, "plane", away) for away in range(1, PLANE)]


EXTRA = 16


def sums_kernel(
    place_ref,
    hidden_ref,
    slope_ref,
    down_ref,
    up_ref,
    own_ref,
    other_ref,
    stat_ref,
    own_rows_ref,
    other_rows_ref,
    *refs,
    skipped,
):
    own_proj_ref, own_act_ref, sum_ref, send_ref = refs[skipped : skipped + 4]
    own_wide, other_wide = refs[-2:]
    width, span = own_ref.shape
    mine = place_ref[0]
    own_rows = pl.ds(pl.multiple_of(mine * width, width), width)
    other_rows = pl.ds(pl.multiple_of((1 - mine) * width, width), width)

    @pl.when(pl.program_id(0) == 0)
    def _():
        own_wide[0] = to_column(own_rows_ref[0:1, :])
        other_wide[0] = to_column(other_rows_ref[0:1, :])

    own_proj_ref[...] = dot(down_ref[own_rows, :], hidden_ref[...]).astype(bf16)
    send_ref[0:width, :] = dot(down_ref[other_rows, :], hidden_ref[...]).astype(bf16)
    mean, scale = stat_ref[0:1, :], stat_ref[1:2, :]
    sums = []
    for own, rows, value_ref, wide in (
        (True, own_rows, own_ref, own_wide),
        (False, other_rows, other_ref, other_wide),
    ):
        act = dot(up_ref[rows, :], slope_ref[...])
        if own:
            own_act_ref[...] = act.astype(bf16)
        else:
            send_ref[width : 2 * width, :] = act.astype(bf16)
        act = act * wide_column(wide, 0, span)
        normed = (value_ref[...].astype(f32) - mean) * scale
        sums.append(jnp.sum(act, axis=0, keepdims=True))
        sums.append(jnp.sum(act * normed, axis=0, keepdims=True))
    plain, tilt = sums[0] + sums[2], sums[1] + sums[3]
    sum_ref[0:1, :] = plain
    sum_ref[1:2, :] = tilt
    parts = []
    for value in (plain, tilt):
        high = value.astype(bf16).astype(f32)
        parts += [high, value - high]
    parts.append(jnp.zeros((EXTRA - 4, span), f32))
    send_ref[2 * width :, :] = jnp.concatenate(parts, axis=0).astype(bf16)


def hidden_sums(place, hidden, slopes, down_turned, up, own, other, stat, own_rows, other_rows, part, tokens, riders):
    width, total = own.shape
    count = total // SUM_PARTS
    hidden_local = hidden.shape[0]
    span = 512
    base = part * (count // span)
    column = lambda i, *_: (0, base + i)
    out = lambda i, *_: (0, i)
    fixed = lambda i, *_: (0, 0)
    wide = pl.BlockSpec((hidden_local, span), column)
    block = pl.BlockSpec((width, span), column)
    result = pl.BlockSpec((width, span), out)
    rows = pl.BlockSpec(own_rows.shape, fixed)
    sent = 2 * width + EXTRA
    grid_spec = pltpu.PrefetchScalarGridSpec(
        num_scalar_prefetch=1,
        grid=(count // span,),
        in_specs=[
            wide,
            wide,
            pl.BlockSpec(down_turned.shape, fixed),
            pl.BlockSpec(up.shape, fixed),
            block,
            block,
            pl.BlockSpec((8, span), column),
            rows,
            rows,
        ]
        + [pl.BlockSpec(memory_space=pl.ANY)] * (len(riders) + len(tokens)),
        out_specs=[result, result, pl.BlockSpec((8, span), out), pl.BlockSpec((sent, span), out)]
        + [pl.BlockSpec(memory_space=pl.ANY)] * len(riders),
        scratch_shapes=[pltpu.VMEM((1, width, LANES), f32)] * 2,
    )
    values = pl.pallas_call(
        functools.partial(sums_kernel, skipped=len(riders) + len(tokens)),
        grid_spec=grid_spec,
        out_shape=[
            jax.ShapeDtypeStruct((width, count), bf16),
            jax.ShapeDtypeStruct((width, count), bf16),
            jax.ShapeDtypeStruct((8, count), f32),
            jax.ShapeDtypeStruct((sent, count), bf16),
        ]
        + [jax.ShapeDtypeStruct(rider.shape, rider.dtype) for rider in riders],
        input_output_aliases={10 + at: 4 + at for at in range(len(riders))},
        compiler_params=params(),
        cost_estimate=cost(40 / SUM_PARTS * 2),
        name="hidden_sums_%d" % part,
    )(place, hidden, slopes, down_turned, up, own, other, stat, own_rows, other_rows, *riders, *tokens)
    return values[:3], values[3], values[4:]


TAPS, ROWS, BIAS = 0, 32, 40
PER_STEP = 2


def correlate(left_ref, right_ref, sum_ref, half, lanes):
    left = [left_ref[block_rows(place), lanes] for place in range(S)]
    right = [right_ref[block_rows(place), lanes].astype(f32) for place in range(S)]
    for back in range(S):
        total = left[back] * right[0]
        for place in range(back + 1, S):
            total += left[place] * right[place - back]
        sum_ref[half, block_rows(back), lanes] += total


def backward_kernel(
    sizes_ref,
    pixels_ref,
    grad_ref,
    mixed_ref,
    first_ref,
    stat_ref,
    own_proj_ref,
    own_act_ref,
    own_sum_ref,
    got_ref,
    rows_ref,
    taps_ref,
    turn_ref,
    *refs,
    base,
    carries,
    skipped,
):
    carry_refs, refs = refs[:carries], refs[carries:]
    out_ref, pixel_grad_ref, small_ref = refs[skipped : skipped + 3]
    sum_ref, channel_sum, cells_ref, low_ref, wide_ref, back_ref, columns = refs[-7:]
    step = pl.program_id(0)
    width = pixels_ref.shape[0]
    full = 2.0 * width

    @pl.when(step == 0)
    def _():
        sum_ref[...] = jnp.zeros_like(sum_ref)
        channel_sum[...] = jnp.zeros_like(channel_sum)
        for row in (0, 2, 3, 4):
            columns[row] = to_column(rows_ref[row : row + 1, :])

    gain, skip, layer, shift = (wide_column(columns, row, AREA) for row in (0, 2, 3, 4))

    def gather(row, value):
        channel_sum[row] += value[:, :LANES] + value[:, LANES:]

    for part in range(PER_STEP):
        spot = slice(part * AREA, (part + 1) * AREA)
        mask = image_mask(sizes_ref, base + step * PER_STEP + part)
        pixels = pixels_ref[:, spot].astype(f32)
        grad = grad_ref[:, spot].astype(f32)
        masked = pixels * mask
        masked_grad = grad * mask
        branch = own_proj_ref[:, spot].astype(f32) + got_ref[0:width, spot].astype(f32) + shift
        out_ref[:, spot] = pixels + mask * layer * branch
        gather(3, masked_grad * branch)
        gather(4, masked_grad)

        scale = stat_ref[1:2, spot]
        normed = (mixed_ref[:, spot].astype(f32) - stat_ref[0:1, spot]) * scale
        act = own_act_ref[:, spot].astype(f32) + got_ref[width : 2 * width, spot].astype(f32)
        gather(0, act * normed)
        gather(1, act)
        got = got_ref[2 * width :, spot].astype(f32)
        plain = (own_sum_ref[0:1, spot] + (got[0:1, :] + got[1:2, :])) / full
        tilt = (own_sum_ref[1:2, spot] + (got[2:3, :] + got[3:4, :])) / full
        mixed_low = (scale * (act * gain - plain - normed * tilt)).astype(bf16)
        mixed_grad = mixed_low.astype(f32)
        gather(2, mixed_grad * masked)

        cells, low, wide, back = cells_ref.at[part], low_ref.at[part], wide_ref.at[part], back_ref.at[part]
        cells[...] = dot(turn_ref[:AREA, :], masked.astype(bf16), NT)
        wide[...] = dot(turn_ref[AREA:, :], mixed_low, NT)
        for start in range(0, width, LANES):
            lanes = slice(start, start + LANES)
            for place, value in enumerate(anticausal(wide, taps_ref, 1, lanes)):
                low[block_rows(place), lanes] = value.astype(bf16)
            correlate(wide, first_ref.at[spot], sum_ref, 1, lanes)
        back[...] = dot(turn_ref[AREA:, :], low[...])
        for start in range(0, width, LANES):
            lanes = slice(start, start + LANES)
            for place, value in enumerate(anticausal(back, taps_ref, 0, lanes)):
                wide[block_rows(place), lanes] = value
            correlate(back, cells, sum_ref, 0, lanes)
        pixel_grad_ref[:, spot] = grad + mask * (wide[...].T + skip * mixed_grad)

    @pl.when(step == pl.num_programs(0) - 1)
    def _():
        if base > 0:
            small_ref[...] = carry_refs[0][...]
        else:
            small_ref[...] = jnp.zeros_like(small_ref)
            row = BIAS
            for ref in carry_refs:
                for start in range(0, ref.shape[1], width):
                    small_ref[row : row + 1, :] = ref[0:1, start : start + width]
                    row += 1
        for half in range(2):
            for back in range(S):
                row = TAPS + half * S + back
                small_ref[row : row + 1, :] += jnp.sum(
                    sum_ref[half, block_rows(back), :], axis=0, keepdims=True
                )
        for row in range(5):
            small_ref[ROWS + row : ROWS + row + 1, :] += jnp.sum(channel_sum[row].T, axis=0, keepdims=True)


def backward(sizes, pixels, grad, mixed, mid, stat, own, got, rows, taps, turn, carries, part, earlier, riders, tokens):
    own_proj, own_act, own_sum = own
    width, total = pixels.shape
    base, count = (at * (total // S) for at in part)
    span = PER_STEP * AREA
    at = base // span
    inner = at % (own_proj.shape[1] // span)
    column = lambda i: (0, at + i)
    here = lambda i: (0, inner + i)
    fixed = lambda i: (0, 0)
    block = pl.BlockSpec((width, span), column)
    local = pl.BlockSpec((width, span), here)
    anywhere = pl.BlockSpec(memory_space=pl.ANY)
    base //= AREA
    in_specs = [
        pl.BlockSpec(sizes.shape, fixed),
        block,
        block,
        block,
        pl.BlockSpec((span, width), lambda i: (at + i, 0)),
        pl.BlockSpec((8, span), column),
        local,
        local,
        pl.BlockSpec((8, span), here),
        pl.BlockSpec((got.shape[0], span), here),
        pl.BlockSpec(rows.shape, fixed),
        pl.BlockSpec(taps.shape, lambda i: (0, 0, 0)),
        pl.BlockSpec(turn.shape, fixed),
    ]
    in_specs += [pl.BlockSpec(carry.shape, fixed) for carry in carries]
    in_specs += [anywhere] * (len(earlier) + len(riders) + len(tokens))
    first = 13 + len(carries)
    small = (BIAS + 8, width)
    return pl.pallas_call(
        functools.partial(backward_kernel, base=base, carries=len(carries), skipped=len(earlier) + len(riders) + len(tokens)),
        grid=(count // span,),
        in_specs=in_specs,
        out_specs=[block, block, pl.BlockSpec(small, fixed)] + [anywhere] * len(riders),
        scratch_shapes=[
            pltpu.VMEM((2, AREA, width), f32),
            pltpu.VMEM((5, width, LANES), f32),
            pltpu.VMEM((PER_STEP, AREA, width), f32),
            pltpu.VMEM((PER_STEP, AREA, width), bf16),
            pltpu.VMEM((PER_STEP, AREA, width), f32),
            pltpu.VMEM((PER_STEP, AREA, width), f32),
            pltpu.VMEM((5, width, LANES), f32),
        ],
        out_shape=[
            jax.ShapeDtypeStruct((width, total), f32),
            jax.ShapeDtypeStruct((width, total), f32),
            jax.ShapeDtypeStruct(small, f32),
        ]
        + [jax.ShapeDtypeStruct(rider.shape, rider.dtype) for rider in riders],
        input_output_aliases={first + at: at for at in range(len(earlier))}
        | {first + len(earlier) + at: 3 + at for at in range(len(riders))},
        compiler_params=params(),
        cost_estimate=cost(90 * part[1] / S),
        name="backward_%d" % base,
    )(
        sizes, pixels, grad, mixed, mid, stat, own_proj, own_act, own_sum, got, rows, taps, turn, *carries, *earlier, *riders, *tokens
    )


UP_ROW, UP_MASS, DOWN_COL, DOWN_MASS, MIXER_COL, MIXER_MASS, SCALARS = range(7)


def fold(value):
    total = value[:, :LANES]
    for start in range(LANES, value.shape[1], LANES):
        total += value[:, start : start + LANES]
    return total


def as_row(ref):
    return ref[...].reshape(1, ref.shape[0])


def to_flat(ref, value):
    ref[...] = value.reshape(ref.shape[0])


def to_column(row):
    return jnp.broadcast_to(row, (LANES, row.shape[1])).T


def to_row(columns):
    return jnp.sum(columns.T, axis=0, keepdims=True)


def statistics_kernel(place_ref, *refs, quarters, skipped, line_parts):
    sources, refs = refs[:quarters], refs[quarters:]
    up_old_ref, down_old_ref, carry_ref = refs[:3]
    up_ref, down_ref, up_new_ref, down_new_ref, stat_ref = refs[3 + skipped : 8 + skipped]
    quarter_ref = refs[-1]
    step = pl.program_id(0)
    plane, line = place_ref[1], place_ref[2]
    steps = PLANE // 2

    @pl.when(step == 0)
    def _():
        stat_ref[...] = carry_ref[...]

    for kind, old_ref, new_ref, columns, mass in (
        (0, up_old_ref, up_new_ref, UP_ROW, UP_MASS),
        (1, down_old_ref, down_new_ref, DOWN_COL, DOWN_MASS),
    ):
        if quarters == 2:
            value = sources[kind][...].astype(f32)
        else:
            for away, source_ref in enumerate(sources):

                @pl.when((kind * steps + step) ^ plane == away)
                def _():
                    rows = quarter_ref.shape[0] // line_parts

                    def move(at, _):
                        target = pl.ds(pl.multiple_of(at * rows, rows), rows)
                        source = pl.ds(pl.multiple_of((at ^ line) * rows, rows), rows)
                        quarter_ref[target, :] = source_ref[source, :].astype(f32)
                        return 0

                    lax.fori_loop(0, line_parts, move, 0)

            value = quarter_ref[...]
        if kind == 0:
            up_ref[...] = value.T
        else:
            down_ref[...] = value
        square = value * value
        mean = jnp.sum(fold(square), axis=1, keepdims=True) / value.shape[1]
        fresh = DECAY * to_column(old_ref[...]) + FRESH * (mean + EPSILON_SQUARE)
        new_ref[...] = fresh.T[0:1, :]
        stat_ref[columns : columns + 1, : value.shape[1]] += jnp.sum(square, axis=0, keepdims=True)
        stat_ref[mass : mass + 1, : value.shape[1]] += jnp.sum(
            square * (1.0 / fresh[:, 0:1]), axis=0, keepdims=True
        )


def statistics(chunk, place, sources, up_cols, down_rows, carry, earlier):
    hidden_local = up_cols.shape[1]
    units = hidden_local // CHUNKS
    full = sources[0].shape[1]
    rows = 2 * units // PLANE
    steps = PLANE // 2
    base = chunk * steps
    row = pl.BlockSpec((1, rows), lambda i: (0, base + i))
    anywhere = pl.BlockSpec(memory_space=pl.ANY)
    fixed = pl.BlockSpec(carry.shape, lambda i: (0, 0))
    if len(sources) == 2:
        specs = [
            pl.BlockSpec((rows, full), lambda i: (i, 0)),
            pl.BlockSpec((rows, full), lambda i: (steps + i, 0)),
        ]
    else:
        specs = [pl.BlockSpec((rows, full), lambda i: (0, 0))] * PLANE
    first = 4 + len(sources)
    return pl.pallas_call(
        functools.partial(statistics_kernel, quarters=len(sources), skipped=len(earlier), line_parts=lax.axis_size("line")),
        grid=(steps,),
        in_specs=[pl.BlockSpec(memory_space=pltpu.SMEM)]
        + specs
        + [row, row, fixed]
        + [anywhere] * len(earlier),
        out_specs=[
            pl.BlockSpec((full, rows), lambda i: (0, base + i)),
            pl.BlockSpec((rows, full), lambda i: (base + i, 0)),
            row,
            row,
            fixed,
        ],
        out_shape=[
            jax.ShapeDtypeStruct((full, hidden_local), f32),
            jax.ShapeDtypeStruct((hidden_local, full), f32),
            jax.ShapeDtypeStruct((1, hidden_local), f32),
            jax.ShapeDtypeStruct((1, hidden_local), f32),
            jax.ShapeDtypeStruct(carry.shape, f32),
        ],
        input_output_aliases={first + at: at for at in range(len(earlier))},
        scratch_shapes=[pltpu.VMEM((rows, full), f32)],
        compiler_params=params(),
        cost_estimate=cost(1),
        name="statistics_%d" % chunk,
    )(place, *sources, up_cols, down_rows, carry, *earlier)


def small_kernel(
    sum_ref,
    stat_ref,
    square_ref,
    params_ref,
    channel_ref,
    moment_ref,
    bias_ref,
    bias_moment_ref,
    rows_ref,
    down_rows_new_ref,
    mixer_grad_ref,
    rows_new_ref,
    channel_grad_ref,
    moment_new_ref,
    channel_update_ref,
    bias_grad_ref,
    bias_moment_new_ref,
    bias_update_ref,
    out_ref,
    channel_square_ref,
    table_ref,
):
    out_ref[...] = stat_ref[...]
    taps_back(params_ref, sum_ref, table_ref)
    grad = table_ref[...].T
    mixer_grad_ref[...] = grad
    states = grad.shape[1]
    square = grad * grad
    mean = jnp.sum(fold(square), axis=1, keepdims=True) / states
    fresh = DECAY * to_column(as_row(rows_ref)) + FRESH * (mean + EPSILON_SQUARE)
    rows_new = fresh.T[0:1, :]
    rows_new_ref[...] = rows_new
    out_ref[MIXER_COL : MIXER_COL + 1, :states] = jnp.sum(square, axis=0, keepdims=True)
    out_ref[MIXER_MASS : MIXER_MASS + 1, :states] = jnp.sum(square * (1.0 / fresh[:, 0:1]), axis=0, keepdims=True)

    layer = channel_ref[3:4, :]
    channel_grad_ref[0:4, :] = sum_ref[ROWS : ROWS + 4, :]
    channel_grad_ref[4:5, :] = sum_ref[ROWS + 4 : ROWS + 5, :] * layer
    grad = channel_grad_ref[...]
    moment = DECAY * moment_ref[...] + FRESH * (grad * grad + EPSILON_SQUARE)
    moment_new_ref[...] = moment
    channel_update = grad * lax.rsqrt(moment)
    channel_update_ref[...] = channel_update

    width = layer.shape[1]
    for at in range(bias_grad_ref.shape[1] // width):
        bias_grad_ref[:, at * width : (at + 1) * width] = sum_ref[BIAS + at : BIAS + at + 1, :]
    grad = bias_grad_ref[...]
    moment = DECAY * as_row(bias_moment_ref) + FRESH * (grad * grad + EPSILON_SQUARE)
    bias_moment_new_ref[...] = moment
    bias_update = grad * lax.rsqrt(moment)
    bias_update_ref[...] = bias_update

    def total(value):
        return jnp.sum(value, keepdims=True)

    channel = channel_ref[...]
    table = params_ref[...]
    bias = as_row(bias_ref)
    scalars = (
        total(channel_update * channel_update) + total(bias_update * bias_update),
        total(down_rows_new_ref[...]),
        total(rows_new),
        total(square_ref[0:1, :]),
        total(square_ref[1:2, :]),
        total(table * table),
        total(bias * bias),
    )
    for at, value in enumerate(scalars):
        out_ref[SCALARS : SCALARS + 1, at * LANES : (at + 1) * LANES] = jnp.broadcast_to(value, (1, LANES))
    channel_square_ref[...] = jnp.broadcast_to(jnp.sum(channel * channel, axis=1, keepdims=True), (5, LANES))


def small_update(total, stat, square, mixer_params, channel_params, channel_moment, bias, bias_moment, rows, down_rows_new):
    width, states = mixer_params.shape
    shapes = [
        (width, states),
        (1, width),
        channel_params.shape,
        channel_params.shape,
        channel_params.shape,
        (1, bias.shape[0]),
        (1, bias.shape[0]),
        (1, bias.shape[0]),
        (8, 8 * LANES),
        (5, LANES),
    ]
    return pl.pallas_call(
        small_kernel,
        out_shape=[jax.ShapeDtypeStruct(shape, f32) for shape in shapes],
        scratch_shapes=[pltpu.VMEM((states, width), f32)],
        compiler_params=params(),
        cost_estimate=cost(5),
        name="small_update",
    )(total, stat, square, mixer_params, channel_params, channel_moment, bias, bias_moment, rows, down_rows_new)


def update_kernel(
    stat_ref,
    got_ref,
    channel_square_ref,
    channel_got_ref,
    up_rows_ref,
    down_cols_ref,
    mixer_cols_ref,
    up_cols_new_ref,
    down_rows_new_ref,
    up_grad_ref,
    up_ref,
    up_average_ref,
    down_grad_ref,
    down_ref,
    down_average_ref,
    mixer_grad_ref,
    mixer_ref,
    mixer_average_ref,
    mixer_rows_new_ref,
    channel_ref,
    channel_average_ref,
    channel_update_ref,
    bias_ref,
    bias_average_ref,
    bias_update_ref,
    bias_grad_ref,
    bias_moment_ref,
    up_cols_all_ref,
    down_rows_all_ref,
    rms_ref,
    up_rows_new_ref,
    down_cols_new_ref,
    mixer_cols_new_ref,
    up_new_ref,
    up_average_new_ref,
    down_new_ref,
    down_average_new_ref,
    mixer_new_ref,
    mixer_average_new_ref,
    channel_new_ref,
    channel_average_new_ref,
    bias_new_ref,
    bias_average_new_ref,
    bias_grad_out_ref,
    bias_moment_out_ref,
    up_cols_out_ref,
    down_rows_out_ref,
    mixer_rows_out_ref,
    left_ref,
):
    full, hidden = up_rows_ref.shape[0], 2 * bias_ref.shape[0]
    states = mixer_cols_ref.shape[0]

    def stat(row, size):
        return stat_ref[row : row + 1, :size] + got_ref[row : row + 1, :size]

    def scalar(at):
        return stat(SCALARS, 8 * LANES)[:, at * LANES : at * LANES + 1]

    def total(value):
        return jnp.sum(value, axis=1, keepdims=True)

    up_rows_new = DECAY * as_row(up_rows_ref) + FRESH * (stat(UP_ROW, full) / hidden + EPSILON_SQUARE)
    down_cols_new = DECAY * as_row(down_cols_ref) + FRESH * (stat(DOWN_COL, full) / hidden + EPSILON_SQUARE)
    mixer_cols_new = DECAY * as_row(mixer_cols_ref) + FRESH * (stat(MIXER_COL, states) / full + EPSILON_SQUARE)
    up_mean = total(up_rows_new) / full
    down_mean = scalar(1) / hidden
    mixer_mean = scalar(2) / full
    square = (
        scalar(0)
        + up_mean * total(stat(UP_MASS, full) / up_rows_new)
        + down_mean * total(stat(DOWN_MASS, full) / down_cols_new)
        + mixer_mean * total(stat(MIXER_MASS, states) / mixer_cols_new)
    )
    rms = jnp.sqrt(square / (2 * full * hidden + states * full + 5 * full + hidden))
    factor = LEARN_RATE * CLIP_LEVEL / jnp.maximum(CLIP_LEVEL, rms)

    def rate(squares, size):
        return factor * jnp.maximum(EPSILON_SCALE, jnp.sqrt(squares / size))

    def settle(weight, change, average_ref, new_ref, average_new_ref):
        new = weight - change
        new_ref[...] = new
        average_new_ref[...] = AVERAGE_KEEP * average_ref[...] + (1.0 - AVERAGE_KEEP) * new

    def column(row):
        return to_column(row)[:, 0:1]

    up_speed = rate(scalar(3), full * hidden) * jnp.sqrt(up_mean)
    rows = up_ref.shape[0]
    left_ref[...] = lax.rsqrt(up_rows_new) * up_speed
    here = pl.ds(pl.multiple_of(pl.program_id(0) * rows, rows), rows)
    settle(
        up_ref[...],
        up_grad_ref[...] * column(left_ref[:, here]) * lax.rsqrt(up_cols_new_ref[...]),
        up_average_ref,
        up_new_ref,
        up_average_new_ref,
    )
    down_speed = rate(scalar(4), full * hidden) * jnp.sqrt(down_mean)
    settle(
        down_ref[...],
        down_grad_ref[...] * column(lax.rsqrt(down_rows_new_ref[...]) * down_speed) * lax.rsqrt(down_cols_new),
        down_average_ref,
        down_new_ref,
        down_average_new_ref,
    )

    @pl.when(pl.program_id(0) == 0)
    def _():
        rms_ref[...] = rms
        to_flat(up_rows_new_ref, up_rows_new)
        to_flat(down_cols_new_ref, down_cols_new)
        to_flat(mixer_cols_new_ref, mixer_cols_new)
        to_flat(bias_grad_out_ref, bias_grad_ref[...])
        to_flat(bias_moment_out_ref, bias_moment_ref[...])
        to_flat(up_cols_out_ref, up_cols_all_ref[...])
        to_flat(down_rows_out_ref, down_rows_all_ref[...])
        to_flat(mixer_rows_out_ref, mixer_rows_new_ref[...])
        mixer_speed = rate(scalar(5), states * full) * jnp.sqrt(mixer_mean)
        settle(
            mixer_ref[...],
            mixer_grad_ref[...]
            * column(lax.rsqrt(mixer_rows_new_ref[...]) * mixer_speed)
            * lax.rsqrt(mixer_cols_new),
            mixer_average_ref,
            mixer_new_ref,
            mixer_average_new_ref,
        )
        channel_square = channel_square_ref[:, 0:1] + channel_got_ref[:, 0:1]
        settle(
            channel_ref[...],
            rate(channel_square, full) * channel_update_ref[...],
            channel_average_ref,
            channel_new_ref,
            channel_average_new_ref,
        )
        bias_new = as_row(bias_ref) - rate(scalar(6), hidden) * bias_update_ref[...]
        to_flat(bias_new_ref, bias_new)
        to_flat(
            bias_average_new_ref, AVERAGE_KEEP * as_row(bias_average_ref) + (1.0 - AVERAGE_KEEP) * bias_new
        )


def final_update(operands, units):
    up, mixer, channel, bias = operands[10], operands[16], operands[19], operands[22]
    full, hidden_local = up.shape
    steps = hidden_local // units
    up_block = pl.BlockSpec((full // steps, hidden_local), lambda i: (i, 0))
    down_block = pl.BlockSpec((units, full), lambda i: (i, 0))
    row_block = pl.BlockSpec((1, units), lambda i: (0, i))

    def whole(array):
        return pl.BlockSpec(array.shape, lambda i: (0,) * len(array.shape))

    in_specs = [whole(array) for array in operands]
    in_specs[8] = row_block
    in_specs[9:12] = [up_block] * 3
    in_specs[12:15] = [down_block] * 3
    shapes = [(1, 1), operands[4].shape, operands[5].shape, operands[6].shape]
    shapes += [up.shape] * 2 + [(hidden_local, full)] * 2 + [mixer.shape] * 2 + [channel.shape] * 2 + [bias.shape] * 2
    shapes += [bias.shape] * 4 + [operands[18].shape[1:]]
    out_specs = [whole(jax.ShapeDtypeStruct(shape, f32)) for shape in shapes]
    out_specs[4:8] = [up_block, up_block, down_block, down_block]
    return pl.pallas_call(
        update_kernel,
        grid=(steps,),
        in_specs=in_specs,
        out_specs=out_specs,
        out_shape=[jax.ShapeDtypeStruct(shape, f32) for shape in shapes],
        scratch_shapes=[pltpu.VMEM((1, full), f32)],
        compiler_params=params(),
        cost_estimate=cost(19),
        name="final_update",
    )(*operands)


def turn_table():
    place = np.arange(AREA)
    swapped = (place % S) * S + place // S
    table = np.concatenate([place[:, None] == place[None, :], swapped[:, None] == place[None, :]])
    return table.astype(ml_dtypes.bfloat16)


def shards(
    pixels,
    image_sizes,
    out_grad,
    up_weight,
    down_weight,
    mixer_params,
    channel_params,
    hidden_bias,
    up_rows,
    up_cols,
    down_rows,
    down_cols,
    mixer_rows,
    mixer_cols,
    channel_moment,
    bias_moment,
    up_average,
    down_average,
    mixer_average,
    channel_average,
    bias_average,
):
    width_local, count = pixels.shape
    hidden_local = up_weight.shape[1]
    place = jnp.stack([lax.axis_index(axis) for axis in ("ch", "plane", "line")]).astype(jnp.int32)

    def exchange(value):
        return lax.ppermute(value, "ch", [(0, 1), (1, 0)])

    def row(value):
        return value.reshape(1, -1)

    other_grad = exchange(out_grad)
    rounded = jnp.concatenate(
        [channel_params[0:2].astype(bf16).astype(f32), channel_params[2:5], jnp.zeros((3, width_local), f32)]
    )
    others = exchange(rounded)
    turn = jnp.asarray(turn_table())
    sizes = image_sizes.T
    mixed, first, taps = mixer_forward(sizes, pixels, mixer_params, channel_params, turn)
    other_mixed = exchange(mixed)
    up_low, up_turned, down_low, down_turned, square = weights_low(up_weight, down_weight)
    sums, bias_parts = [], []
    earlier = ()
    inputs = [sizes, mixed, other_mixed, out_grad, other_grad, rounded, others]
    for chunk in range(CHUNKS):
        values = feed_chunk(chunk, place, inputs, up_turned, down_low, row(hidden_bias), earlier)
        earlier = values[0:2]
        if chunk == 0:
            inputs, stat = values[-3:-1], values[-1]
        bias_parts.append(values[2])
        sums.append(GradientSum(values[3], values[4 : 3 + PLANE]))
    hidden, slopes = earlier
    partial = []
    early, late = sums
    early.to_line()
    tokens, riders = early.sends, [early.kept, late.kept]
    for part in range(SUM_PARTS):
        own, send, riders = hidden_sums(
            place, hidden, slopes, down_turned, up_low, mixed, other_mixed, stat, rounded, others, part, tokens, riders
        )
        if part == 0:
            early.kept, late.kept = riders
            early.gather()
            tokens, riders = [early.piece], [late.kept]
        partial.append((own, exchange(send)))
    done = ()
    (late.kept,) = riders
    late.to_line()
    by_permutes = late.kept.shape[0] % S == 0
    tokens, riders = late.sends, [late.kept]
    carries = bias_parts
    for at, part in enumerate(BACK_PARTS):
        own, got = partial[part[0] * SUM_PARTS // S]
        values = backward(
            sizes, pixels, out_grad, mixed, first, stat, own, got, rounded, taps, turn, carries, part, done, riders, tokens
        )
        done, carries = values[0:2], values[2:3]
        tokens, riders = [], []
        if at == 0:
            (late.kept,) = values[3:]
            if by_permutes:
                late.gather_line()
                tokens, riders = [late.piece], [late.piece]
            else:
                late.gather()
        elif at == 1 and by_permutes:
            late.pieces[0] = values[3]
            late.gather_plane()
            tokens = [late.quarter]
    (carry,) = carries
    block_out, pixel_grad = done

    total, stride = carry, PLANE
    while stride < lax.axis_size("line") * PLANE:
        total, stride = total + across(total, stride), 2 * stride
    there = [across(total, away) for away in range(1, PLANE)]
    total = (total + there[0]) + (there[1] + there[2])
    stats = jnp.zeros((8, 8 * LANES), f32)
    settled = ()
    for chunk, sources in enumerate(([early.sum] * 2, late.quarters if by_permutes else [late.sum] * 2)):
        values = statistics(chunk, place, sources, row(up_cols), row(down_rows), stats, settled)
        settled, stats = values[0:4], values[4]
    up_sum, down_sum, up_cols_new, down_rows_new = settled
    (
        mixer_sum,
        mixer_rows_new,
        channel_sum,
        channel_moment_new,
        channel_update,
        bias_sum,
        bias_moment_new,
        bias_update,
        stats,
        channel_square,
    ) = small_update(
        total,
        stats,
        square,
        mixer_params,
        channel_params,
        channel_moment,
        hidden_bias,
        bias_moment,
        mixer_rows,
        down_rows_new,
    )
    got_stats, got_square = exchange((stats, channel_square))
    (
        update_rms,
        up_rows_new,
        down_cols_new,
        mixer_cols_new,
        up_new,
        up_average_new,
        down_new,
        down_average_new,
        mixer_new,
        mixer_average_new,
        channel_new,
        channel_average_new,
        bias_new,
        bias_average_new,
        bias_sum,
        bias_moment_new,
        up_cols_new,
        down_rows_new,
        mixer_rows_new,
    ) = final_update(
        [
            stats,
            got_stats,
            channel_square,
            got_square,
            up_rows,
            down_cols,
            mixer_cols,
            up_cols_new,
            down_rows_new,
            up_sum,
            up_weight,
            up_average,
            down_sum,
            down_weight,
            down_average,
            mixer_sum,
            mixer_params,
            mixer_average,
            mixer_rows_new,
            channel_params,
            channel_average,
            channel_update,
            hidden_bias,
            bias_average,
            bias_update,
            bias_sum,
            bias_moment_new,
            up_cols_new,
            down_rows_new,
        ],
        256,
    )
    return (
        block_out,
        pixel_grad,
        update_rms.reshape(()),
        up_sum,
        up_rows_new,
        up_cols_new,
        up_new,
        up_average_new,
        down_sum,
        down_rows_new,
        down_cols_new,
        down_new,
        down_average_new,
        mixer_sum,
        mixer_rows_new,
        mixer_cols_new,
        mixer_new,
        mixer_average_new,
        channel_sum,
        channel_moment_new,
        channel_new,
        channel_average_new,
        bias_sum,
        bias_moment_new,
        bias_new,
        bias_average_new,
    )


def solution(mesh):
    mesh = jax.sharding.Mesh(mesh.devices.reshape(-1, PLANE, mesh.shape["ch"]), ("line", "plane", "ch"))
    images = ("line", "plane")
    split = P("ch", images)
    over_rows, over_cols, over = P("ch", None), P(None, "ch"), P("ch")
    return jax.shard_map(
        shards,
        mesh=mesh,
        in_specs=(
            split,
            P(images, None),
            split,
            over_cols,
            over_rows,
            over_rows,
            over_cols,
            over,
            P(),
            over,
            over,
            P(),
            over,
            P(),
            over_cols,
            over,
            over_cols,
            over_rows,
            over_rows,
            over_cols,
            over,
        ),
        out_specs=(
            split,
            split,
            P(),
            over_cols,
            P(),
            over,
            over_cols,
            over_cols,
            over_rows,
            over,
            P(),
            over_rows,
            over_rows,
            over_rows,
            over,
            P(),
            over_rows,
            over_rows,
            over_cols,
            over_cols,
            over_cols,
            over_cols,
            over,
            over,
            over,
            over,
        ),
        check_vma=False,
    )
```
